32 devices in a mesh: row: 4 (over y, x), col: 8 (over z, core).
Axes of the slice: x: 2, y: 2, z: 4, core: 2. Of those that a mesh axis runs over, the one named last changes fastest.
Arguments:
- frontal: bfloat16 [4096, 49152], P('row', 'col')
- sample_cols: bfloat16 [49152, 64], P(('col', 'row')), may hold values from -6 to 6
- leaf_first: int32 [64], replicated, may hold values from 0 to 4064, as said below
- leaf_owner: int32 [64], replicated, may hold values from 0 to 7, as said below
- skeleton: int32 [64, 16], replicated, may hold values from 0 to 4095, as said below
Outputs:
- owner_samples: float32 [256, 2048], P('row', 'col')
- interp: float32 [64, 2048], P('row', 'col')
- worst: float32 [1], replicated
The draws below stay inside these ranges and needn't reach their ends.
Inputs may be any that keep to these rules, and one draw needn't show every extreme that they name: `leaf_first`: leaves are consecutive and ascending; the first leaf of row group g starts at g * 1024; each row group has 16 leaves whose sizes are 1 to 5 times 32, in 4 runs of four consecutive leaves of together 256 rows. `leaf_owner`: each run of four leaves is owned by at most two devices of the group; the leaves one device owns in its group hold at most 256 rows and number at most 4; in every row group some device reaches both. Each leaf's skeleton rows are 16 distinct rows of that leaf, ascending.
All inputs are finite; a program needn't handle non-finite values.
Results may differ from the reference program's by a relative error of at most 0.0003.
Values may be sent and summed in bfloat16 or wider, within the bound.
No kernel may reach another device: no remote copies, remote signals or barrier semaphores. Data moves between devices by JAX's collectives and lax.ppermute only.
A program may use at most 64 MiB of HBM per device.

```python
import jax
import jax.numpy as jnp
from jax import lax

MATRIX_ORDER = 49152
SAMPLES = 64
SKELETON = 16
ROWS_OWNED = 128
CAPACITY = 256
GROUP_ROWS = 1024
WINDOW_ROWS = 4096
LEAVES = 64
N_ROW = 4
N_COL = 8


def leaf_tables(key):
    unit = ROWS_OWNED // 4
    pairs = N_COL // 2
    key_cut, key_side, key_owner, key_skel = jax.random.split(jax.random.fold_in(key, 7), 4)
    cut_scores = jax.random.randint(key_cut, (N_ROW, pairs, 7), 0, 1 << 20) * 8 + jnp.arange(7, dtype=jnp.int32)
    picked = jnp.sort(jnp.argsort(cut_scores, axis=-1)[..., :3].astype(jnp.int32) + 1, axis=-1)
    zeros = jnp.zeros((N_ROW, pairs, 1), jnp.int32)
    bounds = jnp.concatenate([zeros, picked, zeros + 8], axis=-1)
    units = bounds[..., 1:] - bounds[..., :-1]
    sides = jax.random.randint(key_side, (N_ROW, pairs, 4), 0, 2)
    first_pair = (jnp.arange(pairs, dtype=jnp.int32) == 0)[None, :, None]
    sides = jnp.where(first_pair, 0, sides)
    owner_scores = jax.random.randint(key_owner, (N_ROW, N_COL), 0, 1 << 20) * N_COL + jnp.arange(N_COL, dtype=jnp.int32)
    order = jnp.argsort(owner_scores, axis=-1).astype(jnp.int32)
    first_owner = order[:, 0::2]
    second_owner = order[:, 1::2]
    owner = jnp.where(sides == 0, first_owner[..., None], second_owner[..., None]).reshape(LEAVES)
    sizes = (units * unit).reshape(N_ROW, 2 * N_COL)
    starts = jnp.cumsum(sizes, axis=1) - sizes + (jnp.arange(N_ROW, dtype=jnp.int32) * GROUP_ROWS)[:, None]
    starts = starts.reshape(LEAVES).astype(jnp.int32)
    flat_sizes = sizes.reshape(LEAVES)
    top = 5 * unit
    skel_scores = jax.random.randint(key_skel, (LEAVES, top), 0, 1 << 20) * top + jnp.arange(top, dtype=jnp.int32)
    inside = jnp.arange(top, dtype=jnp.int32)[None, :] < flat_sizes[:, None]
    skel_scores = jnp.where(inside, skel_scores, (1 << 20) * top + top)
    chosen = jnp.sort(jnp.argsort(skel_scores, axis=-1)[:, :SKELETON].astype(jnp.int32), axis=-1)
    return (starts, owner.astype(jnp.int32), (chosen + starts[:, None]).astype(jnp.int32))


def draw_leaf_first(key, part):
    return leaf_tables(key)[0]


def draw_leaf_owner(key, part):
    return leaf_tables(key)[1]


def draw_skeleton(key, part):
    return leaf_tables(key)[2]


def draw_frontal(key, part):
    shape = (WINDOW_ROWS, MATRIX_ORDER)
    noise = jax.random.normal(key, shape, jnp.float32)
    base = MATRIX_ORDER ** (-0.5)
    rows = jnp.arange(WINDOW_ROWS, dtype=jnp.float32)[:, None]
    cols = jnp.arange(WINDOW_ROWS, dtype=jnp.float32)[None, :]
    near = base + 0.1 * jnp.exp(-jnp.abs(rows - cols) / ROWS_OWNED)
    left = noise[:, :WINDOW_ROWS] * near
    right = noise[:, WINDOW_ROWS:] * base
    return jnp.concatenate([left, right], axis=1).astype(jnp.bfloat16)


def block_levels(key, extent, pieces, least, top_value):
    def one(axis_at, parts):
        steps = jax.random.uniform(jax.random.fold_in(jax.random.fold_in(key, 6), axis_at), (parts,), jnp.float32, least / len(pieces), top_value / len(pieces))
        return jnp.repeat(jnp.exp(steps), extent[axis_at] // parts).reshape((-1,) + (1,) * (len(extent) - axis_at - 1))

    gain = one(*pieces[0])
    for cut in pieces[1:]:
        gain = gain * one(*cut)
    return gain


def normal_values(own_key, extent, width, bound, pieces=(), kind=jnp.bfloat16):
    values = jax.random.normal(own_key, extent, jnp.float32) * width
    if len(pieces) > 0:
        values = block_levels(own_key, extent, pieces, -0.22, 0.18) * values
    return jnp.clip(values, min=-bound, max=bound).astype(kind)


def setup_inputs(seed: int = 0) -> dict:
    key_of = jax.random.split(jax.random.key(seed), 6)
    return {
        "frontal": draw_frontal(jax.random.fold_in(key_of[5], 71), 0),
        "sample_cols": normal_values(key_of[1], (MATRIX_ORDER, SAMPLES), 1.0, 6.0, ((0, 32),)),
        "leaf_first": draw_leaf_first(jax.random.fold_in(key_of[5], 71), 0),
        "leaf_owner": draw_leaf_owner(jax.random.fold_in(key_of[5], 71), 0),
        "skeleton": draw_skeleton(jax.random.fold_in(key_of[5], 71), 0),
    }


def leaf_index(values, leaf_first):
    return lax.optimization_barrier(jnp.sum((leaf_first[None, :] <= values[:, None]).astype(jnp.int32), axis=1)) - 1

def reference(frontal, sample_cols, leaf_first, leaf_owner, skeleton):
    highest = lax.Precision.HIGHEST
    rows = jnp.arange(WINDOW_ROWS, dtype=jnp.int32)
    row_leaf = leaf_index(rows, leaf_first)
    near_cols = sample_cols[:WINDOW_ROWS]

    def block(carry, index):
        start = (index * GROUP_ROWS).astype(jnp.int32)
        part = lax.dynamic_slice_in_dim(frontal, start, GROUP_ROWS, 0)
        leaves_here = lax.dynamic_slice_in_dim(row_leaf, start, GROUP_ROWS, 0)
        full = jnp.dot(part.astype(jnp.float32), sample_cols.astype(jnp.float32), preferred_element_type=jnp.float32)
        same = leaves_here[:, None] == row_leaf[None, :]
        kept = jnp.where(same, part[:, :WINDOW_ROWS], jnp.zeros((), frontal.dtype))
        diag = jnp.dot(kept.astype(jnp.float32), near_cols.astype(jnp.float32), preferred_element_type=jnp.float32)
        return (carry, full - diag)
    _, blocks = lax.scan(block, jnp.zeros((), jnp.float32), jnp.arange(N_ROW, dtype=jnp.int32))
    samples = blocks.reshape(WINDOW_ROWS, SAMPLES)
    ends = jnp.concatenate([leaf_first[1:], jnp.full((1,), WINDOW_ROWS, jnp.int32)])
    sizes = ends - leaf_first
    per_group = 2 * N_COL
    own_hot = (leaf_owner[:, None] == jnp.arange(N_COL, dtype=jnp.int32)[None, :]).astype(jnp.int32)
    weighted = (own_hot * sizes[:, None]).reshape(N_ROW, per_group, N_COL)
    before = (jnp.cumsum(weighted, axis=1) - weighted).reshape(LEAVES, N_COL)
    offset = lax.optimization_barrier(jnp.sum(before * own_hot, axis=1))
    slot = leaf_owner[row_leaf] * CAPACITY + offset[row_leaf] + rows - leaf_first[row_leaf]
    row_group = rows // GROUP_ROWS
    picked = samples[skeleton]
    gram = jnp.einsum('lkp,ljp->lkj', picked, picked, precision=highest)
    eye = jnp.broadcast_to(jnp.eye(SKELETON, dtype=jnp.float32), gram.shape)
    ginv = jnp.linalg.solve(gram, eye)
    picked_rows = picked[row_leaf]
    proj = jnp.einsum('ikp,ip->ik', picked_rows, samples, precision=highest)
    coeff = jnp.einsum('ij,ijk->ik', proj, ginv[row_leaf], precision=highest)
    rebuilt = jnp.einsum('ik,ikp->ip', coeff, picked_rows, precision=highest)
    resid = samples - rebuilt
    err = jax.ops.segment_sum(lax.optimization_barrier(jnp.sum(resid * resid, axis=1)), row_leaf, LEAVES)
    norm = jax.ops.segment_sum(lax.optimization_barrier(jnp.sum(samples * samples, axis=1)), row_leaf, LEAVES)
    ratio = jnp.sqrt(err) / jnp.sqrt(norm + 1e-06)
    worst = jnp.max(ratio).reshape(1)
    holder = jnp.zeros((N_ROW, N_COL * CAPACITY, SAMPLES), jnp.float32).at[row_group, slot].set(samples)
    owner_samples = jnp.transpose(holder, (0, 2, 1)).reshape(N_ROW * SAMPLES, N_COL * CAPACITY)
    cholder = jnp.zeros((N_ROW, N_COL * CAPACITY, SKELETON), jnp.float32).at[row_group, slot].set(coeff)
    interp = jnp.transpose(cholder, (0, 2, 1)).reshape(N_ROW * SKELETON, N_COL * CAPACITY)
    return (owner_samples, interp, worst)
```

```python
import functools

import jax
import jax.numpy as jnp
from jax import lax
from jax.experimental import pallas as pl
from jax.experimental.pallas import tpu as pltpu
from jax.sharding import PartitionSpec as P

UNIT = 32
LEAF_MOST = 4
RUN_LEAVES = 4
HIGHEST = lax.Precision.HIGHEST


def nt_dot(a, b, precision=None):
    return lax.dot_general(
        a, b, (((1,), (1,)), ((), ())), precision=precision, preferred_element_type=jnp.float32
    )


def product_kernel(
    tile, n_row, n_col, leaf_first, leaf_owner, frontal, cols, out, total, target, used
):
    group_rows = frontal.shape[0]
    leaves = leaf_first.shape[0]
    per_group = leaves // n_row
    runs = per_group // RUN_LEAVES
    run_rows = group_rows // runs
    capacity = 2 * group_rows // n_col
    half = capacity // 2
    per_owner = capacity // UNIT
    samples = cols.shape[1]
    units = group_rows // UNIT
    step = pl.program_id(0)
    steps = pl.num_programs(0)
    row_pos = lax.axis_index("row")
    col_pos = lax.axis_index("col")
    first_col = col_pos * (steps * tile) + step * tile

    block = cols[0]
    twice = jnp.concatenate([block, block], axis=0)

    @pl.when(step == 0)
    def _():
        total[...] = nt_dot(frontal[...], twice)

        def clear(owner, carry):
            used[owner] = 0
            return carry

        lax.fori_loop(0, n_col, clear, 0)

        def place(unit, leaf):
            row = row_pos * group_rows + unit * UNIT
            later = jnp.minimum(leaf + 1, leaves - 1)
            moved = (leaf + 1 < leaves) & (leaf_first[later] <= row)
            leaf = jnp.where(moved, later, leaf)
            owner = leaf_owner[leaf]
            slot = used[owner]
            used[owner] = slot + 1
            target[unit] = owner * per_owner + slot
            return leaf

        lax.fori_loop(0, units, place, row_pos * per_group)

    @pl.when(step > 0)
    def _():
        total[...] += nt_dot(frontal[...], twice)

    def remove(run, carry):
        begin = row_pos * group_rows + run * run_rows
        inside = begin - first_col

        @pl.when((inside >= 0) & (inside < tile))
        def _():
            at = pl.multiple_of(jnp.clip(inside, 0, tile - run_rows), run_rows)
            rows = pl.ds(pl.multiple_of(run * run_rows, run_rows), run_rows)
            part = frontal[rows, pl.ds(at, run_rows)]
            down = lax.broadcasted_iota(jnp.int32, (run_rows, run_rows), 0) + begin
            across = lax.broadcasted_iota(jnp.int32, (run_rows, run_rows), 1) + begin
            leaf_down = jnp.zeros((run_rows, run_rows), jnp.int32)
            leaf_across = jnp.zeros((run_rows, run_rows), jnp.int32)
            for k in range(1, RUN_LEAVES):
                edge = leaf_first[row_pos * per_group + run * RUN_LEAVES + k]
                leaf_down += (down >= edge).astype(jnp.int32)
                leaf_across += (across >= edge).astype(jnp.int32)
            kept = jnp.where(leaf_down == leaf_across, part.astype(jnp.float32), 0.0)
            near = cols[0, :, pl.ds(at, run_rows)]
            near = jnp.concatenate([near, near], axis=0)
            total[rows, :] -= nt_dot(kept.astype(jnp.bfloat16), near)

        return carry

    lax.fori_loop(0, runs, remove, 0)

    @pl.when(step == steps - 1)
    def _():
        out[...] = jnp.zeros_like(out)
        lane = lax.broadcasted_iota(jnp.int32, (UNIT, 2 * samples), 1) // samples

        def send(unit, carry):
            spot = target[unit]
            owner = spot // per_owner
            slot = lax.rem(spot, per_owner) * UNIT
            side = slot // half
            rows = pl.ds(pl.multiple_of(lax.rem(slot, half), UNIT), UNIT)
            value = total[pl.ds(pl.multiple_of(unit * UNIT, UNIT), UNIT), :]
            out[owner, rows, :] = jnp.where(lane == side, value, out[owner, rows, :])
            return carry

        lax.fori_loop(0, units, send, 0)


def product(frontal, pieces, leaf_first, leaf_owner, n_row, n_col):
    group_rows, width = frontal.shape
    n_piece, samples, depth = pieces.shape
    capacity = 2 * group_rows // n_col
    tile = 512 if depth % 512 == 0 else depth
    per_piece = depth // tile
    return pl.pallas_call(
        functools.partial(product_kernel, tile, n_row, n_col),
        grid=(width // tile,),
        in_specs=[
            pl.BlockSpec(memory_space=pltpu.SMEM),
            pl.BlockSpec(memory_space=pltpu.SMEM),
            pl.BlockSpec((group_rows, tile), lambda i: (0, i)),
            pl.BlockSpec((1, samples, tile), lambda i: (i // per_piece, 0, i % per_piece)),
        ],
        out_specs=pl.BlockSpec((n_col, capacity // 2, 2 * samples), lambda i: (0, 0, 0)),
        out_shape=jax.ShapeDtypeStruct((n_col, capacity // 2, 2 * samples), jnp.float32),
        scratch_shapes=[
            pltpu.VMEM((group_rows, 2 * samples), jnp.float32),
            pltpu.SMEM((group_rows // UNIT,), jnp.int32),
            pltpu.SMEM((n_col,), jnp.int32),
        ],
        compiler_params=pltpu.CompilerParams(vmem_limit_bytes=48 * 2**20),
    )(leaf_first, leaf_owner, frontal, pieces)


def leaf_kernel(
    n_row, leaf_first, leaf_owner, skeleton, parts, mine_out, coeff_out, worst_out, mine, picked
):
    leaves = leaf_first.shape[0]
    per_group = leaves // n_row
    half, wide = parts.shape[1:]
    samples = wide // 2
    capacity = 2 * half
    skel = skeleton.shape[0]
    every = LEAF_MOST * skel
    row_pos = lax.axis_index("row")
    col_pos = lax.axis_index("col")
    group_rows = mine_out.shape[1] * lax.axis_size("col") // 2
    group_end = (row_pos + 1) * group_rows

    total = parts[0]
    for k in range(1, parts.shape[0]):
        total = total + parts[k]
    mine[pl.ds(0, half), :] = total
    mine[pl.ds(half, half), :] = pltpu.roll(total, samples, 1)
    turned = total.T
    mine_t = jnp.concatenate([turned[:samples], turned[samples:]], axis=1)
    mine_out[...] = mine_t

    def find(at, carry):
        count, filled, begins, firsts, names = carry
        leaf = row_pos * per_group + at
        first = leaf_first[leaf]
        following = leaf_first[jnp.minimum(leaf + 1, leaves - 1)]
        end = jnp.where(at + 1 < per_group, following, group_end)
        hit = leaf_owner[leaf] == col_pos
        here = [hit & (count == k) for k in range(LEAF_MOST)]
        begins = tuple(jnp.where(h, filled, v) for h, v in zip(here, begins))
        firsts = tuple(jnp.where(h, first, v) for h, v in zip(here, firsts))
        names = tuple(jnp.where(h, leaf, v) for h, v in zip(here, names))
        filled = jnp.where(hit, filled + end - first, filled)
        return jnp.where(hit, count + 1, count), filled, begins, firsts, names

    zero = jnp.int32(0)
    far = jnp.int32(capacity)
    count, _, begins, firsts, names = lax.fori_loop(
        0,
        per_group,
        find,
        (zero, zero, (far,) * LEAF_MOST, (zero,) * LEAF_MOST, (zero,) * LEAF_MOST),
    )
    for b in range(LEAF_MOST):
        there = count > b
        for k in range(skel):
            at = begins[b] + skeleton[k, names[b]] - firsts[b]
            at = jnp.clip(jnp.where(there, at, 0), 0, capacity - 1)
            row = mine[pl.ds(at, 1), :]
            picked[pl.ds(b * skel + k, 1), :] = jnp.where(there, row, 0.0)
    chosen = picked[:, :samples]

    gram = nt_dot(chosen, chosen, HIGHEST)
    proj = jnp.dot(chosen, mine_t, precision=HIGHEST, preferred_element_type=jnp.float32)

    slot = lax.broadcasted_iota(jnp.int32, (skel, capacity), 1)
    rank = jnp.zeros((skel, capacity), jnp.int32)
    for b in range(1, LEAF_MOST):
        rank += (slot >= begins[b]).astype(jnp.int32)
    hot = [rank == b for b in range(LEAF_MOST)]
    hot_rows = jnp.concatenate([h.astype(jnp.float32) for h in hot], axis=0)

    lane_leaf = lax.broadcasted_iota(jnp.int32, (skel, every), 1) // skel
    lane_row = lax.broadcasted_iota(jnp.int32, (skel, every), 1) % skel
    down = lax.broadcasted_iota(jnp.int32, (skel, every), 0)
    joined = jnp.where((down == lane_row) & (count == 0), 1.0, 0.0)
    for b in range(LEAF_MOST):
        joined += jnp.where(lane_leaf == b, gram[b * skel : (b + 1) * skel], 0.0)
    spread = jnp.concatenate([jnp.where(lane_row == i, joined, 0.0) for i in range(skel)], axis=0)
    system = jnp.dot(spread, hot_rows, precision=HIGHEST, preferred_element_type=jnp.float32)

    lines = [system[i * skel : (i + 1) * skel] for i in range(skel)]
    right = jnp.zeros((skel, capacity), jnp.float32)
    for b in range(LEAF_MOST):
        right += jnp.where(hot[b], proj[b * skel : (b + 1) * skel], 0.0)
    index = lax.broadcasted_iota(jnp.int32, (skel, capacity), 0)
    uppers = []
    pivots = []
    for j in range(skel):
        line = lines[j]
        inverse = 1.0 / line[j : j + 1]
        upper = line * inverse
        uppers.append(upper)
        pivots.append(inverse)
        for i in range(j + 1, skel):
            lines[i] = lines[i] - line[i : i + 1] * upper
        right = right - jnp.where(index > j, upper * right[j : j + 1], 0.0)
    solved = right * jnp.concatenate(pivots, axis=0)
    for j in range(skel - 2, -1, -1):
        known = jnp.where(index > j, uppers[j] * solved, 0.0)
        less = jnp.sum(known, axis=0, keepdims=True)
        solved = jnp.where(index == j, solved - less, solved)
    coeff_out[...] = solved

    weights = jnp.concatenate([jnp.where(h, solved, 0.0) for h in hot], axis=0)
    rebuilt = lax.dot_general(
        chosen,
        weights,
        (((0,), (0,)), ((), ())),
        precision=HIGHEST,
        preferred_element_type=jnp.float32,
    )
    resid = mine_t - rebuilt
    err = jnp.sum(resid * resid, axis=0, keepdims=True)
    norm = jnp.sum(mine_t * mine_t, axis=0, keepdims=True)
    worst = jnp.zeros((1, 1), jnp.float32)
    for b in range(LEAF_MOST):
        near = hot[b][:1]
        err_leaf = jnp.sum(jnp.where(near, err, 0.0), axis=1, keepdims=True)
        norm_leaf = jnp.sum(jnp.where(near, norm, 0.0), axis=1, keepdims=True)
        worst = jnp.maximum(worst, jnp.sqrt(err_leaf) / jnp.sqrt(norm_leaf + 1e-06))
    worst_out[...] = jnp.broadcast_to(worst, worst_out.shape)


def leaf_work(parts, leaf_first, leaf_owner, skeleton, n_row):
    n_col, half, wide = parts.shape
    samples = wide // 2
    skel = skeleton.shape[0]
    return pl.pallas_call(
        functools.partial(leaf_kernel, n_row),
        in_specs=[
            pl.BlockSpec(memory_space=pltpu.SMEM),
            pl.BlockSpec(memory_space=pltpu.SMEM),
            pl.BlockSpec(memory_space=pltpu.SMEM),
            pl.BlockSpec(memory_space=pltpu.VMEM),
        ],
        out_specs=[pl.BlockSpec(memory_space=pltpu.VMEM)] * 3,
        out_shape=[
            jax.ShapeDtypeStruct((samples, 2 * half), jnp.float32),
            jax.ShapeDtypeStruct((skel, 2 * half), jnp.float32),
            jax.ShapeDtypeStruct((1, 128), jnp.float32),
        ],
        scratch_shapes=[
            pltpu.VMEM((2 * half, wide), jnp.float32),
            pltpu.VMEM((LEAF_MOST * skel, wide), jnp.float32),
        ],
        compiler_params=pltpu.CompilerParams(vmem_limit_bytes=32 * 2**20),
    )(leaf_first, leaf_owner, skeleton, parts)


def local(frontal, sample_cols, leaf_first, leaf_owner, skeleton):
    n_col = lax.axis_size("col")
    n_row = lax.axis_size("row")
    pieces = lax.all_gather(sample_cols.T, "row", axis=0)
    sent = product(frontal, pieces, leaf_first, leaf_owner, n_row, n_col)
    parts = lax.all_to_all(sent, "col", 0, 0)
    mine, coeff, worst = leaf_work(parts, leaf_first, leaf_owner, skeleton.T, n_row)
    worst = jnp.max(lax.all_gather(worst, ("row", "col"), axis=0, tiled=True), axis=0)
    return (mine, coeff, worst[:1])


def solution(mesh):
    return jax.shard_map(
        local,
        mesh=mesh,
        in_specs=(P("row", "col"), P(("col", "row"), None), P(), P(), P()),
        out_specs=(P("row", "col"), P("row", "col"), P()),
        check_vma=False,
    )
```

```python
import functools

import jax
import jax.numpy as jnp
from jax import lax
from jax.experimental import pallas as pl
from jax.experimental.pallas import tpu as pltpu
from jax.sharding import PartitionSpec as P

UNIT = 32
LANES = 128
LEAF_MOST = 4
RUN_LEAVES = 4
HIGHEST = lax.Precision.HIGHEST


def nt_dot(a, b, precision=None):
    return lax.dot_general(
        a, b, (((1,), (1,)), ((), ())), precision=precision, preferred_element_type=jnp.float32
    )


def remove_runs(pick, n_row, frontal, leaf_first, slabs, total):
    group_rows, width = frontal.shape
    depth = slabs[0].shape[1]
    per_group = leaf_first.shape[0] // n_row
    runs = per_group // RUN_LEAVES
    run_rows = group_rows // runs
    row_pos = lax.axis_index("row")
    first_col = lax.axis_index("col") * width

    def remove(at, carry):
        run = at // (run_rows // LANES)
        begin = row_pos * group_rows + run * run_rows
        begin_col = row_pos * group_rows + at * LANES
        inside = begin_col - first_col
        held = (inside >= 0) & (inside < width)
        inside = jnp.clip(inside, 0, width - LANES)
        turn = (inside // depth) ^ row_pos
        for k, slab in zip(pick, slabs):

            @pl.when(held & (turn == k))
            def _():
                rows = pl.ds(pl.multiple_of(run * run_rows, run_rows), run_rows)
                part = frontal[rows, pl.ds(pl.multiple_of(inside, LANES), LANES)]
                down = lax.broadcasted_iota(jnp.int32, part.shape, 0) + begin
                across = lax.broadcasted_iota(jnp.int32, part.shape, 1) + begin_col
                leaf_down = jnp.zeros(part.shape, jnp.int32)
                leaf_across = jnp.zeros(part.shape, jnp.int32)
                for k in range(1, RUN_LEAVES):
                    edge = leaf_first[row_pos * per_group + run * RUN_LEAVES + k]
                    leaf_down += (down >= edge).astype(jnp.int32)
                    leaf_across += (across >= edge).astype(jnp.int32)
                kept = jnp.where(leaf_down == leaf_across, part.astype(jnp.float32), 0.0)
                near = slab[:, pl.ds(pl.multiple_of(lax.rem(inside, depth), LANES), LANES)]
                near = jnp.concatenate([near, near], axis=0)
                total[rows, :] -= nt_dot(kept.astype(jnp.bfloat16), near)

        return carry

    lax.fori_loop(0, group_rows // LANES, remove, 0)


def multiply(pick, frontal, slabs, total, first):
    group_rows = frontal.shape[0]
    depth = slabs[0].shape[1]
    row_pos = lax.axis_index("row")
    part = min(group_rows, 512)

    def rows_of(at, carry):
        rows = pl.ds(pl.multiple_of(at * part, part), part)
        value = None if first else total[rows, :]
        for k, slab in zip(pick, slabs):
            begin = pl.multiple_of((row_pos ^ k) * depth, LANES)
            twice = jnp.concatenate([slab[...], slab[...]], axis=0)
            add = nt_dot(frontal[rows, pl.ds(begin, depth)], twice)
            value = add if value is None else value + add
        total[rows, :] = value
        return carry

    lax.fori_loop(0, group_rows // part, rows_of, 0)


def own_kernel(n_row, n_col, leaf_first, leaf_owner, frontal, slab, total, source, used):
    group_rows = frontal.shape[0]
    leaves = leaf_first.shape[0]
    per_group = leaves // n_row
    per_owner = 2 * group_rows // n_col // UNIT
    units = group_rows // UNIT
    row_pos = lax.axis_index("row")
    multiply((0,), frontal, (slab,), total, True)
    remove_runs((0,), n_row, frontal, leaf_first, (slab,), total)

    def clear(at, carry):
        source[at] = units
        used[at // per_owner] = 0
        return carry

    lax.fori_loop(0, n_col * per_owner, clear, 0)

    def place(unit, leaf):
        row = row_pos * group_rows + unit * UNIT
        later = jnp.minimum(leaf + 1, leaves - 1)
        moved = (leaf + 1 < leaves) & (leaf_first[later] <= row)
        leaf = jnp.where(moved, later, leaf)
        owner = leaf_owner[leaf]
        slot = used[owner]
        used[owner] = slot + 1
        source[owner * per_owner + slot] = unit
        return leaf

    lax.fori_loop(0, units, place, row_pos * per_group)


def rest_kernel(n_row, pick, leaf_first, source, frontal, begun, *refs):
    slabs, (keep, swap, total) = refs[: len(pick)], refs[len(pick) :]
    group_rows = frontal.shape[0]
    chips, half, wide = keep.shape
    per_half = half // UNIT
    samples = wide // 2
    core = lax.rem(lax.axis_index("col"), 2)
    chip = lax.axis_index("col") // 2
    total[pl.ds(0, group_rows), :] = begun[...]
    total[pl.ds(group_rows, UNIT), :] = jnp.zeros((UNIT, wide), jnp.float32)
    multiply(pick, frontal, slabs, total, False)
    remove_runs(pick, n_row, frontal, leaf_first, slabs, total)
    lane = lax.broadcasted_iota(jnp.int32, (UNIT, wide), 1)

    def lay(turn, carry):
        for other, out in ((0, keep), (1, swap)):
            owner = (chip ^ turn) * 2 + (core ^ other)
            for at in range(per_half):
                values = []
                for side in range(2):
                    unit = source[owner * (2 * per_half) + side * per_half + at]
                    values.append(total[pl.ds(pl.multiple_of(unit * UNIT, UNIT), UNIT), :])
                out[turn, pl.ds(at * UNIT, UNIT), :] = jnp.where(lane < samples, *values)
        return carry

    lax.fori_loop(0, chips, lay, 0, unroll=min(chips, 4))


def vmem(count=None):
    spec = pl.BlockSpec(memory_space=pltpu.VMEM)
    return spec if count is None else [spec] * count


def smem():
    return pl.BlockSpec(memory_space=pltpu.SMEM)


def own_product(frontal, slab, leaf_first, leaf_owner, n_row, n_col):
    group_rows, width = frontal.shape
    samples, depth = slab.shape
    per_owner = 2 * group_rows // n_col // UNIT
    return pl.pallas_call(
        functools.partial(own_kernel, n_row, n_col),
        in_specs=[smem(), smem(), vmem(), vmem()],
        out_specs=[vmem(), smem()],
        out_shape=[
            jax.ShapeDtypeStruct((group_rows, 2 * samples), jnp.float32),
            jax.ShapeDtypeStruct((n_col * per_owner,), jnp.int32),
        ],
        scratch_shapes=[pltpu.SMEM((n_col,), jnp.int32)],
        cost_estimate=pl.CostEstimate(
            flops=8 * group_rows * depth * samples,
            bytes_accessed=2 * group_rows * depth,
            transcendentals=0,
        ),
        compiler_params=pltpu.CompilerParams(vmem_limit_bytes=12 * 2**20),
    )(leaf_first, leaf_owner, frontal, slab)


def rest_product(frontal, begun, source, slabs, leaf_first, n_row, n_col):
    group_rows, width = frontal.shape
    samples, depth = slabs[0].shape
    pick = tuple(range(1, n_row))
    half = group_rows // n_col
    block = jax.ShapeDtypeStruct((n_col // 2, half, 2 * samples), jnp.float32)
    return pl.pallas_call(
        functools.partial(rest_kernel, n_row, pick),
        in_specs=[smem(), smem(), vmem(), vmem()] + vmem(len(slabs)),
        out_specs=vmem(2),
        out_shape=[block, block],
        scratch_shapes=[pltpu.VMEM((group_rows + UNIT, 2 * samples), jnp.float32)],
        cost_estimate=pl.CostEstimate(
            flops=8 * group_rows * depth * samples * len(slabs),
            bytes_accessed=2 * group_rows * depth * len(slabs),
            transcendentals=0,
        ),
        compiler_params=pltpu.CompilerParams(vmem_limit_bytes=12 * 2**20),
    )(leaf_first, source, frontal, begun, *slabs)


def leaf_kernel(
    n_row, count_parts, leaf_first, leaf_owner, skeleton, *refs
):
    leaves = leaf_first.shape[0]
    per_group = leaves // n_row
    parts = refs[:count_parts]
    mine_out, coeff_out, worst_out, mine, picked = refs[count_parts:]
    half, wide = parts[0].shape
    samples = wide // 2
    capacity = 2 * half
    skel = skeleton.shape[0]
    every = LEAF_MOST * skel
    row_pos = lax.axis_index("row")
    col_pos = lax.axis_index("col")
    group_rows = mine_out.shape[1] * lax.axis_size("col") // 2
    group_end = (row_pos + 1) * group_rows

    total = parts[0][...]
    for part in parts[1:]:
        total = total + part[...]
    mine[pl.ds(0, half), :] = total
    mine[pl.ds(half, half), :] = pltpu.roll(total, samples, 1)
    turned = total.T
    mine_t = jnp.concatenate([turned[:samples], turned[samples:]], axis=1)
    mine_out[...] = mine_t

    def find(at, carry):
        count, filled, begins, firsts, names = carry
        leaf = row_pos * per_group + at
        first = leaf_first[leaf]
        following = leaf_first[jnp.minimum(leaf + 1, leaves - 1)]
        end = jnp.where(at + 1 < per_group, following, group_end)
        hit = leaf_owner[leaf] == col_pos
        here = [hit & (count == k) for k in range(LEAF_MOST)]
        begins = tuple(jnp.where(h, filled, v) for h, v in zip(here, begins))
        firsts = tuple(jnp.where(h, first, v) for h, v in zip(here, firsts))
        names = tuple(jnp.where(h, leaf, v) for h, v in zip(here, names))
        filled = jnp.where(hit, filled + end - first, filled)
        return jnp.where(hit, count + 1, count), filled, begins, firsts, names

    zero = jnp.int32(0)
    far = jnp.int32(capacity)
    count, _, begins, firsts, names = lax.fori_loop(
        0,
        per_group,
        find,
        (zero, zero, (far,) * LEAF_MOST, (zero,) * LEAF_MOST, (zero,) * LEAF_MOST),
    )
    for b in range(LEAF_MOST):
        there = count > b
        for k in range(skel):
            at = begins[b] + skeleton[k, names[b]] - firsts[b]
            at = jnp.clip(jnp.where(there, at, 0), 0, capacity - 1)
            row = mine[pl.ds(at, 1), :]
            picked[pl.ds(b * skel + k, 1), :] = jnp.where(there, row, 0.0)
    chosen = picked[:, :samples]

    gram = nt_dot(chosen, chosen, HIGHEST)
    proj = jnp.dot(chosen, mine_t, precision=HIGHEST, preferred_element_type=jnp.float32)

    slot = lax.broadcasted_iota(jnp.int32, (skel, capacity), 1)
    rank = jnp.zeros((skel, capacity), jnp.int32)
    for b in range(1, LEAF_MOST):
        rank += (slot >= begins[b]).astype(jnp.int32)
    hot = [rank == b for b in range(LEAF_MOST)]
    hot_rows = jnp.concatenate([h.astype(jnp.float32) for h in hot], axis=0)

    lane_leaf = lax.broadcasted_iota(jnp.int32, (skel, every), 1) // skel
    lane_row = lax.broadcasted_iota(jnp.int32, (skel, every), 1) % skel
    down = lax.broadcasted_iota(jnp.int32, (skel, every), 0)
    joined = jnp.where((down == lane_row) & (count == 0), 1.0, 0.0)
    for b in range(LEAF_MOST):
        joined += jnp.where(lane_leaf == b, gram[b * skel : (b + 1) * skel], 0.0)
    spread = jnp.concatenate([jnp.where(lane_row == i, joined, 0.0) for i in range(skel)], axis=0)
    system = jnp.dot(spread, hot_rows, precision=HIGHEST, preferred_element_type=jnp.float32)

    lines = [system[i * skel : (i + 1) * skel] for i in range(skel)]
    right = jnp.zeros((skel, capacity), jnp.float32)
    for b in range(LEAF_MOST):
        right += jnp.where(hot[b], proj[b * skel : (b + 1) * skel], 0.0)
    index = lax.broadcasted_iota(jnp.int32, (skel, capacity), 0)
    uppers = []
    pivots = []
    for j in range(skel):
        line = lines[j]
        inverse = 1.0 / line[j : j + 1]
        upper = line * inverse
        uppers.append(upper)
        pivots.append(inverse)
        for i in range(j + 1, skel):
            lines[i] = lines[i] - line[i : i + 1] * upper
        right = right - jnp.where(index > j, upper * right[j : j + 1], 0.0)
    solved = right * jnp.concatenate(pivots, axis=0)
    for j in range(skel - 2, -1, -1):
        known = jnp.where(index > j, uppers[j] * solved, 0.0)
        less = jnp.sum(known, axis=0, keepdims=True)
        solved = jnp.where(index == j, solved - less, solved)
    coeff_out[...] = solved

    weights = jnp.concatenate([jnp.where(h, solved, 0.0) for h in hot], axis=0)
    rebuilt = lax.dot_general(
        chosen,
        weights,
        (((0,), (0,)), ((), ())),
        precision=HIGHEST,
        preferred_element_type=jnp.float32,
    )
    resid = mine_t - rebuilt
    err = jnp.sum(resid * resid, axis=0, keepdims=True)
    norm = jnp.sum(mine_t * mine_t, axis=0, keepdims=True)
    worst = jnp.zeros((1, 1), jnp.float32)
    for b in range(LEAF_MOST):
        near = hot[b][:1]
        err_leaf = jnp.sum(jnp.where(near, err, 0.0), axis=1, keepdims=True)
        norm_leaf = jnp.sum(jnp.where(near, norm, 0.0), axis=1, keepdims=True)
        worst = jnp.maximum(worst, jnp.sqrt(err_leaf) / jnp.sqrt(norm_leaf + 1e-06))
    worst_out[...] = jnp.broadcast_to(worst, worst_out.shape)


def leaf_work(parts, leaf_first, leaf_owner, skeleton, n_row):
    half, wide = parts[0].shape
    samples = wide // 2
    skel = skeleton.shape[0]
    return pl.pallas_call(
        functools.partial(leaf_kernel, n_row, len(parts)),
        in_specs=[smem(), smem(), smem()] + vmem(len(parts)),
        out_specs=vmem(3),
        out_shape=[
            jax.ShapeDtypeStruct((samples, 2 * half), jnp.float32),
            jax.ShapeDtypeStruct((skel, 2 * half), jnp.float32),
            jax.ShapeDtypeStruct((1, LANES), jnp.float32),
        ],
        scratch_shapes=[
            pltpu.VMEM((2 * half, wide), jnp.float32),
            pltpu.VMEM((LEAF_MOST * skel, wide), jnp.float32),
        ],
        compiler_params=pltpu.CompilerParams(vmem_limit_bytes=12 * 2**20),
    )(leaf_first, leaf_owner, skeleton, *parts)


def exchange(value, axis, flip):
    pairs = [(k, k ^ flip) for k in range(lax.axis_size(axis))]
    return lax.ppermute(value, axis, pairs)


def local(frontal, sample_cols, leaf_first, leaf_owner, skeleton):
    n_col = lax.axis_size("col")
    n_row = lax.axis_size("row")
    own = sample_cols.T
    slabs = [exchange(own, "row", k) for k in range(1, n_row)]
    frontal = pltpu.with_memory_space_constraint(frontal, pltpu.VMEM)
    begun, source = own_product(frontal, own, leaf_first, leaf_owner, n_row, n_col)
    keep, swap = rest_product(frontal, begun, source, slabs, leaf_first, n_row, n_col)
    summed = keep + exchange(swap, "col", 1)
    parts = [summed[0]] + [exchange(summed[k], "col", 2 * k) for k in range(1, n_col // 2)]
    mine, coeff, worst = leaf_work(parts, leaf_first, leaf_owner, skeleton.T, n_row)
    for axis, size in (("col", n_col), ("row", n_row)):
        others = [exchange(worst, axis, k) for k in range(1, size)]
        for other in others:
            worst = jnp.maximum(worst, other)
    return (mine, coeff, worst[0, :1])


def solution(mesh):
    return jax.shard_map(
        local,
        mesh=mesh,
        in_specs=(P("row", "col"), P(("col", "row"), None), P(), P(), P()),
        out_specs=(P("row", "col"), P("row", "col"), P()),
        check_vma=False,
    )
```

```python
import functools

import jax
import jax.numpy as jnp
from jax import lax
from jax.experimental import pallas as pl
from jax.experimental.pallas import tpu as pltpu
from jax.sharding import PartitionSpec as P

UNIT = 32
LANES = 128
LEAF_MOST = 4
PICKS = 8
FAN = 6
RUN_LEAVES = 4
HIGHEST = lax.Precision.HIGHEST


def nt_dot(a, b, precision=None):
    return lax.dot_general(
        a, b, (((1,), (1,)), ((), ())), precision=precision, preferred_element_type=jnp.float32
    )


def clear_runs(pick, n_row, depth, frontal, leaf_first):
    group_rows, width = frontal.shape
    per_group = leaf_first.shape[0] // n_row
    runs = per_group // RUN_LEAVES
    run_rows = group_rows // runs
    row_pos = lax.axis_index("row")
    first_col = lax.axis_index("col") * width

    def clear(at, carry):
        run = at // (run_rows // LANES)
        begin = row_pos * group_rows + run * run_rows
        begin_col = row_pos * group_rows + at * LANES
        inside = begin_col - first_col
        held = (inside >= 0) & (inside < width)
        inside = jnp.clip(inside, 0, width - LANES)

        @pl.when(held & (((inside // depth) ^ row_pos) == pick))
        def _():
            rows = pl.ds(pl.multiple_of(run * run_rows, run_rows), run_rows)
            lanes = pl.ds(pl.multiple_of(inside, LANES), LANES)
            part = frontal[rows, lanes]
            down = lax.broadcasted_iota(jnp.int32, part.shape, 0) + begin
            across = lax.broadcasted_iota(jnp.int32, part.shape, 1) + begin_col
            leaf_down = jnp.zeros(part.shape, jnp.int32)
            leaf_across = jnp.zeros(part.shape, jnp.int32)
            for k in range(1, RUN_LEAVES):
                edge = leaf_first[row_pos * per_group + run * RUN_LEAVES + k]
                leaf_down += (down >= edge).astype(jnp.int32)
                leaf_across += (across >= edge).astype(jnp.int32)
            kept = jnp.where(leaf_down == leaf_across, 0.0, part.astype(jnp.float32))
            frontal[rows, lanes] = kept.astype(jnp.bfloat16)

        return carry

    lax.fori_loop(0, group_rows // LANES, clear, 0)


def multiply(pick, frontal, slabs, begun, total):
    group_rows = frontal.shape[0]
    depth = slabs[0].shape[1]
    row_pos = lax.axis_index("row")
    part = min(group_rows, 512)

    def rows_of(at, carry):
        rows = pl.ds(pl.multiple_of(at * part, part), part)
        value = None if begun is None else begun[rows, :]
        for k, slab in zip(pick, slabs):
            begin = pl.multiple_of((row_pos ^ k) * depth, LANES)
            twice = jnp.concatenate([slab[...], slab[...]], axis=0)
            add = nt_dot(frontal[rows, pl.ds(begin, depth)], twice)
            value = add if value is None else value + add
        total[rows, :] = value
        return carry

    lax.fori_loop(0, group_rows // part, rows_of, 0)


def plan_leaves(n_row, group_rows, capacity, first, owners, skel, plan):
    leaves = first.shape[0]
    per_group = leaves // n_row
    count_skel = skel.shape[0]
    row_pos = lax.axis_index("row")
    col_pos = lax.axis_index("col")

    def clear(at, carry):
        plan[at] = capacity
        return carry

    lax.fori_loop(0, plan.shape[0], clear, 0)

    def find(at, carry):
        count, filled = carry
        leaf = row_pos * per_group + at
        begin = first[leaf]
        following = first[jnp.minimum(leaf + 1, leaves - 1)]
        end = jnp.where(at + 1 < per_group, following, (row_pos + 1) * group_rows)
        hit = (owners[leaf] == col_pos) & (count < LEAF_MOST)

        @pl.when(hit)
        def _():
            plan[count] = filled
            for k in range(count_skel):
                plan[PICKS + count * count_skel + k] = filled + skel[k, leaf] - begin

        return jnp.where(hit, count + 1, count), jnp.where(hit, filled + end - begin, filled)

    count, _ = lax.fori_loop(0, per_group, find, (jnp.int32(0), jnp.int32(0)))
    plan[LEAF_MOST] = count


def own_kernel(
    n_row,
    n_col,
    leaf_first,
    leaf_owner,
    skeleton,
    frontal,
    slab,
    held,
    total,
    source,
    plan,
    first,
    owners,
    skel,
    near,
    used,
    table_sems,
    slab_sem,
    sems,
):
    group_rows = frontal.shape[0]
    depth = slab.shape[1]
    leaves = leaf_first.shape[0]
    per_group = leaves // n_row
    per_owner = 2 * group_rows // n_col // UNIT
    units = group_rows // UNIT
    row_pos = lax.axis_index("row")
    tables = [
        pltpu.make_async_copy(leaf_first, first, table_sems.at[0]),
        pltpu.make_async_copy(leaf_owner, owners, table_sems.at[1]),
        pltpu.make_async_copy(skeleton, skel, table_sems.at[2]),
    ]
    bring = pltpu.make_async_copy(slab, near, slab_sem)
    moves = []
    for k in range(n_row):
        lanes = pl.ds(pl.multiple_of((row_pos ^ k) * depth, LANES), depth)
        moves.append(
            pltpu.make_async_copy(frontal.at[:, lanes], held.at[:, lanes], sems.at[k])
        )
    for copy in tables + [bring] + moves:
        copy.start()

    def clear(at, carry):
        source[at] = units
        used[at // per_owner] = 0
        return carry

    lax.fori_loop(0, n_col * per_owner, clear, 0)
    for copy in tables:
        copy.wait()

    def place(unit, leaf):
        row = row_pos * group_rows + unit * UNIT
        later = jnp.minimum(leaf + 1, leaves - 1)
        moved = (leaf + 1 < leaves) & (first[later] <= row)
        leaf = jnp.where(moved, later, leaf)
        owner = owners[leaf]
        slot = used[owner]
        used[owner] = slot + 1
        source[owner * per_owner + slot] = unit
        return leaf

    lax.fori_loop(0, units, place, row_pos * per_group)
    plan_leaves(n_row, group_rows, per_owner * UNIT, first, owners, skel, plan)
    bring.wait()
    moves[0].wait()
    clear_runs(0, n_row, depth, held, first)
    multiply((0,), held, (near,), None, total)
    for k in range(1, n_row):
        moves[k].wait()
        clear_runs(k, n_row, depth, held, first)


def middle_kernel(pick, frontal, begun, *refs):
    multiply(pick, frontal, refs[: len(pick)], begun, refs[len(pick)])


def lay(other, source, total, out):
    chips, half, wide = out.shape
    per_half = half // UNIT
    core = lax.rem(lax.axis_index("col"), 2)
    chip = lax.axis_index("col") // 2
    lane = lax.broadcasted_iota(jnp.int32, (UNIT, wide), 1)

    def one(turn, carry):
        owner = (chip ^ turn) * 2 + (core ^ other)
        for at in range(per_half):
            values = []
            for side in range(2):
                unit = source[owner * (2 * per_half) + side * per_half + at]
                values.append(total[pl.ds(pl.multiple_of(unit * UNIT, UNIT), UNIT), :])
            out[turn, pl.ds(at * UNIT, UNIT), :] = jnp.where(lane < wide // 2, *values)
        return carry

    lax.fori_loop(0, chips, one, 0, unroll=min(chips, 4))


def last_kernel(pick, source, frontal, begun, *refs):
    slabs, (swap, total) = refs[: len(pick)], refs[len(pick) :]
    group_rows = frontal.shape[0]
    total[pl.ds(group_rows, UNIT), :] = jnp.zeros((UNIT, total.shape[1]), jnp.float32)
    multiply(pick, frontal, slabs, begun, total)
    lay(1, source, total, swap)


def keep_kernel(source, total, keep):
    lay(0, source, total, keep)


def vmem(count=None):
    spec = pl.BlockSpec(memory_space=pltpu.VMEM)
    return spec if count is None else [spec] * count


def smem():
    return pl.BlockSpec(memory_space=pltpu.SMEM)


def hbm():
    return pl.BlockSpec(memory_space=pltpu.HBM)


def in_hbm(value):
    return pltpu.with_memory_space_constraint(value, pltpu.HBM)


def product_cost(frontal, slabs):
    group_rows = frontal.shape[0]
    samples, depth = slabs[0].shape
    return pl.CostEstimate(
        flops=8 * group_rows * depth * samples * len(slabs),
        bytes_accessed=2 * group_rows * depth * len(slabs),
        transcendentals=0,
    )


def own_product(frontal, slab, leaf_first, leaf_owner, skeleton, n_row, n_col):
    group_rows, width = frontal.shape
    samples, depth = slab.shape
    per_owner = 2 * group_rows // n_col // UNIT
    leaves = leaf_first.shape[0]
    return pl.pallas_call(
        functools.partial(own_kernel, n_row, n_col),
        in_specs=[hbm()] * 5,
        out_specs=[vmem(), vmem(), smem(), smem()],
        out_shape=[
            jax.ShapeDtypeStruct(frontal.shape, frontal.dtype),
            jax.ShapeDtypeStruct((group_rows, 2 * samples), jnp.float32),
            jax.ShapeDtypeStruct((n_col * per_owner,), jnp.int32),
            jax.ShapeDtypeStruct((PICKS + LEAF_MOST * skeleton.shape[0],), jnp.int32),
        ],
        scratch_shapes=[
            pltpu.SMEM((leaves,), jnp.int32),
            pltpu.SMEM((leaves,), jnp.int32),
            pltpu.SMEM(skeleton.shape, jnp.int32),
            pltpu.VMEM((samples, depth), slab.dtype),
            pltpu.SMEM((n_col,), jnp.int32),
            pltpu.SemaphoreType.DMA((3,)),
            pltpu.SemaphoreType.DMA,
            pltpu.SemaphoreType.DMA((n_row,)),
        ],
        cost_estimate=product_cost(frontal, [slab] * n_row),
        compiler_params=pltpu.CompilerParams(vmem_limit_bytes=24 * 2**20),
    )(*(in_hbm(x) for x in (leaf_first, leaf_owner, skeleton, frontal, slab)))


def middle_product(frontal, begun, slabs, pick):
    return pl.pallas_call(
        functools.partial(middle_kernel, pick),
        in_specs=vmem(2 + len(slabs)),
        out_specs=vmem(),
        out_shape=jax.ShapeDtypeStruct(begun.shape, jnp.float32),
        cost_estimate=product_cost(frontal, slabs),
        compiler_params=pltpu.CompilerParams(vmem_limit_bytes=24 * 2**20),
    )(frontal, begun, *slabs)


def last_product(frontal, begun, source, slabs, pick, n_col):
    group_rows, wide = begun.shape
    block = jax.ShapeDtypeStruct((n_col // 2, group_rows // n_col, wide), jnp.float32)
    return pl.pallas_call(
        functools.partial(last_kernel, pick),
        in_specs=[smem()] + vmem(2 + len(slabs)),
        out_specs=vmem(2),
        out_shape=[block, jax.ShapeDtypeStruct((group_rows + UNIT, wide), jnp.float32)],
        cost_estimate=product_cost(frontal, slabs),
        compiler_params=pltpu.CompilerParams(vmem_limit_bytes=24 * 2**20),
    )(source, frontal, begun, *slabs)


def keep_rows(total, source, n_col):
    group_rows, wide = total.shape[0] - UNIT, total.shape[1]
    return pl.pallas_call(
        keep_kernel,
        in_specs=[smem(), vmem()],
        out_specs=vmem(),
        out_shape=jax.ShapeDtypeStruct((n_col // 2, group_rows // n_col, wide), jnp.float32),
        cost_estimate=pl.CostEstimate(
            flops=group_rows * wide, bytes_accessed=8 * group_rows * wide, transcendentals=0
        ),
        compiler_params=pltpu.CompilerParams(vmem_limit_bytes=24 * 2**20),
    )(source, total)


def leaf_kernel(
    skel, plan, *refs
):
    parts = refs[:-5]
    mine_out, coeff_out, worst_out, mine, picked = refs[-5:]
    half, wide = parts[0].shape
    samples = wide // 2
    capacity = 2 * half
    every = LEAF_MOST * skel

    total = parts[0][...]
    for part in parts[1:]:
        total = total + part[...]
    mine[pl.ds(0, half), :] = total
    mine[pl.ds(half, half), :] = pltpu.roll(total, samples, 1)
    turned = total.T
    mine_t = jnp.concatenate([turned[:samples], turned[samples:]], axis=1)
    mine_out[...] = mine_t

    mine[pl.ds(capacity, 8), :] = jnp.zeros((8, wide), jnp.float32)
    for k in range(every):
        picked[pl.ds(k, 1), :] = mine[pl.ds(plan[PICKS + k], 1), :]
    begins = [plan[b] for b in range(LEAF_MOST)]
    count = plan[LEAF_MOST]
    chosen = picked[:, :samples]

    gram = nt_dot(chosen, chosen, HIGHEST)
    proj = jnp.dot(chosen, mine_t, precision=HIGHEST, preferred_element_type=jnp.float32)

    slot = lax.broadcasted_iota(jnp.int32, (skel, capacity), 1)
    rank = jnp.zeros((skel, capacity), jnp.int32)
    for b in range(1, LEAF_MOST):
        rank += (slot >= begins[b]).astype(jnp.int32)
    hot = [rank == b for b in range(LEAF_MOST)]
    hot_rows = jnp.concatenate([h.astype(jnp.float32) for h in hot], axis=0)

    lane_leaf = lax.broadcasted_iota(jnp.int32, (skel, every), 1) // skel
    lane_row = lax.broadcasted_iota(jnp.int32, (skel, every), 1) % skel
    down = lax.broadcasted_iota(jnp.int32, (skel, every), 0)
    joined = jnp.where((down == lane_row) & (count == 0), 1.0, 0.0)
    for b in range(LEAF_MOST):
        joined += jnp.where(lane_leaf == b, gram[b * skel : (b + 1) * skel], 0.0)
    spread = jnp.concatenate([jnp.where(lane_row == i, joined, 0.0) for i in range(skel)], axis=0)
    system = jnp.dot(spread, hot_rows, precision=HIGHEST, preferred_element_type=jnp.float32)

    lines = [system[i * skel : (i + 1) * skel] for i in range(skel)]
    right = jnp.zeros((skel, capacity), jnp.float32)
    for b in range(LEAF_MOST):
        right += jnp.where(hot[b], proj[b * skel : (b + 1) * skel], 0.0)
    index = lax.broadcasted_iota(jnp.int32, (skel, capacity), 0)
    uppers = []
    pivots = []
    for j in range(skel):
        line = lines[j]
        inverse = 1.0 / line[j : j + 1]
        upper = line * inverse
        uppers.append(upper)
        pivots.append(inverse)
        for i in range(j + 1, skel):
            lines[i] = lines[i] - line[i : i + 1] * upper
        right = right - jnp.where(index > j, upper * right[j : j + 1], 0.0)
    solved = right * jnp.concatenate(pivots, axis=0)
    for j in range(skel - 2, -1, -1):
        known = jnp.where(index > j, uppers[j] * solved, 0.0)
        less = jnp.sum(known, axis=0, keepdims=True)
        solved = jnp.where(index == j, solved - less, solved)
    coeff_out[...] = solved

    weights = jnp.concatenate([jnp.where(h, solved, 0.0) for h in hot], axis=0)
    rebuilt = lax.dot_general(
        chosen,
        weights,
        (((0,), (0,)), ((), ())),
        precision=HIGHEST,
        preferred_element_type=jnp.float32,
    )
    resid = mine_t - rebuilt
    err = jnp.sum(resid * resid, axis=0, keepdims=True)
    norm = jnp.sum(mine_t * mine_t, axis=0, keepdims=True)
    worst = jnp.zeros((1, 1), jnp.float32)
    for b in range(LEAF_MOST):
        near = hot[b][:1]
        err_leaf = jnp.sum(jnp.where(near, err, 0.0), axis=1, keepdims=True)
        norm_leaf = jnp.sum(jnp.where(near, norm, 0.0), axis=1, keepdims=True)
        worst = jnp.maximum(worst, jnp.sqrt(err_leaf) / jnp.sqrt(norm_leaf + 1e-06))
    worst_out[...] = jnp.broadcast_to(worst, worst_out.shape)


def leaf_work(parts, plan):
    half, wide = parts[0].shape
    samples = wide // 2
    skel = (plan.shape[0] - PICKS) // LEAF_MOST
    return pl.pallas_call(
        functools.partial(leaf_kernel, skel),
        in_specs=[smem()] + vmem(len(parts)),
        out_specs=vmem(3),
        out_shape=[
            jax.ShapeDtypeStruct((samples, 2 * half), jnp.float32),
            jax.ShapeDtypeStruct((skel, 2 * half), jnp.float32),
            jax.ShapeDtypeStruct((1, LANES), jnp.float32),
        ],
        scratch_shapes=[
            pltpu.VMEM((2 * half + 8, wide), jnp.float32),
            pltpu.VMEM((LEAF_MOST * skel, wide), jnp.float32),
        ],
        compiler_params=pltpu.CompilerParams(vmem_limit_bytes=12 * 2**20),
    )(plan, *parts)


def exchange(value, axis, flip):
    pairs = [(k, k ^ flip) for k in range(lax.axis_size(axis))]
    return lax.ppermute(value, axis, pairs)


def largest(value, axes):
    size = lax.axis_size(axes)
    strides = [1]
    while strides[-1] * FAN < size:
        strides.append(strides[-1] * FAN)

    def pass_on(value, stride, up):
        others = []
        for k in range(1, FAN):
            pairs = [(at + k * stride, at) for at in range(0, size, FAN * stride)]
            pairs = [pair for pair in pairs if pair[0] < size]
            if pairs:
                pairs = pairs if up else [pair[::-1] for pair in pairs]
                others.append(lax.ppermute(value, axes, pairs))
        return functools.reduce(jnp.maximum, others, value)

    for stride in strides:
        value = pass_on(value, stride, True)
    for stride in strides[::-1]:
        value = pass_on(value, stride, False)
    return value


def local(frontal, sample_cols, leaf_first, leaf_owner, skeleton):
    n_col = lax.axis_size("col")
    n_row = lax.axis_size("row")
    own = sample_cols.T
    slabs = [exchange(own, "row", k) for k in range(1, n_row)]
    held, begun, source, plan = own_product(
        frontal, own, leaf_first, leaf_owner, skeleton.T, n_row, n_col
    )
    pick = tuple(range(1, n_row))
    begun = middle_product(held, begun, slabs[:-1], pick[:-1])
    swap, total = last_product(held, begun, source, slabs[-1:], pick[-1:], n_col)
    swapped = exchange(swap, "col", 1)
    summed = keep_rows(total, source, n_col) + swapped
    parts = [summed[0]] + [exchange(summed[k], "col", 2 * k) for k in range(1, n_col // 2)]
    mine, coeff, worst = leaf_work(parts, plan)
    worst = largest(worst, ("row", "col"))
    return (mine, coeff, worst[0, :1])


def solution(mesh):
    return jax.shard_map(
        local,
        mesh=mesh,
        in_specs=(P("row", "col"), P(("col", "row"), None), P(), P(), P()),
        out_specs=(P("row", "col"), P("row", "col"), P()),
        check_vma=False,
    )
```

```python
import functools

import jax
import jax.numpy as jnp
from jax import lax
from jax.experimental import pallas as pl
from jax.experimental.pallas import tpu as pltpu
from jax.sharding import PartitionSpec as P

UNIT = 32
LANES = 128
LEAF_MOST = 4
PICKS = 8
LEVELS = 32760.0
EXTRA = 16
STEPS = 64.0
RUN_LEAVES = 4
HIGHEST = lax.Precision.HIGHEST


def nt_dot(a, b, precision=None):
    return lax.dot_general(
        a, b, (((1,), (1,)), ((), ())), precision=precision, preferred_element_type=jnp.float32
    )


def clear_runs(pick, n_row, depth, frontal, leaf_first):
    group_rows, width = frontal.shape
    per_group = leaf_first.shape[0] // n_row
    runs = per_group // RUN_LEAVES
    run_rows = group_rows // runs
    row_pos = lax.axis_index("row")
    first_col = lax.axis_index("col") * width

    def clear(at, carry):
        run = at // (run_rows // LANES)
        begin = row_pos * group_rows + run * run_rows
        begin_col = row_pos * group_rows + at * LANES
        inside = begin_col - first_col
        held = (inside >= 0) & (inside < width)
        inside = jnp.clip(inside, 0, width - LANES)

        @pl.when(held & (((inside // depth) ^ row_pos) == pick))
        def _():
            rows = pl.ds(pl.multiple_of(run * run_rows, run_rows), run_rows)
            lanes = pl.ds(pl.multiple_of(inside, LANES), LANES)
            part = frontal[rows, lanes]
            down = lax.broadcasted_iota(jnp.int32, part.shape, 0) + begin
            across = lax.broadcasted_iota(jnp.int32, part.shape, 1) + begin_col
            leaf_down = jnp.zeros(part.shape, jnp.int32)
            leaf_across = jnp.zeros(part.shape, jnp.int32)
            for k in range(1, RUN_LEAVES):
                edge = leaf_first[row_pos * per_group + run * RUN_LEAVES + k]
                leaf_down += (down >= edge).astype(jnp.int32)
                leaf_across += (across >= edge).astype(jnp.int32)
            kept = jnp.where(leaf_down == leaf_across, 0.0, part.astype(jnp.float32))
            frontal[rows, lanes] = kept.astype(jnp.bfloat16)

        return carry

    lax.fori_loop(0, group_rows // LANES, clear, 0)


def multiply(pick, frontal, slabs, begun, total):
    group_rows = frontal.shape[0]
    depth = slabs[0].shape[1]
    row_pos = lax.axis_index("row")
    part = min(group_rows, 512)

    def rows_of(at, carry):
        rows = pl.ds(pl.multiple_of(at * part, part), part)
        value = None if begun is None else begun[rows, :]
        for k, slab in zip(pick, slabs):
            begin = pl.multiple_of((row_pos ^ k) * depth, LANES)
            twice = jnp.concatenate([slab[...], slab[...]], axis=0)
            add = nt_dot(frontal[rows, pl.ds(begin, depth)], twice)
            value = add if value is None else value + add
        total[rows, :] = value
        return carry

    lax.fori_loop(0, group_rows // part, rows_of, 0)


def plan_leaves(n_row, group_rows, capacity, first, owners, skel, plan):
    leaves = first.shape[0]
    per_group = leaves // n_row
    count_skel = skel.shape[0]
    row_pos = lax.axis_index("row")
    col_pos = lax.axis_index("col")

    def clear(at, carry):
        plan[at] = capacity
        return carry

    lax.fori_loop(0, plan.shape[0], clear, 0)

    def find(at, carry):
        count, filled = carry
        leaf = row_pos * per_group + at
        begin = first[leaf]
        following = first[jnp.minimum(leaf + 1, leaves - 1)]
        end = jnp.where(at + 1 < per_group, following, (row_pos + 1) * group_rows)
        hit = (owners[leaf] == col_pos) & (count < LEAF_MOST)

        @pl.when(hit)
        def _():
            plan[count] = filled
            for k in range(count_skel):
                plan[PICKS + count * count_skel + k] = filled + skel[k, leaf] - begin

        return jnp.where(hit, count + 1, count), jnp.where(hit, filled + end - begin, filled)

    count, _ = lax.fori_loop(0, per_group, find, (jnp.int32(0), jnp.int32(0)))
    plan[LEAF_MOST] = count


def own_kernel(
    n_row,
    n_col,
    leaf_first,
    leaf_owner,
    skeleton,
    frontal,
    slab,
    held,
    total,
    source,
    plan,
    first,
    owners,
    skel,
    near,
    used,
    table_sems,
    slab_sem,
    sems,
):
    group_rows = frontal.shape[0]
    depth = slab.shape[1]
    leaves = leaf_first.shape[0]
    per_group = leaves // n_row
    per_owner = 2 * group_rows // n_col // UNIT
    units = group_rows // UNIT
    row_pos = lax.axis_index("row")
    tables = [
        pltpu.make_async_copy(leaf_first, first, table_sems.at[0]),
        pltpu.make_async_copy(leaf_owner, owners, table_sems.at[1]),
        pltpu.make_async_copy(skeleton, skel, table_sems.at[2]),
    ]
    bring = pltpu.make_async_copy(slab, near, slab_sem)
    moves = []
    for k in range(n_row):
        lanes = pl.ds(pl.multiple_of((row_pos ^ k) * depth, LANES), depth)
        moves.append(
            pltpu.make_async_copy(frontal.at[:, lanes], held.at[:, lanes], sems.at[k])
        )
    for copy in tables + [bring] + moves:
        copy.start()

    def clear(at, carry):
        source[at] = units
        used[at // per_owner] = 0
        return carry

    lax.fori_loop(0, n_col * per_owner, clear, 0)
    for copy in tables:
        copy.wait()

    def place(unit, leaf):
        row = row_pos * group_rows + unit * UNIT
        later = jnp.minimum(leaf + 1, leaves - 1)
        moved = (leaf + 1 < leaves) & (first[later] <= row)
        leaf = jnp.where(moved, later, leaf)
        owner = owners[leaf]
        slot = used[owner]
        used[owner] = slot + 1
        source[owner * per_owner + slot] = unit
        return leaf

    lax.fori_loop(0, units, place, row_pos * per_group)
    plan_leaves(n_row, group_rows, per_owner * UNIT, first, owners, skel, plan)
    bring.wait()
    moves[0].wait()
    clear_runs(0, n_row, depth, held, first)
    multiply((0,), held, (near,), None, total)
    for k in range(1, n_row):
        moves[k].wait()
        clear_runs(k, n_row, depth, held, first)


def middle_kernel(pick, frontal, begun, *refs):
    multiply(pick, frontal, refs[: len(pick)], begun, refs[len(pick)])


def lay(other, source, total, out):
    chips, half, wide = out.shape
    per_half = half // UNIT
    core = lax.rem(lax.axis_index("col"), 2)
    chip = lax.axis_index("col") // 2
    lane = lax.broadcasted_iota(jnp.int32, (UNIT, wide), 1)

    def one(turn, carry):
        owner = (chip ^ turn) * 2 + (core ^ other)
        for at in range(per_half):
            values = []
            for side in range(2):
                unit = source[owner * (2 * per_half) + side * per_half + at]
                values.append(total[pl.ds(pl.multiple_of(unit * UNIT, UNIT), UNIT), :])
            out[turn, pl.ds(at * UNIT, UNIT), :] = jnp.where(lane < wide // 2, *values)
        return carry

    lax.fori_loop(0, chips, one, 0, unroll=min(chips, 4))


def last_kernel(pick, source, frontal, begun, *refs):
    slabs, (swap, total) = refs[: len(pick)], refs[len(pick) :]
    group_rows = frontal.shape[0]
    total[pl.ds(group_rows, UNIT), :] = jnp.zeros((UNIT, total.shape[1]), jnp.float32)
    multiply(pick, frontal, slabs, begun, total)
    lay(1, source, total, swap)


def keep_kernel(source, total, keep):
    lay(0, source, total, keep)


def vmem(count=None):
    spec = pl.BlockSpec(memory_space=pltpu.VMEM)
    return spec if count is None else [spec] * count


def smem():
    return pl.BlockSpec(memory_space=pltpu.SMEM)


def hbm():
    return pl.BlockSpec(memory_space=pltpu.HBM)


def in_hbm(value):
    return pltpu.with_memory_space_constraint(value, pltpu.HBM)


def product_cost(frontal, slabs):
    group_rows = frontal.shape[0]
    samples, depth = slabs[0].shape
    return pl.CostEstimate(
        flops=8 * group_rows * depth * samples * len(slabs),
        bytes_accessed=2 * group_rows * depth * len(slabs),
        transcendentals=0,
    )


def own_product(frontal, slab, leaf_first, leaf_owner, skeleton, n_row, n_col):
    group_rows, width = frontal.shape
    samples, depth = slab.shape
    per_owner = 2 * group_rows // n_col // UNIT
    leaves = leaf_first.shape[0]
    return pl.pallas_call(
        functools.partial(own_kernel, n_row, n_col),
        in_specs=[hbm()] * 5,
        out_specs=[vmem(), vmem(), smem(), smem()],
        out_shape=[
            jax.ShapeDtypeStruct(frontal.shape, frontal.dtype),
            jax.ShapeDtypeStruct((group_rows, 2 * samples), jnp.float32),
            jax.ShapeDtypeStruct((n_col * per_owner,), jnp.int32),
            jax.ShapeDtypeStruct((PICKS + LEAF_MOST * skeleton.shape[0],), jnp.int32),
        ],
        scratch_shapes=[
            pltpu.SMEM((leaves,), jnp.int32),
            pltpu.SMEM((leaves,), jnp.int32),
            pltpu.SMEM(skeleton.shape, jnp.int32),
            pltpu.VMEM((samples, depth), slab.dtype),
            pltpu.SMEM((n_col,), jnp.int32),
            pltpu.SemaphoreType.DMA((3,)),
            pltpu.SemaphoreType.DMA,
            pltpu.SemaphoreType.DMA((n_row,)),
        ],
        cost_estimate=product_cost(frontal, [slab] * n_row),
        compiler_params=pltpu.CompilerParams(vmem_limit_bytes=24 * 2**20),
    )(*(in_hbm(x) for x in (leaf_first, leaf_owner, skeleton, frontal, slab)))


def middle_product(frontal, begun, slabs, pick):
    return pl.pallas_call(
        functools.partial(middle_kernel, pick),
        in_specs=vmem(2 + len(slabs)),
        out_specs=vmem(),
        out_shape=jax.ShapeDtypeStruct(begun.shape, jnp.float32),
        cost_estimate=product_cost(frontal, slabs),
        compiler_params=pltpu.CompilerParams(vmem_limit_bytes=24 * 2**20),
    )(frontal, begun, *slabs)


def last_product(frontal, begun, source, slabs, pick, n_col):
    group_rows, wide = begun.shape
    block = jax.ShapeDtypeStruct((n_col // 2, group_rows // n_col, wide), jnp.float32)
    return pl.pallas_call(
        functools.partial(last_kernel, pick),
        in_specs=[smem()] + vmem(2 + len(slabs)),
        out_specs=vmem(2),
        out_shape=[block, jax.ShapeDtypeStruct((group_rows + UNIT, wide), jnp.float32)],
        cost_estimate=product_cost(frontal, slabs),
        compiler_params=pltpu.CompilerParams(vmem_limit_bytes=24 * 2**20),
    )(source, frontal, begun, *slabs)


def keep_rows(total, source, n_col):
    group_rows, wide = total.shape[0] - UNIT, total.shape[1]
    return pl.pallas_call(
        keep_kernel,
        in_specs=[smem(), vmem()],
        out_specs=vmem(),
        out_shape=jax.ShapeDtypeStruct((n_col // 2, group_rows // n_col, wide), jnp.float32),
        cost_estimate=pl.CostEstimate(
            flops=group_rows * wide, bytes_accessed=8 * group_rows * wide, transcendentals=0
        ),
        compiler_params=pltpu.CompilerParams(vmem_limit_bytes=24 * 2**20),
    )(source, total)


def squeeze_kernel(keep, swapped, here, *away):
    samples = keep.shape[2] // 2
    here[...] = (keep[0] + swapped[0]).T
    row = lax.broadcasted_iota(jnp.int32, (EXTRA, keep.shape[1]), 0)
    for k, out in enumerate(away):
        block = (keep[k + 1] + swapped[k + 1]).T
        tail = jnp.zeros(row.shape, jnp.float32)
        for side in range(2):
            rows = slice(side * samples, (side + 1) * samples)
            part = block[rows]
            most = jnp.maximum(jnp.max(jnp.abs(part), axis=0, keepdims=True), 1e-30)
            power = jnp.ceil(jnp.log2(most) * STEPS)
            scaled = part * (LEVELS * jnp.exp2(power * (-1.0 / STEPS)))
            whole = jnp.floor(scaled + 0.5).astype(jnp.int32)
            out[rows, :] = whole.astype(jnp.int16)
            tail = jnp.where(row == side, power, tail)
        out[pl.ds(2 * samples, EXTRA), :] = tail.astype(jnp.int32).astype(jnp.int16)


def squeeze(keep, swapped):
    chips, half, wide = keep.shape
    small = jax.ShapeDtypeStruct((wide + EXTRA, half), jnp.int16)
    return pl.pallas_call(
        squeeze_kernel,
        in_specs=vmem(2),
        out_specs=vmem(chips),
        out_shape=[jax.ShapeDtypeStruct((wide, half), jnp.float32)] + [small] * (chips - 1),
        compiler_params=pltpu.CompilerParams(vmem_limit_bytes=24 * 2**20),
    )(keep, swapped)


def leaf_kernel(
    skel, plan, *refs
):
    here, *parts = refs[:-5]
    mine_out, coeff_out, worst_out, mine, picked = refs[-5:]
    wide, half = here.shape
    samples = wide // 2
    capacity = 2 * half
    every = LEAF_MOST * skel

    sides = [here[pl.ds(0, samples), :], here[pl.ds(samples, samples), :]]
    for part in parts:
        tail = part[pl.ds(wide, EXTRA), :].astype(jnp.int32).astype(jnp.float32)
        step = jnp.exp2(tail * (1.0 / STEPS)) * (1.0 / LEVELS)
        for side in range(2):
            value = part[pl.ds(side * samples, samples), :].astype(jnp.int32).astype(jnp.float32)
            sides[side] = sides[side] + value * step[side : side + 1]
    mine_t = jnp.concatenate(sides, axis=1)
    mine_out[...] = mine_t
    total = jnp.concatenate(sides, axis=0).T
    mine[pl.ds(0, half), :] = total
    mine[pl.ds(half, half), :] = pltpu.roll(total, samples, 1)
    mine[pl.ds(capacity, 8), :] = jnp.zeros((8, wide), jnp.float32)
    for k in range(every):
        picked[pl.ds(k, 1), :] = mine[pl.ds(plan[PICKS + k], 1), :]
    begins = [plan[b] for b in range(LEAF_MOST)]
    count = plan[LEAF_MOST]
    chosen = picked[:, :samples]

    gram = nt_dot(chosen, chosen, HIGHEST)
    proj = jnp.dot(chosen, mine_t, precision=HIGHEST, preferred_element_type=jnp.float32)

    slot = lax.broadcasted_iota(jnp.int32, (skel, capacity), 1)
    rank = jnp.zeros((skel, capacity), jnp.int32)
    for b in range(1, LEAF_MOST):
        rank += (slot >= begins[b]).astype(jnp.int32)
    hot = [rank == b for b in range(LEAF_MOST)]
    hot_rows = jnp.concatenate([h.astype(jnp.float32) for h in hot], axis=0)

    lane_leaf = lax.broadcasted_iota(jnp.int32, (skel, every), 1) // skel
    lane_row = lax.broadcasted_iota(jnp.int32, (skel, every), 1) % skel
    down = lax.broadcasted_iota(jnp.int32, (skel, every), 0)
    joined = jnp.where((down == lane_row) & (count == 0), 1.0, 0.0)
    for b in range(LEAF_MOST):
        joined += jnp.where(lane_leaf == b, gram[b * skel : (b + 1) * skel], 0.0)
    spread = jnp.concatenate([jnp.where(lane_row == i, joined, 0.0) for i in range(skel)], axis=0)
    system = jnp.dot(spread, hot_rows, precision=HIGHEST, preferred_element_type=jnp.float32)

    lines = [system[i * skel : (i + 1) * skel] for i in range(skel)]
    right = jnp.zeros((skel, capacity), jnp.float32)
    for b in range(LEAF_MOST):
        right += jnp.where(hot[b], proj[b * skel : (b + 1) * skel], 0.0)
    index = lax.broadcasted_iota(jnp.int32, (skel, capacity), 0)
    uppers = []
    pivots = []
    for j in range(skel):
        line = lines[j]
        inverse = 1.0 / line[j : j + 1]
        upper = line * inverse
        uppers.append(upper)
        pivots.append(inverse)
        for i in range(j + 1, skel):
            lines[i] = lines[i] - line[i : i + 1] * upper
        right = right - jnp.where(index > j, upper * right[j : j + 1], 0.0)
    solved = right * jnp.concatenate(pivots, axis=0)
    for j in range(skel - 2, -1, -1):
        known = jnp.where(index > j, uppers[j] * solved, 0.0)
        less = jnp.sum(known, axis=0, keepdims=True)
        solved = jnp.where(index == j, solved - less, solved)
    coeff_out[...] = solved

    weights = jnp.concatenate([jnp.where(h, solved, 0.0) for h in hot], axis=0)
    rebuilt = lax.dot_general(
        chosen,
        weights,
        (((0,), (0,)), ((), ())),
        precision=HIGHEST,
        preferred_element_type=jnp.float32,
    )
    resid = mine_t - rebuilt
    err = jnp.sum(resid * resid, axis=0, keepdims=True)
    norm = jnp.sum(mine_t * mine_t, axis=0, keepdims=True)
    worst = jnp.zeros((1, 1), jnp.float32)
    for b in range(LEAF_MOST):
        near = hot[b][:1]
        err_leaf = jnp.sum(jnp.where(near, err, 0.0), axis=1, keepdims=True)
        norm_leaf = jnp.sum(jnp.where(near, norm, 0.0), axis=1, keepdims=True)
        worst = jnp.maximum(worst, jnp.sqrt(err_leaf) / jnp.sqrt(norm_leaf + 1e-06))
    worst_out[...] = jnp.broadcast_to(worst, worst_out.shape)


def leaf_work(here, parts, plan):
    wide, half = here.shape
    samples = wide // 2
    skel = (plan.shape[0] - PICKS) // LEAF_MOST
    return pl.pallas_call(
        functools.partial(leaf_kernel, skel),
        in_specs=[smem()] + vmem(1 + len(parts)),
        out_specs=vmem(3),
        out_shape=[
            jax.ShapeDtypeStruct((samples, 2 * half), jnp.float32),
            jax.ShapeDtypeStruct((skel, 2 * half), jnp.float32),
            jax.ShapeDtypeStruct((1, LANES), jnp.float32),
        ],
        scratch_shapes=[
            pltpu.VMEM((2 * half + 8, wide), jnp.float32),
            pltpu.VMEM((LEAF_MOST * skel, wide), jnp.float32),
        ],
        compiler_params=pltpu.CompilerParams(vmem_limit_bytes=12 * 2**20),
    )(plan, here, *parts)


def exchange(value, axis, flip):
    pairs = [(k, k ^ flip) for k in range(lax.axis_size(axis))]
    return lax.ppermute(value, axis, pairs)


def largest(value, axes):
    size = lax.axis_size(axes)
    every = jnp.broadcast_to(value[None], (size, *value.shape))
    return jnp.max(lax.all_to_all(every, axes, 0, 0), axis=0)


def local(frontal, sample_cols, leaf_first, leaf_owner, skeleton):
    n_col = lax.axis_size("col")
    n_row = lax.axis_size("row")
    own = sample_cols.T
    slabs = [exchange(own, "row", k) for k in range(1, n_row)]
    held, begun, source, plan = own_product(
        frontal, own, leaf_first, leaf_owner, skeleton.T, n_row, n_col
    )
    pick = tuple(range(1, n_row))
    begun = middle_product(held, begun, slabs[:-1], pick[:-1])
    swap, total = last_product(held, begun, source, slabs[-1:], pick[-1:], n_col)
    swapped = exchange(swap, "col", 1)
    here, *away = squeeze(keep_rows(total, source, n_col), swapped)
    parts = [exchange(value, "col", 2 * (k + 1)) for k, value in enumerate(away)]
    mine, coeff, worst = leaf_work(here, parts, plan)
    worst = largest(worst, ("row", "col"))
    return (mine, coeff, worst[0, :1])


def solution(mesh):
    return jax.shard_map(
        local,
        mesh=mesh,
        in_specs=(P("row", "col"), P(("col", "row"), None), P(), P(), P()),
        out_specs=(P("row", "col"), P("row", "col"), P()),
        check_vma=False,
    )
```

```python
import functools

import jax
import jax.numpy as jnp
from jax import lax
from jax.experimental import pallas as pl
from jax.experimental.pallas import tpu as pltpu
from jax.sharding import PartitionSpec as P

UNIT = 32
LANES = 128
LEAF_MOST = 4
PICKS = 8
LEVELS = 32760.0
EXTRA = 16
STEPS = 64.0
RUN_LEAVES = 4
HIGHEST = lax.Precision.HIGHEST


def nt_dot(a, b, precision=None):
    return lax.dot_general(
        a, b, (((1,), (1,)), ((), ())), precision=precision, preferred_element_type=jnp.float32
    )


def clear_runs(pick, n_row, depth, frontal, leaf_first):
    group_rows, width = frontal.shape
    per_group = leaf_first.shape[0] // n_row
    runs = per_group // RUN_LEAVES
    run_rows = group_rows // runs
    row_pos = lax.axis_index("row")
    first_col = lax.axis_index("col") * width

    def clear(at, carry):
        run = at // (run_rows // LANES)
        begin = row_pos * group_rows + run * run_rows
        begin_col = row_pos * group_rows + at * LANES
        inside = begin_col - first_col
        held = (inside >= 0) & (inside < width)
        inside = jnp.clip(inside, 0, width - LANES)

        @pl.when(held & (((inside // depth) ^ row_pos) == pick))
        def _():
            rows = pl.ds(pl.multiple_of(run * run_rows, run_rows), run_rows)
            lanes = pl.ds(pl.multiple_of(inside, LANES), LANES)
            part = frontal[rows, lanes]
            down = lax.broadcasted_iota(jnp.int32, part.shape, 0) + begin
            across = lax.broadcasted_iota(jnp.int32, part.shape, 1) + begin_col
            leaf_down = jnp.zeros(part.shape, jnp.int32)
            leaf_across = jnp.zeros(part.shape, jnp.int32)
            for k in range(1, RUN_LEAVES):
                edge = leaf_first[row_pos * per_group + run * RUN_LEAVES + k]
                leaf_down += (down >= edge).astype(jnp.int32)
                leaf_across += (across >= edge).astype(jnp.int32)
            kept = jnp.where(leaf_down == leaf_across, 0.0, part.astype(jnp.float32))
            frontal[rows, lanes] = kept.astype(jnp.bfloat16)

        return carry

    lax.fori_loop(0, group_rows // LANES, clear, 0)


def multiply(pick, frontal, slabs, begun, total):
    group_rows, width = frontal.shape
    depth = width // lax.axis_size("row")
    row_pos = lax.axis_index("row")
    part = min(group_rows, 512)

    def rows_of(at, carry):
        rows = pl.ds(pl.multiple_of(at * part, part), part)
        value = None if begun is None else begun[rows, :]
        for (k, offset), slab in zip(pick, slabs):
            begin = pl.multiple_of((row_pos ^ k) * depth + offset, LANES)
            twice = jnp.concatenate([slab[...], slab[...]], axis=0)
            add = nt_dot(frontal[rows, pl.ds(begin, slab.shape[1])], twice)
            value = add if value is None else value + add
        total[rows, :] = value
        return carry

    lax.fori_loop(0, group_rows // part, rows_of, 0)


def plan_leaves(n_row, group_rows, capacity, first, owners, skel, plan):
    leaves = first.shape[0]
    per_group = leaves // n_row
    count_skel = skel.shape[0]
    row_pos = lax.axis_index("row")
    col_pos = lax.axis_index("col")

    def clear(at, carry):
        plan[at] = capacity
        return carry

    lax.fori_loop(0, plan.shape[0], clear, 0)

    def find(at, carry):
        count, filled = carry
        leaf = row_pos * per_group + at
        begin = first[leaf]
        following = first[jnp.minimum(leaf + 1, leaves - 1)]
        end = jnp.where(at + 1 < per_group, following, (row_pos + 1) * group_rows)
        hit = (owners[leaf] == col_pos) & (count < LEAF_MOST)

        @pl.when(hit)
        def _():
            plan[count] = filled
            for k in range(count_skel):
                plan[PICKS + count * count_skel + k] = filled + skel[k, leaf] - begin

        return jnp.where(hit, count + 1, count), jnp.where(hit, filled + end - begin, filled)

    count, _ = lax.fori_loop(0, per_group, find, (jnp.int32(0), jnp.int32(0)))
    plan[LEAF_MOST] = count


def own_kernel(
    n_row,
    n_col,
    leaf_first,
    leaf_owner,
    skeleton,
    frontal,
    slab,
    held,
    total,
    source,
    plan,
    first,
    owners,
    skel,
    near,
    used,
    table_sems,
    slab_sem,
    sems,
):
    group_rows = frontal.shape[0]
    depth = slab.shape[1]
    leaves = leaf_first.shape[0]
    per_group = leaves // n_row
    per_owner = 2 * group_rows // n_col // UNIT
    units = group_rows // UNIT
    row_pos = lax.axis_index("row")
    tables = [
        pltpu.make_async_copy(leaf_first, first, table_sems.at[0]),
        pltpu.make_async_copy(leaf_owner, owners, table_sems.at[1]),
        pltpu.make_async_copy(skeleton, skel, table_sems.at[2]),
    ]
    bring = pltpu.make_async_copy(slab, near, slab_sem)
    moves = []
    for k in range(n_row):
        lanes = pl.ds(pl.multiple_of((row_pos ^ k) * depth, LANES), depth)
        moves.append(
            pltpu.make_async_copy(frontal.at[:, lanes], held.at[:, lanes], sems.at[k])
        )
    for copy in tables + [bring] + moves:
        copy.start()

    def clear(at, carry):
        source[at] = units
        used[at // per_owner] = 0
        return carry

    lax.fori_loop(0, n_col * per_owner, clear, 0)
    for copy in tables:
        copy.wait()

    def place(unit, leaf):
        row = row_pos * group_rows + unit * UNIT
        later = jnp.minimum(leaf + 1, leaves - 1)
        moved = (leaf + 1 < leaves) & (first[later] <= row)
        leaf = jnp.where(moved, later, leaf)
        owner = owners[leaf]
        slot = used[owner]
        used[owner] = slot + 1
        source[owner * per_owner + slot] = unit
        return leaf

    lax.fori_loop(0, units, place, row_pos * per_group)
    plan_leaves(n_row, group_rows, per_owner * UNIT, first, owners, skel, plan)
    bring.wait()
    moves[0].wait()
    clear_runs(0, n_row, depth, held, first)
    multiply(((0, 0),), held, (near,), None, total)
    for k in range(1, n_row):
        moves[k].wait()
        clear_runs(k, n_row, depth, held, first)


def middle_kernel(pick, frontal, begun, *refs):
    multiply(pick, frontal, refs[: len(pick)], begun, refs[len(pick)])


def lay(other, source, total, out):
    chips, half, wide = out.shape
    per_half = half // UNIT
    core = lax.rem(lax.axis_index("col"), 2)
    chip = lax.axis_index("col") // 2
    lane = lax.broadcasted_iota(jnp.int32, (UNIT, wide), 1)

    def one(turn, carry):
        owner = (chip ^ turn) * 2 + (core ^ other)
        for at in range(per_half):
            values = []
            for side in range(2):
                unit = source[owner * (2 * per_half) + side * per_half + at]
                values.append(total[pl.ds(pl.multiple_of(unit * UNIT, UNIT), UNIT), :])
            out[turn, pl.ds(at * UNIT, UNIT), :] = jnp.where(lane < wide // 2, *values)
        return carry

    lax.fori_loop(0, chips, one, 0, unroll=min(chips, 4))


def last_kernel(pick, source, frontal, begun, *refs):
    slabs, (swap, total) = refs[: len(pick)], refs[len(pick) :]
    group_rows = frontal.shape[0]
    total[pl.ds(group_rows, UNIT), :] = jnp.zeros((UNIT, total.shape[1]), jnp.float32)
    multiply(pick, frontal, slabs, begun, total)
    lay(1, source, total, swap)


def keep_kernel(source, total, keep):
    lay(0, source, total, keep)


def vmem(count=None):
    spec = pl.BlockSpec(memory_space=pltpu.VMEM)
    return spec if count is None else [spec] * count


def smem():
    return pl.BlockSpec(memory_space=pltpu.SMEM)


def hbm():
    return pl.BlockSpec(memory_space=pltpu.HBM)


def in_hbm(value):
    return pltpu.with_memory_space_constraint(value, pltpu.HBM)


def product_cost(frontal, slabs):
    group_rows = frontal.shape[0]
    samples = slabs[0].shape[0]
    depth = sum(slab.shape[1] for slab in slabs)
    return pl.CostEstimate(
        flops=8 * group_rows * depth * samples,
        bytes_accessed=2 * group_rows * depth,
        transcendentals=0,
    )


def own_product(frontal, slab, leaf_first, leaf_owner, skeleton, n_row, n_col):
    group_rows, width = frontal.shape
    samples, depth = slab.shape
    per_owner = 2 * group_rows // n_col // UNIT
    leaves = leaf_first.shape[0]
    return pl.pallas_call(
        functools.partial(own_kernel, n_row, n_col),
        in_specs=[hbm()] * 5,
        out_specs=[vmem(), vmem(), smem(), smem()],
        out_shape=[
            jax.ShapeDtypeStruct(frontal.shape, frontal.dtype),
            jax.ShapeDtypeStruct((group_rows, 2 * samples), jnp.float32),
            jax.ShapeDtypeStruct((n_col * per_owner,), jnp.int32),
            jax.ShapeDtypeStruct((PICKS + LEAF_MOST * skeleton.shape[0],), jnp.int32),
        ],
        scratch_shapes=[
            pltpu.SMEM((leaves,), jnp.int32),
            pltpu.SMEM((leaves,), jnp.int32),
            pltpu.SMEM(skeleton.shape, jnp.int32),
            pltpu.VMEM((samples, depth), slab.dtype),
            pltpu.SMEM((n_col,), jnp.int32),
            pltpu.SemaphoreType.DMA((3,)),
            pltpu.SemaphoreType.DMA,
            pltpu.SemaphoreType.DMA((n_row,)),
        ],
        cost_estimate=product_cost(frontal, [slab] * n_row),
        compiler_params=pltpu.CompilerParams(vmem_limit_bytes=24 * 2**20),
    )(*(in_hbm(x) for x in (leaf_first, leaf_owner, skeleton, frontal, slab)))


def middle_product(frontal, begun, slabs, pick):
    return pl.pallas_call(
        functools.partial(middle_kernel, pick),
        in_specs=vmem(2 + len(slabs)),
        out_specs=vmem(),
        out_shape=jax.ShapeDtypeStruct(begun.shape, jnp.float32),
        cost_estimate=product_cost(frontal, slabs),
        compiler_params=pltpu.CompilerParams(vmem_limit_bytes=24 * 2**20),
    )(frontal, begun, *slabs)


def last_product(frontal, begun, source, slabs, pick, n_col):
    group_rows, wide = begun.shape
    block = jax.ShapeDtypeStruct((n_col // 2, group_rows // n_col, wide), jnp.float32)
    return pl.pallas_call(
        functools.partial(last_kernel, pick),
        in_specs=[smem()] + vmem(2 + len(slabs)),
        out_specs=vmem(2),
        out_shape=[block, jax.ShapeDtypeStruct((group_rows + UNIT, wide), jnp.float32)],
        cost_estimate=product_cost(frontal, slabs),
        compiler_params=pltpu.CompilerParams(vmem_limit_bytes=24 * 2**20),
    )(source, frontal, begun, *slabs)


def keep_rows(total, source, n_col):
    group_rows, wide = total.shape[0] - UNIT, total.shape[1]
    return pl.pallas_call(
        keep_kernel,
        in_specs=[smem(), vmem()],
        out_specs=vmem(),
        out_shape=jax.ShapeDtypeStruct((n_col // 2, group_rows // n_col, wide), jnp.float32),
        cost_estimate=pl.CostEstimate(
            flops=group_rows * wide, bytes_accessed=8 * group_rows * wide, transcendentals=0
        ),
        compiler_params=pltpu.CompilerParams(vmem_limit_bytes=24 * 2**20),
    )(source, total)


def squeeze_kernel(keep, swapped, here, *away):
    samples = keep.shape[2] // 2
    here[...] = (keep[0] + swapped[0]).T
    row = lax.broadcasted_iota(jnp.int32, (EXTRA, keep.shape[1]), 0)
    for k, out in enumerate(away):
        block = (keep[k + 1] + swapped[k + 1]).T
        tail = jnp.zeros(row.shape, jnp.float32)
        for side in range(2):
            rows = slice(side * samples, (side + 1) * samples)
            part = block[rows]
            most = jnp.maximum(jnp.max(jnp.abs(part), axis=0, keepdims=True), 1e-30)
            power = jnp.ceil(jnp.log2(most) * STEPS)
            scaled = part * (LEVELS * jnp.exp2(power * (-1.0 / STEPS)))
            whole = jnp.floor(scaled + 0.5).astype(jnp.int32)
            out[rows, :] = whole.astype(jnp.int16)
            tail = jnp.where(row == side, power, tail)
        out[pl.ds(2 * samples, EXTRA), :] = tail.astype(jnp.int32).astype(jnp.int16)


def squeeze(keep, swapped):
    chips, half, wide = keep.shape
    small = jax.ShapeDtypeStruct((wide + EXTRA, half), jnp.int16)
    return pl.pallas_call(
        squeeze_kernel,
        in_specs=vmem(2),
        out_specs=vmem(chips),
        out_shape=[jax.ShapeDtypeStruct((wide, half), jnp.float32)] + [small] * (chips - 1),
        compiler_params=pltpu.CompilerParams(vmem_limit_bytes=24 * 2**20),
    )(keep, swapped)


def leaf_kernel(
    skel, plan, *refs
):
    here, *parts = refs[:-5]
    mine_out, coeff_out, worst_out, mine, picked = refs[-5:]
    wide, half = here.shape
    samples = wide // 2
    capacity = 2 * half
    every = LEAF_MOST * skel

    sides = [here[pl.ds(0, samples), :], here[pl.ds(samples, samples), :]]
    for part in parts:
        tail = part[pl.ds(wide, EXTRA), :].astype(jnp.int32).astype(jnp.float32)
        step = jnp.exp2(tail * (1.0 / STEPS)) * (1.0 / LEVELS)
        for side in range(2):
            value = part[pl.ds(side * samples, samples), :].astype(jnp.int32).astype(jnp.float32)
            sides[side] = sides[side] + value * step[side : side + 1]
    mine_t = jnp.concatenate(sides, axis=1)
    mine_out[...] = mine_t
    total = jnp.concatenate(sides, axis=0).T
    mine[pl.ds(0, half), :] = total
    mine[pl.ds(half, half), :] = pltpu.roll(total, samples, 1)
    mine[pl.ds(capacity, 8), :] = jnp.zeros((8, wide), jnp.float32)
    for k in range(every):
        picked[pl.ds(k, 1), :] = mine[pl.ds(plan[PICKS + k], 1), :]
    begins = [plan[b] for b in range(LEAF_MOST)]
    count = plan[LEAF_MOST]
    chosen = picked[:, :samples]

    gram = nt_dot(chosen, chosen, HIGHEST)
    proj = jnp.dot(chosen, mine_t, precision=HIGHEST, preferred_element_type=jnp.float32)

    slot = lax.broadcasted_iota(jnp.int32, (skel, capacity), 1)
    rank = jnp.zeros((skel, capacity), jnp.int32)
    for b in range(1, LEAF_MOST):
        rank += (slot >= begins[b]).astype(jnp.int32)
    hot = [rank == b for b in range(LEAF_MOST)]
    hot_rows = jnp.concatenate([h.astype(jnp.float32) for h in hot], axis=0)

    lane_leaf = lax.broadcasted_iota(jnp.int32, (skel, every), 1) // skel
    lane_row = lax.broadcasted_iota(jnp.int32, (skel, every), 1) % skel
    down = lax.broadcasted_iota(jnp.int32, (skel, every), 0)
    joined = jnp.where((down == lane_row) & (count == 0), 1.0, 0.0)
    for b in range(LEAF_MOST):
        joined += jnp.where(lane_leaf == b, gram[b * skel : (b + 1) * skel], 0.0)
    spread = jnp.concatenate([jnp.where(lane_row == i, joined, 0.0) for i in range(skel)], axis=0)
    system = jnp.dot(spread, hot_rows, precision=HIGHEST, preferred_element_type=jnp.float32)

    lines = [system[i * skel : (i + 1) * skel] for i in range(skel)]
    right = jnp.zeros((skel, capacity), jnp.float32)
    for b in range(LEAF_MOST):
        right += jnp.where(hot[b], proj[b * skel : (b + 1) * skel], 0.0)
    index = lax.broadcasted_iota(jnp.int32, (skel, capacity), 0)
    uppers = []
    pivots = []
    for j in range(skel):
        line = lines[j]
        inverse = 1.0 / line[j : j + 1]
        upper = line * inverse
        uppers.append(upper)
        pivots.append(inverse)
        for i in range(j + 1, skel):
            lines[i] = lines[i] - line[i : i + 1] * upper
        right = right - jnp.where(index > j, upper * right[j : j + 1], 0.0)
    solved = right * jnp.concatenate(pivots, axis=0)
    for j in range(skel - 2, -1, -1):
        known = jnp.where(index > j, uppers[j] * solved, 0.0)
        less = jnp.sum(known, axis=0, keepdims=True)
        solved = jnp.where(index == j, solved - less, solved)
    coeff_out[...] = solved

    weights = jnp.concatenate([jnp.where(h, solved, 0.0) for h in hot], axis=0)
    rebuilt = lax.dot_general(
        chosen,
        weights,
        (((0,), (0,)), ((), ())),
        precision=HIGHEST,
        preferred_element_type=jnp.float32,
    )
    resid = mine_t - rebuilt
    err = jnp.sum(resid * resid, axis=0, keepdims=True)
    norm = jnp.sum(mine_t * mine_t, axis=0, keepdims=True)
    worst = jnp.zeros((1, 1), jnp.float32)
    for b in range(LEAF_MOST):
        near = hot[b][:1]
        err_leaf = jnp.sum(jnp.where(near, err, 0.0), axis=1, keepdims=True)
        norm_leaf = jnp.sum(jnp.where(near, norm, 0.0), axis=1, keepdims=True)
        worst = jnp.maximum(worst, jnp.sqrt(err_leaf) / jnp.sqrt(norm_leaf + 1e-06))
    worst_out[...] = jnp.broadcast_to(worst, worst_out.shape)


def leaf_work(here, parts, plan):
    wide, half = here.shape
    samples = wide // 2
    skel = (plan.shape[0] - PICKS) // LEAF_MOST
    return pl.pallas_call(
        functools.partial(leaf_kernel, skel),
        in_specs=[smem()] + vmem(1 + len(parts)),
        out_specs=vmem(3),
        out_shape=[
            jax.ShapeDtypeStruct((samples, 2 * half), jnp.float32),
            jax.ShapeDtypeStruct((skel, 2 * half), jnp.float32),
            jax.ShapeDtypeStruct((1, LANES), jnp.float32),
        ],
        scratch_shapes=[
            pltpu.VMEM((2 * half + 8, wide), jnp.float32),
            pltpu.VMEM((LEAF_MOST * skel, wide), jnp.float32),
        ],
        compiler_params=pltpu.CompilerParams(vmem_limit_bytes=12 * 2**20),
    )(plan, here, *parts)


def exchange(value, axis, flip):
    pairs = [(k, k ^ flip) for k in range(lax.axis_size(axis))]
    return lax.ppermute(value, axis, pairs)


def largest(value, axis):
    size = lax.axis_size(axis)
    every = jnp.broadcast_to(value[None], (size, *value.shape))
    return jnp.max(lax.all_to_all(every, axis, 0, 0), axis=0)


def gather_near(own, n_row):
    depth = own.shape[1]
    near = {(k, 0): exchange(own, "row", k) for k in range(1, n_row - 1)}
    if n_row != 4:
        return near, {(n_row - 1, 0): exchange(own, "row", n_row - 1)}
    cut = depth // 2 // LANES * LANES
    left = exchange(near[2, 0][:, :cut], "row", 1)
    right = exchange(near[1, 0][:, cut:], "row", 2)
    return near, {(3, 0): left, (3, cut): right}


def local(frontal, sample_cols, leaf_first, leaf_owner, skeleton):
    n_col = lax.axis_size("col")
    n_row = lax.axis_size("row")
    own = sample_cols.T
    first, second = gather_near(own, n_row)
    held, begun, source, plan = own_product(
        frontal, own, leaf_first, leaf_owner, skeleton.T, n_row, n_col
    )
    begun = middle_product(held, begun, list(first.values()), tuple(first))
    swap, total = last_product(
        held, begun, source, list(second.values()), tuple(second), n_col
    )
    swapped = exchange(swap, "col", 1)
    here, *away = squeeze(keep_rows(total, source, n_col), swapped)
    parts = [exchange(value, "col", 2 * (k + 1)) for k, value in enumerate(away)]
    mine, coeff, worst = leaf_work(here, parts, plan)
    worst = largest(largest(worst, "col"), "row")
    return (mine, coeff, worst[0, :1])


def solution(mesh):
    return jax.shard_map(
        local,
        mesh=mesh,
        in_specs=(P("row", "col"), P(("col", "row"), None), P(), P(), P()),
        out_specs=(P("row", "col"), P("row", "col"), P()),
        check_vma=False,
    )
```

```python
import functools

import jax
import jax.numpy as jnp
from jax import lax
from jax.experimental import pallas as pl
from jax.experimental.pallas import tpu as pltpu
from jax.sharding import PartitionSpec as P

UNIT = 32
LANES = 128
LEAF_MOST = 4
PICKS = 8
LEVELS = 32760.0
EXTRA = 16
PART = 256
STEPS = 64.0
RUN_LEAVES = 4


def nt_dot(a, b):
    return lax.dot_general(a, b, (((1,), (1,)), ((), ())), preferred_element_type=jnp.float32)


def clear_runs(pick, n_row, depth, frontal, leaf_first):
    group_rows, width = frontal.shape
    per_group = leaf_first.shape[0] // n_row
    runs = per_group // RUN_LEAVES
    run_rows = group_rows // runs
    row_pos = lax.axis_index("row")
    first_col = lax.axis_index("col") * width

    def clear(at, carry):
        run = at // (run_rows // LANES)
        begin = row_pos * group_rows + run * run_rows
        begin_col = row_pos * group_rows + at * LANES
        inside = begin_col - first_col
        held = (inside >= 0) & (inside < width)
        inside = jnp.clip(inside, 0, width - LANES)

        @pl.when(held & (((inside // depth) ^ row_pos) == pick))
        def _():
            rows = pl.ds(pl.multiple_of(run * run_rows, run_rows), run_rows)
            lanes = pl.ds(pl.multiple_of(inside, LANES), LANES)
            part = frontal[rows, lanes]
            down = lax.broadcasted_iota(jnp.int32, part.shape, 0) + begin
            across = lax.broadcasted_iota(jnp.int32, part.shape, 1) + begin_col
            leaf_down = jnp.zeros(part.shape, jnp.int32)
            leaf_across = jnp.zeros(part.shape, jnp.int32)
            for k in range(1, RUN_LEAVES):
                edge = leaf_first[row_pos * per_group + run * RUN_LEAVES + k]
                leaf_down += (down >= edge).astype(jnp.int32)
                leaf_across += (across >= edge).astype(jnp.int32)
            kept = jnp.where(leaf_down == leaf_across, 0.0, part.astype(jnp.float32))
            frontal[rows, lanes] = kept.astype(jnp.bfloat16)

        return carry

    lax.fori_loop(0, group_rows // LANES, clear, 0)


def multiply(pick, frontal, slabs, begun, total):
    group_rows, width = frontal.shape
    depth = width // lax.axis_size("row")
    row_pos = lax.axis_index("row")
    part = min(group_rows, 512)

    def rows_of(at, carry):
        rows = pl.ds(pl.multiple_of(at * part, part), part)
        value = None if begun is None else begun[rows, :]
        for (k, offset), slab in zip(pick, slabs):
            begin = pl.multiple_of((row_pos ^ k) * depth + offset, LANES)
            twice = jnp.concatenate([slab[...], slab[...]], axis=0)
            add = nt_dot(frontal[rows, pl.ds(begin, slab.shape[1])], twice)
            value = add if value is None else value + add
        total[rows, :] = value
        return carry

    lax.fori_loop(0, group_rows // part, rows_of, 0)


def plan_leaves(n_row, group_rows, capacity, first, owners, skel, plan):
    leaves = first.shape[0]
    per_group = leaves // n_row
    count_skel = skel.shape[0]
    row_pos = lax.axis_index("row")
    col_pos = lax.axis_index("col")

    def clear(at, carry):
        plan[at] = capacity
        return carry

    lax.fori_loop(0, plan.shape[0], clear, 0)

    def find(at, carry):
        count, filled = carry
        leaf = row_pos * per_group + at
        begin = first[leaf]
        following = first[jnp.minimum(leaf + 1, leaves - 1)]
        end = jnp.where(at + 1 < per_group, following, (row_pos + 1) * group_rows)
        hit = (owners[leaf] == col_pos) & (count < LEAF_MOST)

        @pl.when(hit)
        def _():
            plan[count] = filled
            for k in range(count_skel):
                plan[PICKS + count * count_skel + k] = filled + skel[k, leaf] - begin

        return jnp.where(hit, count + 1, count), jnp.where(hit, filled + end - begin, filled)

    count, _ = lax.fori_loop(0, per_group, find, (jnp.int32(0), jnp.int32(0)))
    plan[LEAF_MOST] = count


def own_kernel(
    n_row,
    n_col,
    leaf_first,
    leaf_owner,
    skeleton,
    frontal,
    slab,
    held,
    total,
    target,
    plan,
    first,
    owners,
    skel,
    near,
    used,
    table_sems,
    slab_sem,
    sems,
):
    group_rows = frontal.shape[0]
    depth = slab.shape[1]
    leaves = leaf_first.shape[0]
    per_group = leaves // n_row
    per_owner = 2 * group_rows // n_col // UNIT
    units = group_rows // UNIT
    row_pos = lax.axis_index("row")
    col_pos = lax.axis_index("col")
    tables = [
        pltpu.make_async_copy(leaf_first, first, table_sems.at[0]),
        pltpu.make_async_copy(leaf_owner, owners, table_sems.at[1]),
        pltpu.make_async_copy(skeleton, skel, table_sems.at[2]),
    ]
    bring = pltpu.make_async_copy(slab, near, slab_sem)
    moves = []
    for k in range(n_row):
        lanes = pl.ds(pl.multiple_of((row_pos ^ k) * depth, LANES), depth)
        moves.append(
            pltpu.make_async_copy(frontal.at[:, lanes], held.at[:, lanes], sems.at[k])
        )
    for copy in tables + [bring] + moves:
        copy.start()

    def clear(at, carry):
        used[at] = 0
        return carry

    lax.fori_loop(0, n_col, clear, 0)
    for copy in tables:
        copy.wait()

    def place(unit, leaf):
        row = row_pos * group_rows + unit * UNIT
        later = jnp.minimum(leaf + 1, leaves - 1)
        moved = (leaf + 1 < leaves) & (first[later] <= row)
        leaf = jnp.where(moved, later, leaf)
        owner = owners[leaf]
        slot = used[owner]
        used[owner] = slot + 1
        target[unit] = (owner ^ col_pos) * per_owner + slot
        return leaf

    lax.fori_loop(0, units, place, row_pos * per_group)
    plan_leaves(n_row, group_rows, per_owner * UNIT, first, owners, skel, plan)
    bring.wait()
    moves[0].wait()
    clear_runs(0, n_row, depth, held, first)
    multiply(((0, 0),), held, (near,), None, total)
    for k in range(1, n_row):
        moves[k].wait()
        clear_runs(k, n_row, depth, held, first)


def middle_kernel(pick, frontal, begun, *refs):
    multiply(pick, frontal, refs[: len(pick)], begun, refs[len(pick)])


def last_kernel(pick, target, frontal, begun, *refs):
    slabs, (keep, swap) = refs[: len(pick)], refs[len(pick) :]
    group_rows, width = frontal.shape
    depth = width // lax.axis_size("row")
    row_pos = lax.axis_index("row")
    chips, half, wide = keep.shape
    per_half = half // UNIT
    lane = lax.broadcasted_iota(jnp.int32, (UNIT, wide), 1) // (wide // 2)
    twice = [jnp.concatenate([slab[...], slab[...]], axis=0) for slab in slabs]
    keep[...] = jnp.zeros(keep.shape, jnp.float32)
    swap[...] = jnp.zeros(swap.shape, jnp.float32)

    def rows_of(at, carry):
        rows = pl.ds(pl.multiple_of(at * PART, PART), PART)
        value = begun[rows, :]
        for (k, offset), slab in zip(pick, twice):
            begin = pl.multiple_of((row_pos ^ k) * depth + offset, LANES)
            value = value + nt_dot(frontal[rows, pl.ds(begin, slab.shape[1])], slab)
        for unit in range(PART // UNIT):
            spot = target[at * (PART // UNIT) + unit]
            turn, slot = spot // (2 * per_half), spot % (2 * per_half)
            to_rows = pl.ds(pl.multiple_of(slot % per_half * UNIT, UNIT), UNIT)
            piece = value[unit * UNIT : (unit + 1) * UNIT]
            near = lane == slot // per_half
            for other, out in ((0, keep), (1, swap)):
                mask = near & (turn % 2 == other)
                pltpu.store(out.at[turn // 2, to_rows, :], piece, mask=mask)
        return carry

    steps = group_rows // PART
    lax.fori_loop(0, steps, rows_of, 0, unroll=min(steps, 4))


def vmem(count=None):
    spec = pl.BlockSpec(memory_space=pltpu.VMEM)
    return spec if count is None else [spec] * count


def smem():
    return pl.BlockSpec(memory_space=pltpu.SMEM)


def hbm():
    return pl.BlockSpec(memory_space=pltpu.HBM)


def in_hbm(value):
    return pltpu.with_memory_space_constraint(value, pltpu.HBM)


def product_cost(frontal, slabs):
    group_rows = frontal.shape[0]
    samples = slabs[0].shape[0]
    depth = sum(slab.shape[1] for slab in slabs)
    return pl.CostEstimate(
        flops=8 * group_rows * depth * samples,
        bytes_accessed=2 * group_rows * depth,
        transcendentals=0,
    )


def own_product(frontal, slab, leaf_first, leaf_owner, skeleton, n_row, n_col):
    group_rows, width = frontal.shape
    samples, depth = slab.shape
    leaves = leaf_first.shape[0]
    return pl.pallas_call(
        functools.partial(own_kernel, n_row, n_col),
        in_specs=[hbm()] * 5,
        out_specs=[vmem(), vmem(), smem(), smem()],
        out_shape=[
            jax.ShapeDtypeStruct(frontal.shape, frontal.dtype),
            jax.ShapeDtypeStruct((group_rows, 2 * samples), jnp.float32),
            jax.ShapeDtypeStruct((group_rows // UNIT,), jnp.int32),
            jax.ShapeDtypeStruct((PICKS + LEAF_MOST * skeleton.shape[0],), jnp.int32),
        ],
        scratch_shapes=[
            pltpu.SMEM((leaves,), jnp.int32),
            pltpu.SMEM((leaves,), jnp.int32),
            pltpu.SMEM(skeleton.shape, jnp.int32),
            pltpu.VMEM((samples, depth), slab.dtype),
            pltpu.SMEM((n_col,), jnp.int32),
            pltpu.SemaphoreType.DMA((3,)),
            pltpu.SemaphoreType.DMA,
            pltpu.SemaphoreType.DMA((n_row,)),
        ],
        cost_estimate=product_cost(frontal, [slab] * n_row),
        compiler_params=pltpu.CompilerParams(vmem_limit_bytes=24 * 2**20),
    )(*(in_hbm(x) for x in (leaf_first, leaf_owner, skeleton, frontal, slab)))


def middle_product(frontal, begun, slabs, pick):
    return pl.pallas_call(
        functools.partial(middle_kernel, pick),
        in_specs=vmem(2 + len(slabs)),
        out_specs=vmem(),
        out_shape=jax.ShapeDtypeStruct(begun.shape, jnp.float32),
        cost_estimate=product_cost(frontal, slabs),
        compiler_params=pltpu.CompilerParams(vmem_limit_bytes=24 * 2**20),
    )(frontal, begun, *slabs)


def last_product(frontal, begun, target, slabs, pick, n_col):
    group_rows, wide = begun.shape
    block = jax.ShapeDtypeStruct((n_col // 2, group_rows // n_col, wide), jnp.float32)
    return pl.pallas_call(
        functools.partial(last_kernel, pick),
        in_specs=[smem()] + vmem(2 + len(slabs)),
        out_specs=vmem(2),
        out_shape=[block, block],
        cost_estimate=product_cost(frontal, slabs),
        compiler_params=pltpu.CompilerParams(vmem_limit_bytes=24 * 2**20),
    )(target, frontal, begun, *slabs)


def squeeze_kernel(keep, swapped, here, *away):
    samples = keep.shape[2] // 2
    here[...] = (keep[0] + swapped[0]).T
    row = lax.broadcasted_iota(jnp.int32, (EXTRA, keep.shape[1]), 0)
    for k, out in enumerate(away):
        block = (keep[k + 1] + swapped[k + 1]).T
        tail = jnp.zeros(row.shape, jnp.float32)
        for side in range(2):
            rows = slice(side * samples, (side + 1) * samples)
            part = block[rows]
            most = jnp.maximum(jnp.max(jnp.abs(part), axis=0, keepdims=True), 1e-30)
            power = jnp.ceil(jnp.log2(most) * STEPS)
            scaled = part * (LEVELS * jnp.exp2(power * (-1.0 / STEPS)))
            whole = jnp.floor(scaled + 0.5).astype(jnp.int32)
            out[rows, :] = whole.astype(jnp.int16)
            tail = jnp.where(row == side, power, tail)
        out[pl.ds(2 * samples, EXTRA), :] = tail.astype(jnp.int32).astype(jnp.int16)


def squeeze(keep, swapped):
    chips, half, wide = keep.shape
    small = jax.ShapeDtypeStruct((wide + EXTRA, half), jnp.int16)
    return pl.pallas_call(
        squeeze_kernel,
        in_specs=vmem(2),
        out_specs=vmem(chips),
        out_shape=[jax.ShapeDtypeStruct((wide, half), jnp.float32)] + [small] * (chips - 1),
        compiler_params=pltpu.CompilerParams(vmem_limit_bytes=24 * 2**20),
    )(keep, swapped)


def thirds(value):
    high = value.astype(jnp.bfloat16)
    rest = value - high.astype(jnp.float32)
    middle = rest.astype(jnp.bfloat16)
    low = (rest - middle.astype(jnp.float32)).astype(jnp.bfloat16)
    return high, middle, low


def beside(left, right):
    wide = left.shape[1]
    lane = lax.broadcasted_iota(jnp.int32, left.shape, 1)
    joined = jnp.where(lane < wide // 2, left.astype(jnp.float32), right.astype(jnp.float32))
    return joined.astype(jnp.bfloat16)


def left_terms(high, middle, low):
    return jnp.concatenate([high, beside(middle, high), beside(low, middle)], axis=1)


def right_terms(high, middle, low):
    return jnp.concatenate([high, middle, high, low, high, middle], axis=0)


def plain_dot(a, b):
    return jnp.dot(a, b, preferred_element_type=jnp.float32)


def leaf_kernel(skel, plan, *refs):
    here, *parts = refs[:-8]
    mine_out, coeff_out, worst_out, mine, picked, turned, coeff, sems = refs[-8:]
    wide, half = here.shape
    samples = wide // 2
    capacity = 2 * half
    every = LEAF_MOST * skel

    sides = [here[pl.ds(0, samples), :], here[pl.ds(samples, samples), :]]
    for part in parts:
        tail = part[pl.ds(wide, EXTRA), :].astype(jnp.int32).astype(jnp.float32)
        step = jnp.exp2(tail * (1.0 / STEPS)) * (1.0 / LEVELS)
        for side in range(2):
            value = part[pl.ds(side * samples, samples), :].astype(jnp.int32).astype(jnp.float32)
            sides[side] = sides[side] + value * step[side : side + 1]
    mine_t = jnp.concatenate(sides, axis=1)
    turned[...] = mine_t
    send_mine = pltpu.make_async_copy(turned, mine_out, sems.at[0])
    send_mine.start()
    total = jnp.concatenate(sides, axis=0).T
    other = pltpu.roll(total, samples, 1)
    low_half = lax.broadcasted_iota(jnp.int32, total.shape, 1) < samples
    mine[pl.ds(0, half), :] = jnp.where(low_half, total, other)
    mine[pl.ds(half, half), :] = jnp.where(low_half, other, total)
    mine[pl.ds(capacity, 8), :] = jnp.zeros((8, wide), jnp.float32)
    for k in range(every):
        picked[pl.ds(k, 1), :] = mine[pl.ds(plan[PICKS + k], 1), :]
    begins = [plan[b] for b in range(LEAF_MOST)]
    count = plan[LEAF_MOST]
    chosen = picked[...]

    high, middle, low = thirds(chosen)
    across = left_terms(high, middle, low)
    down = jnp.concatenate([beside(high, middle), beside(high, low), beside(high, middle)], axis=1)
    gram = nt_dot(across, down)
    proj = plain_dot(across, right_terms(*thirds(mine_t)))

    slot = lax.broadcasted_iota(jnp.int32, (skel, capacity), 1)
    rank = jnp.zeros((skel, capacity), jnp.int32)
    for b in range(1, LEAF_MOST):
        rank += (slot >= begins[b]).astype(jnp.int32)
    hot = [rank == b for b in range(LEAF_MOST)]
    hot_rows = jnp.concatenate([h.astype(jnp.float32) for h in hot], axis=0).astype(jnp.bfloat16)

    lane_leaf = lax.broadcasted_iota(jnp.int32, (skel, every), 1) // skel
    lane_row = lax.broadcasted_iota(jnp.int32, (skel, every), 1) % skel
    below = lax.broadcasted_iota(jnp.int32, (skel, every), 0)
    joined = jnp.where((below == lane_row) & (count == 0), 1.0, 0.0)
    for b in range(LEAF_MOST):
        joined += jnp.where(lane_leaf == b, gram[b * skel : (b + 1) * skel], 0.0)
    terms = [term.astype(jnp.float32) for term in thirds(joined)]
    terms = jnp.concatenate(terms + [jnp.zeros_like(joined)], axis=1)
    turn = lax.broadcasted_iota(jnp.int32, terms.shape, 1) % skel
    spread = jnp.concatenate([jnp.where(turn == i, terms, 0.0) for i in range(skel)], axis=0)
    system = plain_dot(spread.astype(jnp.bfloat16), jnp.concatenate([hot_rows] * 4, axis=0))

    lines = [system[i * skel : (i + 1) * skel] for i in range(skel)]
    right = jnp.zeros((skel, capacity), jnp.float32)
    for b in range(LEAF_MOST):
        right += jnp.where(hot[b], proj[b * skel : (b + 1) * skel], 0.0)
    index = lax.broadcasted_iota(jnp.int32, (skel, capacity), 0)
    uppers = []
    pivots = []
    for j in range(skel):
        line = lines[j]
        inverse = 1.0 / line[j : j + 1]
        upper = line * inverse
        uppers.append(upper)
        pivots.append(inverse)
        for i in range(j + 1, skel):
            lines[i] = lines[i] - line[i : i + 1] * upper
        right = right - jnp.where(index > j, upper * right[j : j + 1], 0.0)
    solved = right * jnp.concatenate(pivots, axis=0)
    for j in range(skel - 2, -1, -1):
        known = jnp.where(index > j, uppers[j] * solved, 0.0)
        less = jnp.sum(known, axis=0, keepdims=True)
        solved = jnp.where(index == j, solved - less, solved)
    coeff[...] = solved
    send_coeff = pltpu.make_async_copy(coeff, coeff_out, sems.at[1])
    send_coeff.start()

    weights = jnp.concatenate([jnp.where(h, solved, 0.0) for h in hot], axis=0)
    upright = chosen.T[:samples]
    upright = thirds(jnp.concatenate([upright, upright], axis=1))
    rebuilt = plain_dot(left_terms(*upright), right_terms(*thirds(weights)))
    resid = mine_t - rebuilt
    err = jnp.sum(resid * resid, axis=0, keepdims=True)
    norm = jnp.sum(mine_t * mine_t, axis=0, keepdims=True)
    worst = jnp.zeros((1, 1), jnp.float32)
    for b in range(LEAF_MOST):
        near = hot[b][:1]
        err_leaf = jnp.sum(jnp.where(near, err, 0.0), axis=1, keepdims=True)
        norm_leaf = jnp.sum(jnp.where(near, norm, 0.0), axis=1, keepdims=True)
        worst = jnp.maximum(worst, jnp.sqrt(err_leaf) / jnp.sqrt(norm_leaf + 1e-06))
    worst_out[...] = jnp.broadcast_to(worst, worst_out.shape)
    send_mine.wait()
    send_coeff.wait()


def leaf_work(here, parts, plan):
    wide, half = here.shape
    samples = wide // 2
    skel = (plan.shape[0] - PICKS) // LEAF_MOST
    return pl.pallas_call(
        functools.partial(leaf_kernel, skel),
        in_specs=[smem()] + vmem(1 + len(parts)),
        out_specs=[hbm(), hbm(), vmem()],
        out_shape=[
            jax.ShapeDtypeStruct((samples, 2 * half), jnp.float32),
            jax.ShapeDtypeStruct((skel, 2 * half), jnp.float32),
            jax.ShapeDtypeStruct((1, LANES), jnp.float32),
        ],
        scratch_shapes=[
            pltpu.VMEM((2 * half + 8, wide), jnp.float32),
            pltpu.VMEM((LEAF_MOST * skel, wide), jnp.float32),
            pltpu.VMEM((samples, 2 * half), jnp.float32),
            pltpu.VMEM((skel, 2 * half), jnp.float32),
            pltpu.SemaphoreType.DMA((2,)),
        ],
        compiler_params=pltpu.CompilerParams(vmem_limit_bytes=12 * 2**20),
    )(plan, here, *parts)


def exchange(value, axis, flip):
    pairs = [(k, k ^ flip) for k in range(lax.axis_size(axis))]
    return lax.ppermute(value, axis, pairs)


def largest(value, axis):
    size = lax.axis_size(axis)
    every = jnp.broadcast_to(value[None], (size, *value.shape))
    return jnp.max(lax.all_to_all(every, axis, 0, 0), axis=0)


def gather_near(own, n_row):
    depth = own.shape[1]
    near = {(k, 0): exchange(own, "row", k) for k in range(1, n_row - 1)}
    if n_row != 4:
        return near, {(n_row - 1, 0): exchange(own, "row", n_row - 1)}
    cut = depth // 2 // LANES * LANES
    left = exchange(near[2, 0][:, :cut], "row", 1)
    right = exchange(near[1, 0][:, cut:], "row", 2)
    return near, {(3, 0): left, (3, cut): right}


def local(frontal, sample_cols, leaf_first, leaf_owner, skeleton):
    n_col = lax.axis_size("col")
    n_row = lax.axis_size("row")
    own = sample_cols.T
    first, second = gather_near(own, n_row)
    held, begun, target, plan = own_product(
        frontal, own, leaf_first, leaf_owner, skeleton.T, n_row, n_col
    )
    begun = middle_product(held, begun, list(first.values()), tuple(first))
    keep, swap = last_product(held, begun, target, list(second.values()), tuple(second), n_col)
    swapped = exchange(swap, "col", 1)
    here, *away = squeeze(keep, swapped)
    parts = [exchange(away[k - 1], "col", 2 * k) for k in range(n_col // 2 - 1, 0, -1)]
    mine, coeff, worst = leaf_work(here, parts, plan)
    worst = largest(worst, ("row", "col"))
    return (mine, coeff, worst[0, :1])


def solution(mesh):
    return jax.shard_map(
        local,
        mesh=mesh,
        in_specs=(P("row", "col"), P(("col", "row"), None), P(), P(), P()),
        out_specs=(P("row", "col"), P("row", "col"), P()),
        check_vma=False,
    )
```

```python
import functools

import jax
import jax.numpy as jnp
from jax import lax
from jax.experimental import pallas as pl
from jax.experimental.pallas import tpu as pltpu
from jax.sharding import PartitionSpec as P

UNIT = 32
LANES = 128
LEAF_MOST = 4
PICKS = 8
LEVELS = 32760.0
EXTRA = 16
PART = 1024
STEPS = 64.0
RUN_LEAVES = 4


def nt_dot(a, b):
    return lax.dot_general(a, b, (((1,), (1,)), ((), ())), preferred_element_type=jnp.float32)


def leaf_blocks(run_rows, width, edges, act):
    group_rows = edges.shape[0] // RUN_LEAVES * run_rows
    row_pos = lax.axis_index("row")
    first_col = lax.axis_index("col") * width
    depth = width // lax.axis_size("row")

    def one(at, carry):
        run = at // (run_rows // LANES)
        begin_row = row_pos * group_rows + run * run_rows
        begin_col = row_pos * group_rows + at * LANES
        inside = begin_col - first_col

        @pl.when((inside >= 0) & (inside < width))
        def _():
            shape = (run_rows, LANES)
            down = lax.broadcasted_iota(jnp.int32, shape, 0) + begin_row
            across = lax.broadcasted_iota(jnp.int32, shape, 1) + begin_col
            leaf_down = jnp.zeros(shape, jnp.int32)
            leaf_across = jnp.zeros(shape, jnp.int32)
            for k in range(1, RUN_LEAVES):
                edge = edges[run * RUN_LEAVES + k]
                leaf_down += (down >= edge).astype(jnp.int32)
                leaf_across += (across >= edge).astype(jnp.int32)
            column = jnp.clip(inside, 0, width - LANES)
            rows = pl.ds(pl.multiple_of(run * run_rows, run_rows), run_rows)
            act((column // depth) ^ row_pos, rows, column, leaf_down == leaf_across)

        return carry

    lax.fori_loop(0, group_rows // LANES, one, 0)


def multiply(items, value, rows):
    for block, begin, slab in items:
        twice = jnp.concatenate([slab[...], slab[...]], axis=0)
        add = nt_dot(block[rows, pl.ds(begin, slab.shape[1])], twice)
        value = add if value is None else value + add
    return value


def clear_runs(run_rows, width, edges, turn, block):
    def act(here, rows, column, same):
        @pl.when(here == turn)
        def _():
            inside = lax.rem(column, block.shape[1])
            lanes = pl.ds(pl.multiple_of(inside, LANES), LANES)
            part = block[rows, lanes].astype(jnp.float32)
            block[rows, lanes] = jnp.where(same, 0.0, part).astype(jnp.bfloat16)

    leaf_blocks(run_rows, width, edges, act)


def bring_block(frontal, turn, block, sem):
    depth = block.shape[1]
    begin = pl.multiple_of((lax.axis_index("row") ^ turn) * depth, LANES)
    return pltpu.make_async_copy(frontal.at[:, pl.ds(begin, depth)], block, sem)


def parts_of(group_rows):
    part = min(group_rows, PART)
    return [pl.ds(at, part) for at in range(0, group_rows, part)]


def plan_leaves(n_row, group_rows, capacity, first, owners, skel, plan):
    leaves = first.shape[0]
    per_group = leaves // n_row
    count_skel = skel.shape[0]
    row_pos = lax.axis_index("row")
    col_pos = lax.axis_index("col")

    def clear(at, carry):
        plan[at] = capacity
        return carry

    lax.fori_loop(0, plan.shape[0], clear, 0)

    def find(at, carry):
        count, filled = carry
        leaf = row_pos * per_group + at
        begin = first[leaf]
        following = first[jnp.minimum(leaf + 1, leaves - 1)]
        end = jnp.where(at + 1 < per_group, following, (row_pos + 1) * group_rows)
        hit = (owners[leaf] == col_pos) & (count < LEAF_MOST)

        @pl.when(hit)
        def _():
            plan[count] = filled
            for k in range(count_skel):
                plan[PICKS + count * count_skel + k] = filled + skel[k, leaf] - begin

        return jnp.where(hit, count + 1, count), jnp.where(hit, filled + end - begin, filled)

    count, _ = lax.fori_loop(0, per_group, find, (jnp.int32(0), jnp.int32(0)))
    plan[LEAF_MOST] = count


def own_kernel(
    n_row,
    n_col,
    leaf_first,
    leaf_owner,
    skeleton,
    frontal,
    own,
    block_one,
    total,
    target,
    plan,
    edges,
    first,
    owners,
    skel,
    used,
    block_own,
    near,
    sems,
):
    group_rows, width = frontal.shape
    leaves = leaf_first.shape[0]
    per_group = leaves // n_row
    run_rows = group_rows // (per_group // RUN_LEAVES)
    per_owner = 2 * group_rows // n_col // UNIT
    row_pos = lax.axis_index("row")
    col_pos = lax.axis_index("col")
    copies = [
        pltpu.make_async_copy(leaf_first, first, sems.at[0]),
        pltpu.make_async_copy(leaf_owner, owners, sems.at[1]),
        pltpu.make_async_copy(skeleton, skel, sems.at[2]),
        pltpu.make_async_copy(own, near, sems.at[3]),
        bring_block(frontal, 0, block_own, sems.at[4]),
        bring_block(frontal, 1, block_one, sems.at[5]),
    ]
    for copy in copies:
        copy.start()

    def clear(at, carry):
        used[at] = 0
        return carry

    lax.fori_loop(0, n_col, clear, 0)
    for copy in copies[:3]:
        copy.wait()

    def edge(at, carry):
        edges[at] = first[row_pos * per_group + at]
        return carry

    lax.fori_loop(0, per_group, edge, 0)

    def place(unit, leaf):
        row = row_pos * group_rows + unit * UNIT
        later = jnp.minimum(leaf + 1, leaves - 1)
        moved = (leaf + 1 < leaves) & (first[later] <= row)
        leaf = jnp.where(moved, later, leaf)
        owner = owners[leaf]
        slot = used[owner]
        used[owner] = slot + 1
        target[unit] = (owner ^ col_pos) * per_owner + slot
        return leaf

    lax.fori_loop(0, group_rows // UNIT, place, row_pos * per_group)
    plan_leaves(n_row, group_rows, per_owner * UNIT, first, owners, skel, plan)
    for copy in copies[3:5]:
        copy.wait()
    clear_runs(run_rows, width, edges, 0, block_own)
    for rows in parts_of(group_rows):
        total[rows, :] = multiply([(block_own, 0, near)], None, rows)
    copies[5].wait()
    clear_runs(run_rows, width, edges, 1, block_one)


def near_kernel(edges, frontal, block_one, begun, one, two, block_two, block_last, total, sems):
    group_rows, width = frontal.shape
    run_rows = group_rows // (edges.shape[0] // RUN_LEAVES)
    copies = [
        bring_block(frontal, 2, block_two, sems.at[0]),
        bring_block(frontal, 3, block_last, sems.at[1]),
    ]
    for copy in copies:
        copy.start()
    from_one = block_one.shape[1] - one.shape[1]
    for rows in parts_of(group_rows):
        total[rows, :] = multiply([(block_one, from_one, one)], begun[rows, :], rows)
    copies[0].wait()
    clear_runs(run_rows, width, edges, 2, block_two)
    for rows in parts_of(group_rows):
        total[rows, :] = multiply([(block_two, 0, two)], total[rows, :], rows)
    copies[1].wait()
    clear_runs(run_rows, width, edges, 3, block_last)


def middle_kernel(block_one, block_two, begun, one, two, total):
    from_two = block_two.shape[1] - two.shape[1]
    items = [(block_one, 0, one), (block_two, from_two, two)]
    for rows in parts_of(begun.shape[0]):
        total[rows, :] = multiply(items, begun[rows, :], rows)


def last_kernel(target, block, begun, left, right, keep, swap):
    items = [(block, 0, left), (block, left.shape[1], right)]
    chips, half, wide = keep.shape
    per_half = half // UNIT
    lane = lax.broadcasted_iota(jnp.int32, (UNIT, wide), 1) // (wide // 2)
    keep[...] = jnp.zeros(keep.shape, jnp.float32)
    swap[...] = jnp.zeros(swap.shape, jnp.float32)
    for rows in parts_of(block.shape[0]):
        value = multiply(items, begun[rows, :], rows)
        for unit in range(rows.size // UNIT):
            spot = target[rows.start // UNIT + unit]
            step, slot = spot // (2 * per_half), spot % (2 * per_half)
            to_rows = pl.ds(pl.multiple_of(slot % per_half * UNIT, UNIT), UNIT)
            piece = value[unit * UNIT : (unit + 1) * UNIT]
            near = lane == slot // per_half
            for other, out in ((0, keep), (1, swap)):
                mask = near & (step % 2 == other)
                pltpu.store(out.at[step // 2, to_rows, :], piece, mask=mask)


def vmem(count=None):
    spec = pl.BlockSpec(memory_space=pltpu.VMEM)
    return spec if count is None else [spec] * count


def smem():
    return pl.BlockSpec(memory_space=pltpu.SMEM)


def hbm():
    return pl.BlockSpec(memory_space=pltpu.HBM)


def in_hbm(value):
    return pltpu.with_memory_space_constraint(value, pltpu.HBM)


def product_cost(frontal, samples, slabs):
    group_rows, width = frontal.shape
    flops = 8 * group_rows * width * samples * slabs // 4
    return pl.CostEstimate(flops=flops, bytes_accessed=flops // samples, transcendentals=0)


def own_product(frontal, own, leaf_first, leaf_owner, skeleton, n_row, n_col):
    group_rows, width = frontal.shape
    leaves = leaf_first.shape[0]
    samples, depth = own.shape
    return pl.pallas_call(
        functools.partial(own_kernel, n_row, n_col),
        in_specs=[hbm()] * 5,
        out_specs=vmem(2) + [smem()] * 3,
        out_shape=[
            jax.ShapeDtypeStruct((group_rows, depth), frontal.dtype),
            jax.ShapeDtypeStruct((group_rows, 2 * samples), jnp.float32),
            jax.ShapeDtypeStruct((group_rows // UNIT,), jnp.int32),
            jax.ShapeDtypeStruct((PICKS + LEAF_MOST * skeleton.shape[0],), jnp.int32),
            jax.ShapeDtypeStruct((leaves // n_row,), jnp.int32),
        ],
        scratch_shapes=[
            pltpu.SMEM((leaves,), jnp.int32),
            pltpu.SMEM((leaves,), jnp.int32),
            pltpu.SMEM(skeleton.shape, jnp.int32),
            pltpu.SMEM((n_col,), jnp.int32),
            pltpu.VMEM((group_rows, depth), frontal.dtype),
            pltpu.VMEM(own.shape, own.dtype),
            pltpu.SemaphoreType.DMA((6,)),
        ],
        cost_estimate=product_cost(frontal, samples, 2),
        compiler_params=pltpu.CompilerParams(vmem_limit_bytes=24 * 2**20),
    )(*(in_hbm(x) for x in (leaf_first, leaf_owner, skeleton, frontal, own)))


def near_product(frontal, block_one, begun, edges, one, two):
    group_rows, width = frontal.shape
    block = jax.ShapeDtypeStruct(block_one.shape, frontal.dtype)
    return pl.pallas_call(
        near_kernel,
        in_specs=[smem(), hbm()] + vmem(4),
        out_specs=vmem(3),
        out_shape=[block, block, jax.ShapeDtypeStruct(begun.shape, jnp.float32)],
        scratch_shapes=[pltpu.SemaphoreType.DMA((2,))],
        cost_estimate=product_cost(frontal, one.shape[0], 2),
        compiler_params=pltpu.CompilerParams(vmem_limit_bytes=24 * 2**20),
    )(edges, in_hbm(frontal), block_one, begun, one, two)


def middle_product(block_one, block_two, begun, one, two):
    return pl.pallas_call(
        middle_kernel,
        in_specs=vmem(5),
        out_specs=vmem(),
        out_shape=jax.ShapeDtypeStruct(begun.shape, jnp.float32),
        cost_estimate=product_cost(block_one, one.shape[0], 4),
        compiler_params=pltpu.CompilerParams(vmem_limit_bytes=24 * 2**20),
    )(block_one, block_two, begun, one, two)


def last_product(frontal, begun, target, slab, n_col):
    group_rows, wide = begun.shape
    block = jax.ShapeDtypeStruct((n_col // 2, group_rows // n_col, wide), jnp.float32)
    return pl.pallas_call(
        last_kernel,
        in_specs=[smem()] + vmem(2 + len(slab)),
        out_specs=vmem(2),
        out_shape=[block, block],
        cost_estimate=product_cost(frontal, wide // 2, 4),
        compiler_params=pltpu.CompilerParams(vmem_limit_bytes=24 * 2**20),
    )(target, frontal, begun, *slab)


def squeeze_kernel(keep, swapped, here, *away):
    samples = keep.shape[2] // 2
    here[...] = (keep[0] + swapped[0]).T
    row = lax.broadcasted_iota(jnp.int32, (EXTRA, keep.shape[1]), 0)
    for k, out in enumerate(away):
        block = (keep[k + 1] + swapped[k + 1]).T
        tail = jnp.zeros(row.shape, jnp.float32)
        for side in range(2):
            rows = slice(side * samples, (side + 1) * samples)
            part = block[rows]
            most = jnp.maximum(jnp.max(jnp.abs(part), axis=0, keepdims=True), 1e-30)
            power = jnp.ceil(jnp.log2(most) * STEPS)
            scaled = part * (LEVELS * jnp.exp2(power * (-1.0 / STEPS)))
            whole = jnp.floor(scaled + 0.5).astype(jnp.int32)
            out[rows, :] = whole.astype(jnp.int16)
            tail = jnp.where(row == side, power, tail)
        out[pl.ds(2 * samples, EXTRA), :] = tail.astype(jnp.int32).astype(jnp.int16)


def squeeze(keep, swapped):
    chips, half, wide = keep.shape
    small = jax.ShapeDtypeStruct((wide + EXTRA, half), jnp.int16)
    return pl.pallas_call(
        squeeze_kernel,
        in_specs=vmem(2),
        out_specs=vmem(chips),
        out_shape=[jax.ShapeDtypeStruct((wide, half), jnp.float32)] + [small] * (chips - 1),
        compiler_params=pltpu.CompilerParams(vmem_limit_bytes=24 * 2**20),
    )(keep, swapped)


def thirds(value):
    high = value.astype(jnp.bfloat16)
    rest = value - high.astype(jnp.float32)
    middle = rest.astype(jnp.bfloat16)
    low = (rest - middle.astype(jnp.float32)).astype(jnp.bfloat16)
    return high, middle, low


def beside(left, right):
    wide = left.shape[1]
    lane = lax.broadcasted_iota(jnp.int32, left.shape, 1)
    joined = jnp.where(lane < wide // 2, left.astype(jnp.float32), right.astype(jnp.float32))
    return joined.astype(jnp.bfloat16)


def left_terms(high, middle, low):
    return jnp.concatenate([high, beside(middle, high), beside(low, middle)], axis=1)


def right_terms(high, middle, low):
    return jnp.concatenate([high, middle, high, low, high, middle], axis=0)


def plain_dot(a, b):
    return jnp.dot(a, b, preferred_element_type=jnp.float32)


def leaf_kernel(skel, plan, *refs):
    here, *parts = refs[:-8]
    mine_out, coeff_out, worst_out, mine, picked, turned, coeff, sems = refs[-8:]
    wide, half = here.shape
    samples = wide // 2
    capacity = 2 * half
    every = LEAF_MOST * skel

    sides = [here[pl.ds(0, samples), :], here[pl.ds(samples, samples), :]]
    for part in parts:
        tail = part[pl.ds(wide, EXTRA), :].astype(jnp.int32).astype(jnp.float32)
        step = jnp.exp2(tail * (1.0 / STEPS)) * (1.0 / LEVELS)
        for side in range(2):
            value = part[pl.ds(side * samples, samples), :].astype(jnp.int32).astype(jnp.float32)
            sides[side] = sides[side] + value * step[side : side + 1]
    mine_t = jnp.concatenate(sides, axis=1)
    turned[...] = mine_t
    send_mine = pltpu.make_async_copy(turned, mine_out, sems.at[0])
    send_mine.start()
    total = jnp.concatenate(sides, axis=0).T
    other = pltpu.roll(total, samples, 1)
    low_half = lax.broadcasted_iota(jnp.int32, total.shape, 1) < samples
    mine[pl.ds(0, half), :] = jnp.where(low_half, total, other)
    mine[pl.ds(half, half), :] = jnp.where(low_half, other, total)
    mine[pl.ds(capacity, 8), :] = jnp.zeros((8, wide), jnp.float32)
    for k in range(every):
        picked[pl.ds(k, 1), :] = mine[pl.ds(plan[PICKS + k], 1), :]
    begins = [plan[b] for b in range(LEAF_MOST)]
    count = plan[LEAF_MOST]
    chosen = picked[...]

    high, middle, low = thirds(chosen)
    across = left_terms(high, middle, low)
    down = jnp.concatenate([beside(high, middle), beside(high, low), beside(high, middle)], axis=1)
    gram = nt_dot(across, down)
    proj = plain_dot(across, right_terms(*thirds(mine_t)))

    slot = lax.broadcasted_iota(jnp.int32, (skel, capacity), 1)
    rank = jnp.zeros((skel, capacity), jnp.int32)
    for b in range(1, LEAF_MOST):
        rank += (slot >= begins[b]).astype(jnp.int32)
    hot = [rank == b for b in range(LEAF_MOST)]
    hot_rows = jnp.concatenate([h.astype(jnp.float32) for h in hot], axis=0).astype(jnp.bfloat16)

    lane_leaf = lax.broadcasted_iota(jnp.int32, (skel, every), 1) // skel
    lane_row = lax.broadcasted_iota(jnp.int32, (skel, every), 1) % skel
    below = lax.broadcasted_iota(jnp.int32, (skel, every), 0)
    joined = jnp.where((below == lane_row) & (count == 0), 1.0, 0.0)
    for b in range(LEAF_MOST):
        joined += jnp.where(lane_leaf == b, gram[b * skel : (b + 1) * skel], 0.0)
    terms = [term.astype(jnp.float32) for term in thirds(joined)]
    terms = jnp.concatenate(terms + [jnp.zeros_like(joined)], axis=1)
    turn = lax.broadcasted_iota(jnp.int32, terms.shape, 1) % skel
    spread = jnp.concatenate([jnp.where(turn == i, terms, 0.0) for i in range(skel)], axis=0)
    system = plain_dot(spread.astype(jnp.bfloat16), jnp.concatenate([hot_rows] * 4, axis=0))

    lines = [system[i * skel : (i + 1) * skel] for i in range(skel)]
    right = jnp.zeros((skel, capacity), jnp.float32)
    for b in range(LEAF_MOST):
        right += jnp.where(hot[b], proj[b * skel : (b + 1) * skel], 0.0)
    index = lax.broadcasted_iota(jnp.int32, (skel, capacity), 0)
    uppers = []
    pivots = []
    for j in range(skel):
        line = lines[j]
        inverse = 1.0 / line[j : j + 1]
        upper = line * inverse
        uppers.append(upper)
        pivots.append(inverse)
        for i in range(j + 1, skel):
            lines[i] = lines[i] - line[i : i + 1] * upper
        right = right - jnp.where(index > j, upper * right[j : j + 1], 0.0)
    solved = right * jnp.concatenate(pivots, axis=0)
    for j in range(skel - 2, -1, -1):
        known = jnp.where(index > j, uppers[j] * solved, 0.0)
        less = jnp.sum(known, axis=0, keepdims=True)
        solved = jnp.where(index == j, solved - less, solved)
    coeff[...] = solved
    send_coeff = pltpu.make_async_copy(coeff, coeff_out, sems.at[1])
    send_coeff.start()

    weights = jnp.concatenate([jnp.where(h, solved, 0.0) for h in hot], axis=0)
    upright = chosen.T[:samples]
    upright = thirds(jnp.concatenate([upright, upright], axis=1))
    rebuilt = plain_dot(left_terms(*upright), right_terms(*thirds(weights)))
    resid = mine_t - rebuilt
    err = jnp.sum(resid * resid, axis=0, keepdims=True)
    norm = jnp.sum(mine_t * mine_t, axis=0, keepdims=True)
    worst = jnp.zeros((1, 1), jnp.float32)
    for b in range(LEAF_MOST):
        near = hot[b][:1]
        err_leaf = jnp.sum(jnp.where(near, err, 0.0), axis=1, keepdims=True)
        norm_leaf = jnp.sum(jnp.where(near, norm, 0.0), axis=1, keepdims=True)
        worst = jnp.maximum(worst, jnp.sqrt(err_leaf) / jnp.sqrt(norm_leaf + 1e-06))
    worst_out[...] = jnp.broadcast_to(worst, worst_out.shape)
    send_mine.wait()
    send_coeff.wait()


def leaf_work(here, parts, plan):
    wide, half = here.shape
    samples = wide // 2
    skel = (plan.shape[0] - PICKS) // LEAF_MOST
    return pl.pallas_call(
        functools.partial(leaf_kernel, skel),
        in_specs=[smem()] + vmem(1 + len(parts)),
        out_specs=[hbm(), hbm(), vmem()],
        out_shape=[
            jax.ShapeDtypeStruct((samples, 2 * half), jnp.float32),
            jax.ShapeDtypeStruct((skel, 2 * half), jnp.float32),
            jax.ShapeDtypeStruct((1, LANES), jnp.float32),
        ],
        scratch_shapes=[
            pltpu.VMEM((2 * half + 8, wide), jnp.float32),
            pltpu.VMEM((LEAF_MOST * skel, wide), jnp.float32),
            pltpu.VMEM((samples, 2 * half), jnp.float32),
            pltpu.VMEM((skel, 2 * half), jnp.float32),
            pltpu.SemaphoreType.DMA((2,)),
        ],
        compiler_params=pltpu.CompilerParams(vmem_limit_bytes=12 * 2**20),
    )(plan, here, *parts)


def exchange(value, axis, flip):
    pairs = [(k, k ^ flip) for k in range(lax.axis_size(axis))]
    return lax.ppermute(value, axis, pairs)


def largest(value, axis):
    size = lax.axis_size(axis)
    every = jnp.broadcast_to(value[None], (size, *value.shape))
    return jnp.max(lax.all_to_all(every, axis, 0, 0), axis=0)


def local(frontal, sample_cols, leaf_first, leaf_owner, skeleton):
    n_col = lax.axis_size("col")
    n_row = lax.axis_size("row")
    own = sample_cols.T
    cut = own.shape[1] // 2 // LANES * LANES
    left, right = own[:, :cut], own[:, cut:]
    one_right = exchange(right, "row", 1)
    two_left = exchange(left, "row", 2)
    block_one, begun, target, plan, edges = own_product(
        frontal, own, leaf_first, leaf_owner, skeleton.T, n_row, n_col
    )
    left, right, one_right, two_left, edges = lax.optimization_barrier(
        (left, right, one_right, two_left, edges)
    )
    one_left = exchange(left, "row", 1)
    two_right = exchange(right, "row", 2)
    last = [exchange(two_left, "row", 1), exchange(one_right, "row", 2)]
    block_two, block_last, begun = near_product(
        frontal, block_one, begun, edges, one_right, two_left
    )
    begun = middle_product(block_one, block_two, begun, one_left, two_right)
    keep, swap = last_product(block_last, begun, target, last, n_col)
    swapped = exchange(swap, "col", 1)
    here, *away = squeeze(keep, swapped)
    parts = [exchange(away[k - 1], "col", 2 * k) for k in range(n_col // 2 - 1, 0, -1)]
    mine, coeff, worst = leaf_work(here, parts, plan)
    worst = largest(worst, ("row", "col"))
    return (mine, coeff, worst[0, :1])


def solution(mesh):
    return jax.shard_map(
        local,
        mesh=mesh,
        in_specs=(P("row", "col"), P(("col", "row"), None), P(), P(), P()),
        out_specs=(P("row", "col"), P("row", "col"), P()),
        check_vma=False,
    )
```

```python
import functools

import jax
import jax.numpy as jnp
from jax import lax
from jax.experimental import pallas as pl
from jax.experimental.pallas import tpu as pltpu
from jax.sharding import PartitionSpec as P

UNIT = 32
LANES = 128
LEAF_MOST = 4
PICKS = 8
LEVELS = 32760.0
EXTRA = 16
PART = 1024
STEPS = 64.0
RUN_LEAVES = 4


def nt_dot(a, b):
    return lax.dot_general(a, b, (((1,), (1,)), ((), ())), preferred_element_type=jnp.float32)


def leaf_blocks(run_rows, width, edges, act):
    group_rows = edges.shape[0] // RUN_LEAVES * run_rows
    row_pos = lax.axis_index("row")
    first_col = lax.axis_index("col") * width
    depth = width // lax.axis_size("row")

    def one(at, carry):
        run = at // (run_rows // LANES)
        begin_row = row_pos * group_rows + run * run_rows
        begin_col = row_pos * group_rows + at * LANES
        inside = begin_col - first_col

        @pl.when((inside >= 0) & (inside < width))
        def _():
            shape = (run_rows, LANES)
            down = lax.broadcasted_iota(jnp.int32, shape, 0) + begin_row
            across = lax.broadcasted_iota(jnp.int32, shape, 1) + begin_col
            leaf_down = jnp.zeros(shape, jnp.int32)
            leaf_across = jnp.zeros(shape, jnp.int32)
            for k in range(1, RUN_LEAVES):
                edge = edges[run * RUN_LEAVES + k]
                leaf_down += (down >= edge).astype(jnp.int32)
                leaf_across += (across >= edge).astype(jnp.int32)
            column = jnp.clip(inside, 0, width - LANES)
            rows = pl.ds(pl.multiple_of(run * run_rows, run_rows), run_rows)
            act((column // depth) ^ row_pos, rows, column, leaf_down == leaf_across)

        return carry

    lax.fori_loop(0, group_rows // LANES, one, 0)


def multiply(items, value, rows):
    for block, begin, slab in items:
        twice = jnp.concatenate([slab[...], slab[...]], axis=0)
        add = nt_dot(block[rows, pl.ds(begin, slab.shape[1])], twice)
        value = add if value is None else value + add
    return value


def clear_runs(run_rows, width, edges, turns, blocks):
    def act(here, rows, column, same):
        for turn, block in zip(turns, blocks):

            @pl.when(here == turn)
            def _():
                inside = lax.rem(column, block.shape[1])
                lanes = pl.ds(pl.multiple_of(inside, LANES), LANES)
                part = block[rows, lanes].astype(jnp.float32)
                block[rows, lanes] = jnp.where(same, 0.0, part).astype(jnp.bfloat16)

    leaf_blocks(run_rows, width, edges, act)


def bring_block(frontal, turn, block, sem):
    depth = block.shape[1]
    begin = pl.multiple_of((lax.axis_index("row") ^ turn) * depth, LANES)
    return pltpu.make_async_copy(frontal.at[:, pl.ds(begin, depth)], block, sem)


def parts_of(group_rows):
    part = min(group_rows, PART)
    return [pl.ds(at, part) for at in range(0, group_rows, part)]


def plan_leaves(n_row, group_rows, capacity, first, owners, skel, plan):
    leaves = first.shape[0]
    per_group = leaves // n_row
    count_skel = skel.shape[0]
    row_pos = lax.axis_index("row")
    col_pos = lax.axis_index("col")

    def clear(at, carry):
        plan[at] = capacity
        return carry

    lax.fori_loop(0, plan.shape[0], clear, 0)

    def find(at, carry):
        count, filled = carry
        leaf = row_pos * per_group + at
        begin = first[leaf]
        following = first[jnp.minimum(leaf + 1, leaves - 1)]
        end = jnp.where(at + 1 < per_group, following, (row_pos + 1) * group_rows)
        hit = (owners[leaf] == col_pos) & (count < LEAF_MOST)

        @pl.when(hit)
        def _():
            plan[count] = filled
            for k in range(count_skel):
                plan[PICKS + count * count_skel + k] = filled + skel[k, leaf] - begin

        return jnp.where(hit, count + 1, count), jnp.where(hit, filled + end - begin, filled)

    count, _ = lax.fori_loop(0, per_group, find, (jnp.int32(0), jnp.int32(0)))
    plan[LEAF_MOST] = count


def bring_kernel(n_row, n_col, leaf_first, leaf_owner, frontal, *refs):
    *blocks, place_row, place_kind, edges, first, owners, used, sems = refs
    group_rows, width = frontal.shape
    leaves = leaf_first.shape[0]
    per_group = leaves // n_row
    run_rows = group_rows // (per_group // RUN_LEAVES)
    half = group_rows // n_col
    per_half = half // UNIT
    row_pos = lax.axis_index("row")
    col_pos = lax.axis_index("col")
    copies = [
        pltpu.make_async_copy(leaf_first, first, sems.at[0]),
        pltpu.make_async_copy(leaf_owner, owners, sems.at[1]),
    ]
    for turn, block in enumerate(blocks):
        copies.append(bring_block(frontal, turn, block, sems.at[2 + turn]))
    for copy in copies:
        copy.start()

    def clear(at, carry):
        used[at] = 0
        return carry

    lax.fori_loop(0, n_col, clear, 0)
    for copy in copies[:2]:
        copy.wait()

    def edge(at, carry):
        edges[at] = first[row_pos * per_group + at]
        return carry

    lax.fori_loop(0, per_group, edge, 0)

    def place(unit, leaf):
        row = row_pos * group_rows + unit * UNIT
        later = jnp.minimum(leaf + 1, leaves - 1)
        moved = (leaf + 1 < leaves) & (first[later] <= row)
        leaf = jnp.where(moved, later, leaf)
        owner = owners[leaf]
        slot = used[owner]
        used[owner] = slot + 1
        step = owner ^ col_pos
        place_row[unit] = step // 2 * half + slot % per_half * UNIT
        place_kind[unit] = step % 2 * 2 + slot // per_half
        return leaf

    lax.fori_loop(0, group_rows // UNIT, place, row_pos * per_group)
    for copy in copies[2:]:
        copy.wait()
    clear_runs(run_rows, width, edges, range(len(blocks)), blocks)


def near_kernel(edges, frontal, own, *refs):
    *blocks, one, two, block_last, total, near, sems = refs
    group_rows, width = frontal.shape
    run_rows = group_rows // (edges.shape[0] // RUN_LEAVES)
    copies = [
        pltpu.make_async_copy(own, near, sems.at[0]),
        bring_block(frontal, len(blocks), block_last, sems.at[1]),
    ]
    for copy in copies:
        copy.start()
    for rows in parts_of(group_rows):
        total[rows, :] = multiply([(blocks[1], 0, one), (blocks[2], 0, two)], None, rows)
    copies[0].wait()
    for rows in parts_of(group_rows):
        total[rows, :] = multiply([(blocks[0], 0, near)], total[rows, :], rows)
    copies[1].wait()
    clear_runs(run_rows, width, edges, [len(blocks)], [block_last])


def last_kernel(place_row, place_kind, block, begun, left, right, keep, swap):
    items = [(block, 0, left), (block, left.shape[1], right)]
    wide = keep.shape[1]
    lane = lax.broadcasted_iota(jnp.int32, (UNIT, wide), 1) // (wide // 2)
    keep[...] = jnp.zeros(keep.shape, jnp.float32)
    swap[...] = jnp.zeros(swap.shape, jnp.float32)
    for rows in parts_of(block.shape[0]):
        value = multiply(items, begun[rows, :], rows)
        for at in range(rows.size // UNIT):
            unit = rows.start // UNIT + at
            to_rows = pl.ds(pl.multiple_of(place_row[unit], UNIT), UNIT)
            piece = value[at * UNIT : (at + 1) * UNIT]
            kind = place_kind[unit]
            pltpu.store(keep.at[to_rows, :], piece, mask=lane == kind)
            pltpu.store(swap.at[to_rows, :], piece, mask=lane + 2 == kind)


def plan_kernel(n_row, group_rows, capacity, first, owners, skel, plan):
    plan_leaves(n_row, group_rows, capacity, first, owners, skel, plan)


def vmem(count=None):
    spec = pl.BlockSpec(memory_space=pltpu.VMEM)
    return spec if count is None else [spec] * count


def smem():
    return pl.BlockSpec(memory_space=pltpu.SMEM)


def hbm():
    return pl.BlockSpec(memory_space=pltpu.HBM)


def in_hbm(value):
    return pltpu.with_memory_space_constraint(value, pltpu.HBM)


def product_cost(frontal, samples, slabs):
    group_rows, width = frontal.shape
    flops = 8 * group_rows * width * samples * slabs // 4
    return pl.CostEstimate(flops=flops, bytes_accessed=flops // samples, transcendentals=0)


def bring(frontal, leaf_first, leaf_owner, depth, n_row, n_col):
    group_rows, width = frontal.shape
    leaves = leaf_first.shape[0]
    units = jax.ShapeDtypeStruct((group_rows // UNIT,), jnp.int32)
    block = jax.ShapeDtypeStruct((group_rows, depth), frontal.dtype)
    return pl.pallas_call(
        functools.partial(bring_kernel, n_row, n_col),
        in_specs=[hbm()] * 3,
        out_specs=vmem(n_row - 1) + [smem()] * 3,
        out_shape=[block] * (n_row - 1)
        + [units, units, jax.ShapeDtypeStruct((leaves // n_row,), jnp.int32)],
        scratch_shapes=[
            pltpu.SMEM((leaves,), jnp.int32),
            pltpu.SMEM((leaves,), jnp.int32),
            pltpu.SMEM((n_col,), jnp.int32),
            pltpu.SemaphoreType.DMA((1 + n_row,)),
        ],
        cost_estimate=product_cost(frontal, 64, 4),
        compiler_params=pltpu.CompilerParams(vmem_limit_bytes=24 * 2**20),
    )(*(in_hbm(x) for x in (leaf_first, leaf_owner, frontal)))


def near_product(frontal, own, edges, blocks, one, two):
    group_rows, width = frontal.shape
    samples = own.shape[0]
    return pl.pallas_call(
        near_kernel,
        in_specs=[smem(), hbm(), hbm()] + vmem(len(blocks) + 2),
        out_specs=vmem(2),
        out_shape=[
            jax.ShapeDtypeStruct(blocks[0].shape, frontal.dtype),
            jax.ShapeDtypeStruct((group_rows, 2 * samples), jnp.float32),
        ],
        scratch_shapes=[pltpu.VMEM(own.shape, own.dtype), pltpu.SemaphoreType.DMA((2,))],
        cost_estimate=product_cost(frontal, samples, 4),
        compiler_params=pltpu.CompilerParams(vmem_limit_bytes=24 * 2**20),
    )(edges, in_hbm(frontal), in_hbm(own), *blocks, one, two)


def plan_of(leaf_first, leaf_owner, skeleton, group_rows, n_row, n_col):
    size = PICKS + LEAF_MOST * skeleton.shape[0]
    return pl.pallas_call(
        functools.partial(plan_kernel, n_row, group_rows, 2 * group_rows // n_col),
        in_specs=[smem()] * 3,
        out_specs=smem(),
        out_shape=jax.ShapeDtypeStruct((size,), jnp.int32),
        cost_estimate=pl.CostEstimate(flops=10**6, bytes_accessed=2**20, transcendentals=0),
    )(leaf_first, leaf_owner, skeleton)


def last_product(block, begun, places, last, n_col):
    group_rows, wide = begun.shape
    laid = jax.ShapeDtypeStruct((group_rows // 2, wide), jnp.float32)
    return pl.pallas_call(
        last_kernel,
        in_specs=[smem()] * 2 + vmem(4),
        out_specs=vmem(2),
        out_shape=[laid, laid],
        cost_estimate=product_cost(block, wide // 2, 4),
        compiler_params=pltpu.CompilerParams(vmem_limit_bytes=24 * 2**20),
    )(*places, block, begun, *last)


def squeeze_kernel(keep, swapped, here, *away):
    wide, half = here.shape
    samples = wide // 2
    here[...] = (keep[:half] + swapped[:half]).T
    row = lax.broadcasted_iota(jnp.int32, (EXTRA, half), 0)
    for k, out in enumerate(away):
        at = pl.ds((k + 1) * half, half)
        block = (keep[at, :] + swapped[at, :]).T
        tail = jnp.zeros(row.shape, jnp.float32)
        for side in range(2):
            rows = slice(side * samples, (side + 1) * samples)
            part = block[rows]
            most = jnp.maximum(jnp.max(jnp.abs(part), axis=0, keepdims=True), 1e-30)
            power = jnp.ceil(jnp.log2(most) * STEPS)
            scaled = part * (LEVELS * jnp.exp2(power * (-1.0 / STEPS)))
            whole = jnp.floor(scaled + 0.5).astype(jnp.int32)
            out[rows, :] = whole.astype(jnp.int16)
            tail = jnp.where(row == side, power, tail)
        out[pl.ds(2 * samples, EXTRA), :] = tail.astype(jnp.int32).astype(jnp.int16)


def squeeze(keep, swapped, chips):
    rows, wide = keep.shape
    half = rows // chips
    small = jax.ShapeDtypeStruct((wide + EXTRA, half), jnp.int16)
    return pl.pallas_call(
        squeeze_kernel,
        in_specs=vmem(2),
        out_specs=vmem(chips),
        out_shape=[jax.ShapeDtypeStruct((wide, half), jnp.float32)] + [small] * (chips - 1),
        compiler_params=pltpu.CompilerParams(vmem_limit_bytes=24 * 2**20),
    )(keep, swapped)


def thirds(value):
    high = value.astype(jnp.bfloat16)
    rest = value - high.astype(jnp.float32)
    middle = rest.astype(jnp.bfloat16)
    low = (rest - middle.astype(jnp.float32)).astype(jnp.bfloat16)
    return high, middle, low


def beside(left, right):
    wide = left.shape[1]
    lane = lax.broadcasted_iota(jnp.int32, left.shape, 1)
    joined = jnp.where(lane < wide // 2, left.astype(jnp.float32), right.astype(jnp.float32))
    return joined.astype(jnp.bfloat16)


def left_terms(high, middle, low):
    return jnp.concatenate([high, beside(middle, high), beside(low, middle)], axis=1)


def right_terms(high, middle, low):
    return jnp.concatenate([high, middle, high, low, high, middle], axis=0)


def plain_dot(a, b):
    return jnp.dot(a, b, preferred_element_type=jnp.float32)


def leaf_kernel(skel, plan, *refs):
    here, *parts = refs[:-8]
    mine_out, coeff_out, worst_out, mine, picked, turned, coeff, sems = refs[-8:]
    wide, half = here.shape
    samples = wide // 2
    capacity = 2 * half
    every = LEAF_MOST * skel

    sides = [here[pl.ds(0, samples), :], here[pl.ds(samples, samples), :]]
    for part in parts:
        tail = part[pl.ds(wide, EXTRA), :].astype(jnp.int32).astype(jnp.float32)
        step = jnp.exp2(tail * (1.0 / STEPS)) * (1.0 / LEVELS)
        for side in range(2):
            value = part[pl.ds(side * samples, samples), :].astype(jnp.int32).astype(jnp.float32)
            sides[side] = sides[side] + value * step[side : side + 1]
    mine_t = jnp.concatenate(sides, axis=1)
    turned[...] = mine_t
    send_mine = pltpu.make_async_copy(turned, mine_out, sems.at[0])
    send_mine.start()
    total = jnp.concatenate(sides, axis=0).T
    other = pltpu.roll(total, samples, 1)
    low_half = lax.broadcasted_iota(jnp.int32, total.shape, 1) < samples
    mine[pl.ds(0, half), :] = jnp.where(low_half, total, other)
    mine[pl.ds(half, half), :] = jnp.where(low_half, other, total)
    mine[pl.ds(capacity, 8), :] = jnp.zeros((8, wide), jnp.float32)
    for k in range(every):
        picked[pl.ds(k, 1), :] = mine[pl.ds(plan[PICKS + k], 1), :]
    begins = [plan[b] for b in range(LEAF_MOST)]
    count = plan[LEAF_MOST]
    chosen = picked[...]

    high, middle, low = thirds(chosen)
    across = left_terms(high, middle, low)
    down = jnp.concatenate([beside(high, middle), beside(high, low), beside(high, middle)], axis=1)
    gram = nt_dot(across, down)
    proj = plain_dot(across, right_terms(*thirds(mine_t)))

    slot = lax.broadcasted_iota(jnp.int32, (skel, capacity), 1)
    rank = jnp.zeros((skel, capacity), jnp.int32)
    for b in range(1, LEAF_MOST):
        rank += (slot >= begins[b]).astype(jnp.int32)
    hot = [rank == b for b in range(LEAF_MOST)]
    hot_rows = jnp.concatenate([h.astype(jnp.float32) for h in hot], axis=0).astype(jnp.bfloat16)

    lane_leaf = lax.broadcasted_iota(jnp.int32, (skel, every), 1) // skel
    lane_row = lax.broadcasted_iota(jnp.int32, (skel, every), 1) % skel
    below = lax.broadcasted_iota(jnp.int32, (skel, every), 0)
    joined = jnp.where((below == lane_row) & (count == 0), 1.0, 0.0)
    for b in range(LEAF_MOST):
        joined += jnp.where(lane_leaf == b, gram[b * skel : (b + 1) * skel], 0.0)
    terms = [term.astype(jnp.float32) for term in thirds(joined)]
    terms = jnp.concatenate(terms + [jnp.zeros_like(joined)], axis=1)
    turn = lax.broadcasted_iota(jnp.int32, terms.shape, 1) % skel
    spread = jnp.concatenate([jnp.where(turn == i, terms, 0.0) for i in range(skel)], axis=0)
    system = plain_dot(spread.astype(jnp.bfloat16), jnp.concatenate([hot_rows] * 4, axis=0))

    lines = [system[i * skel : (i + 1) * skel] for i in range(skel)]
    right = jnp.zeros((skel, capacity), jnp.float32)
    for b in range(LEAF_MOST):
        right += jnp.where(hot[b], proj[b * skel : (b + 1) * skel], 0.0)
    index = lax.broadcasted_iota(jnp.int32, (skel, capacity), 0)
    uppers = []
    pivots = []
    for j in range(skel):
        line = lines[j]
        inverse = 1.0 / line[j : j + 1]
        upper = line * inverse
        uppers.append(upper)
        pivots.append(inverse)
        for i in range(j + 1, skel):
            lines[i] = lines[i] - line[i : i + 1] * upper
        right = right - jnp.where(index > j, upper * right[j : j + 1], 0.0)
    solved = right * jnp.concatenate(pivots, axis=0)
    for j in range(skel - 2, -1, -1):
        known = jnp.where(index > j, uppers[j] * solved, 0.0)
        less = jnp.sum(known, axis=0, keepdims=True)
        solved = jnp.where(index == j, solved - less, solved)
    coeff[...] = solved
    send_coeff = pltpu.make_async_copy(coeff, coeff_out, sems.at[1])
    send_coeff.start()

    weights = jnp.concatenate([jnp.where(h, solved, 0.0) for h in hot], axis=0)
    upright = chosen.T[:samples]
    upright = thirds(jnp.concatenate([upright, upright], axis=1))
    rebuilt = plain_dot(left_terms(*upright), right_terms(*thirds(weights)))
    resid = mine_t - rebuilt
    err = jnp.sum(resid * resid, axis=0, keepdims=True)
    norm = jnp.sum(mine_t * mine_t, axis=0, keepdims=True)
    worst = jnp.zeros((1, 1), jnp.float32)
    for b in range(LEAF_MOST):
        near = hot[b][:1]
        err_leaf = jnp.sum(jnp.where(near, err, 0.0), axis=1, keepdims=True)
        norm_leaf = jnp.sum(jnp.where(near, norm, 0.0), axis=1, keepdims=True)
        worst = jnp.maximum(worst, jnp.sqrt(err_leaf) / jnp.sqrt(norm_leaf + 1e-06))
    worst_out[...] = jnp.broadcast_to(worst, worst_out.shape)
    send_mine.wait()
    send_coeff.wait()


def leaf_work(here, parts, plan):
    wide, half = here.shape
    samples = wide // 2
    skel = (plan.shape[0] - PICKS) // LEAF_MOST
    return pl.pallas_call(
        functools.partial(leaf_kernel, skel),
        in_specs=[smem()] + vmem(1 + len(parts)),
        out_specs=[hbm(), hbm(), vmem()],
        out_shape=[
            jax.ShapeDtypeStruct((samples, 2 * half), jnp.float32),
            jax.ShapeDtypeStruct((skel, 2 * half), jnp.float32),
            jax.ShapeDtypeStruct((1, LANES), jnp.float32),
        ],
        scratch_shapes=[
            pltpu.VMEM((2 * half + 8, wide), jnp.float32),
            pltpu.VMEM((LEAF_MOST * skel, wide), jnp.float32),
            pltpu.VMEM((samples, 2 * half), jnp.float32),
            pltpu.VMEM((skel, 2 * half), jnp.float32),
            pltpu.SemaphoreType.DMA((2,)),
        ],
        compiler_params=pltpu.CompilerParams(vmem_limit_bytes=12 * 2**20),
    )(plan, here, *parts)


def exchange(value, axis, flip):
    pairs = [(k, k ^ flip) for k in range(lax.axis_size(axis))]
    return lax.ppermute(value, axis, pairs)


def largest(value, axis):
    size = lax.axis_size(axis)
    every = jnp.broadcast_to(value[None], (size, *value.shape))
    return jnp.max(lax.all_to_all(every, axis, 0, 0), axis=0)


def local(frontal, sample_cols, leaf_first, leaf_owner, skeleton):
    n_col = lax.axis_size("col")
    n_row = lax.axis_size("row")
    own = sample_cols.T
    group_rows = frontal.shape[0]
    depth = own.shape[1]
    cut = depth // 2 // LANES * LANES
    one = exchange(own, "row", 1)
    two = exchange(own, "row", 2)
    *blocks, place_row, place_kind, edges = bring(
        frontal, leaf_first, leaf_owner, depth, n_row, n_col
    )
    one, two, edges = lax.optimization_barrier((one, two, edges))
    last = [exchange(two[:, :cut], "row", 1), exchange(one[:, cut:], "row", 2)]
    block_last, begun = near_product(frontal, own, edges, blocks, one, two)
    keep, swap = last_product(block_last, begun, (place_row, place_kind), last, n_col)
    swap, leaf_first = lax.optimization_barrier((swap, leaf_first))
    swapped = exchange(swap, "col", 1)
    plan = plan_of(leaf_first, leaf_owner, skeleton.T, group_rows, n_row, n_col)
    here, *away = squeeze(keep, swapped, n_col // 2)
    parts = [exchange(away[k - 1], "col", 2 * k) for k in range(n_col // 2 - 1, 0, -1)]
    mine, coeff, worst = leaf_work(here, parts, plan)
    worst = largest(worst, ("row", "col"))
    return (mine, coeff, worst[0, :1])


def solution(mesh):
    return jax.shard_map(
        local,
        mesh=mesh,
        in_specs=(P("row", "col"), P(("col", "row"), None), P(), P(), P()),
        out_specs=(P("row", "col"), P("row", "col"), P()),
        check_vma=False,
    )
```

```python
import functools

import jax
import jax.numpy as jnp
from jax import lax
from jax.experimental import pallas as pl
from jax.experimental.pallas import tpu as pltpu
from jax.sharding import PartitionSpec as P

UNIT = 32
LANES = 128
LEAF_MOST = 4
PICKS = 8
COPIES = 4
LEVELS = 32760.0
EXTRA = 16
PART = 1024
STEPS = 64.0
RUN_LEAVES = 4


def nt_dot(a, b):
    return lax.dot_general(a, b, (((1,), (1,)), ((), ())), preferred_element_type=jnp.float32)


def leaf_blocks(run_rows, width, edges, act):
    group_rows = edges.shape[0] // RUN_LEAVES * run_rows
    row_pos = lax.axis_index("row")
    first_col = lax.axis_index("col") * width
    depth = width // lax.axis_size("row")

    def one(at, carry):
        run = at // (run_rows // LANES)
        begin_row = row_pos * group_rows + run * run_rows
        begin_col = row_pos * group_rows + at * LANES
        inside = begin_col - first_col

        @pl.when((inside >= 0) & (inside < width))
        def _():
            shape = (run_rows, LANES)
            down = lax.broadcasted_iota(jnp.int32, shape, 0) + begin_row
            across = lax.broadcasted_iota(jnp.int32, shape, 1) + begin_col
            leaf_down = jnp.zeros(shape, jnp.int32)
            leaf_across = jnp.zeros(shape, jnp.int32)
            for k in range(1, RUN_LEAVES):
                edge = edges[run * RUN_LEAVES + k]
                leaf_down += (down >= edge).astype(jnp.int32)
                leaf_across += (across >= edge).astype(jnp.int32)
            column = jnp.clip(inside, 0, width - LANES)
            rows = pl.ds(pl.multiple_of(run * run_rows, run_rows), run_rows)
            act((column // depth) ^ row_pos, rows, column, leaf_down == leaf_across)

        return carry

    lax.fori_loop(0, group_rows // LANES, one, 0)


def multiply(items, value, rows):
    for block, begin, slab in items:
        twice = jnp.concatenate([slab[...], slab[...]], axis=0)
        add = nt_dot(block[rows, pl.ds(begin, slab.shape[1])], twice)
        value = add if value is None else value + add
    return value


def clear_runs(run_rows, width, edges, turns, blocks):
    def act(here, rows, column, same):
        for turn, block in zip(turns, blocks):

            @pl.when(here == turn)
            def _():
                inside = lax.rem(column, block.shape[1])
                lanes = pl.ds(pl.multiple_of(inside, LANES), LANES)
                part = block[rows, lanes].astype(jnp.float32)
                block[rows, lanes] = jnp.where(same, 0.0, part).astype(jnp.bfloat16)

    leaf_blocks(run_rows, width, edges, act)


def bring_block(frontal, turn, block, sems):
    group_rows, depth = block.shape
    begin = pl.multiple_of((lax.axis_index("row") ^ turn) * depth, LANES)
    part = group_rows // COPIES
    copies = []
    for at in range(COPIES):
        rows = pl.ds(at * part, part)
        piece = frontal.at[rows, pl.ds(begin, depth)]
        copies.append(pltpu.make_async_copy(piece, block.at[rows, :], sems.at[at]))
    return copies


def parts_of(group_rows):
    part = min(group_rows, PART)
    return [pl.ds(at, part) for at in range(0, group_rows, part)]


def plan_leaves(n_row, group_rows, capacity, first, owners, skel, plan):
    leaves = first.shape[0]
    per_group = leaves // n_row
    count_skel = skel.shape[0]
    row_pos = lax.axis_index("row")
    col_pos = lax.axis_index("col")

    def clear(at, carry):
        plan[at] = capacity
        return carry

    lax.fori_loop(0, plan.shape[0], clear, 0)

    def find(at, carry):
        count, filled = carry
        leaf = row_pos * per_group + at
        begin = first[leaf]
        following = first[jnp.minimum(leaf + 1, leaves - 1)]
        end = jnp.where(at + 1 < per_group, following, (row_pos + 1) * group_rows)
        hit = (owners[leaf] == col_pos) & (count < LEAF_MOST)

        @pl.when(hit)
        def _():
            plan[count] = filled
            for k in range(count_skel):
                plan[PICKS + count * count_skel + k] = filled + skel[k, leaf] - begin

        return jnp.where(hit, count + 1, count), jnp.where(hit, filled + end - begin, filled)

    count, _ = lax.fori_loop(0, per_group, find, (jnp.int32(0), jnp.int32(0)))
    plan[LEAF_MOST] = count


def bring_kernel(n_row, n_col, leaf_first, leaf_owner, skeleton, frontal, *refs):
    *blocks, place_row, place_kind, plan, edges, first, owners, skel, used, sems, block_sems = refs
    group_rows, width = frontal.shape
    leaves = leaf_first.shape[0]
    per_group = leaves // n_row
    run_rows = group_rows // (per_group // RUN_LEAVES)
    half = group_rows // n_col
    per_half = half // UNIT
    row_pos = lax.axis_index("row")
    col_pos = lax.axis_index("col")
    copies = [
        pltpu.make_async_copy(leaf_first, first, sems.at[0]),
        pltpu.make_async_copy(leaf_owner, owners, sems.at[1]),
        pltpu.make_async_copy(skeleton, skel, sems.at[2]),
    ]
    for turn, block in enumerate(blocks):
        copies.extend(bring_block(frontal, turn, block, block_sems.at[turn]))
    for copy in copies:
        copy.start()

    def clear(at, carry):
        used[at] = 0
        return carry

    lax.fori_loop(0, n_col, clear, 0)
    for copy in copies[:3]:
        copy.wait()

    def edge(at, carry):
        edges[at] = first[row_pos * per_group + at]
        return carry

    lax.fori_loop(0, per_group, edge, 0)

    def place(unit, leaf):
        row = row_pos * group_rows + unit * UNIT
        later = jnp.minimum(leaf + 1, leaves - 1)
        moved = (leaf + 1 < leaves) & (first[later] <= row)
        leaf = jnp.where(moved, later, leaf)
        owner = owners[leaf]
        slot = used[owner]
        used[owner] = slot + 1
        step = owner ^ col_pos
        place_row[unit] = step // 2 * half + slot % per_half * UNIT
        place_kind[unit] = step % 2 * 2 + slot // per_half
        return leaf

    lax.fori_loop(0, group_rows // UNIT, place, row_pos * per_group)
    plan_leaves(n_row, group_rows, 2 * half, first, owners, skel, plan)
    for copy in copies[3:]:
        copy.wait()
    clear_runs(run_rows, width, edges, range(len(blocks)), blocks)


def near_kernel(edges, frontal, own, *refs):
    *blocks, one, two, block_last, total, near, sem, sems = refs
    group_rows, width = frontal.shape
    run_rows = group_rows // (edges.shape[0] // RUN_LEAVES)
    own_copy = pltpu.make_async_copy(own, near, sem)
    copies = bring_block(frontal, len(blocks), block_last, sems)
    for copy in [own_copy, *copies]:
        copy.start()
    for rows in parts_of(group_rows):
        total[rows, :] = multiply([(blocks[1], 0, one), (blocks[2], 0, two)], None, rows)
    own_copy.wait()
    for rows in parts_of(group_rows):
        total[rows, :] = multiply([(blocks[0], 0, near)], total[rows, :], rows)
    for copy in copies:
        copy.wait()
    clear_runs(run_rows, width, edges, [len(blocks)], [block_last])


def last_kernel(place_row, place_kind, block, begun, left, right, keep, swap):
    items = [(block, 0, left), (block, left.shape[1], right)]
    wide = keep.shape[1]
    lane = lax.broadcasted_iota(jnp.int32, (UNIT, wide), 1) // (wide // 2)
    keep[...] = jnp.zeros(keep.shape, jnp.float32)
    swap[...] = jnp.zeros(swap.shape, jnp.float32)
    for rows in parts_of(block.shape[0]):
        value = multiply(items, begun[rows, :], rows)
        for at in range(rows.size // UNIT):
            unit = rows.start // UNIT + at
            to_rows = pl.ds(pl.multiple_of(place_row[unit], UNIT), UNIT)
            piece = value[at * UNIT : (at + 1) * UNIT]
            kind = place_kind[unit]
            pltpu.store(keep.at[to_rows, :], piece, mask=lane == kind)
            pltpu.store(swap.at[to_rows, :], piece, mask=lane + 2 == kind)


def vmem(count=None):
    spec = pl.BlockSpec(memory_space=pltpu.VMEM)
    return spec if count is None else [spec] * count


def smem():
    return pl.BlockSpec(memory_space=pltpu.SMEM)


def hbm():
    return pl.BlockSpec(memory_space=pltpu.HBM)


def in_hbm(value):
    return pltpu.with_memory_space_constraint(value, pltpu.HBM)


def product_cost(frontal, samples, slabs):
    group_rows, width = frontal.shape
    flops = 8 * group_rows * width * samples * slabs // 4
    return pl.CostEstimate(flops=flops, bytes_accessed=flops // samples, transcendentals=0)


def bring(frontal, leaf_first, leaf_owner, skeleton, depth, n_row, n_col):
    group_rows, width = frontal.shape
    leaves = leaf_first.shape[0]
    units = jax.ShapeDtypeStruct((group_rows // UNIT,), jnp.int32)
    block = jax.ShapeDtypeStruct((group_rows, depth), frontal.dtype)
    return pl.pallas_call(
        functools.partial(bring_kernel, n_row, n_col),
        in_specs=[hbm()] * 4,
        out_specs=vmem(n_row - 1) + [smem()] * 4,
        out_shape=[block] * (n_row - 1)
        + [
            units,
            units,
            jax.ShapeDtypeStruct((PICKS + LEAF_MOST * skeleton.shape[0],), jnp.int32),
            jax.ShapeDtypeStruct((leaves // n_row,), jnp.int32),
        ],
        scratch_shapes=[
            pltpu.SMEM((leaves,), jnp.int32),
            pltpu.SMEM((leaves,), jnp.int32),
            pltpu.SMEM(skeleton.shape, jnp.int32),
            pltpu.SMEM((n_col,), jnp.int32),
            pltpu.SemaphoreType.DMA((3,)),
            pltpu.SemaphoreType.DMA((n_row - 1, COPIES)),
        ],
        cost_estimate=product_cost(frontal, 64, 4),
        compiler_params=pltpu.CompilerParams(vmem_limit_bytes=24 * 2**20),
    )(*(in_hbm(x) for x in (leaf_first, leaf_owner, skeleton, frontal)))


def near_product(frontal, own, edges, blocks, one, two):
    group_rows, width = frontal.shape
    samples = own.shape[0]
    return pl.pallas_call(
        near_kernel,
        in_specs=[smem(), hbm(), hbm()] + vmem(len(blocks) + 2),
        out_specs=vmem(2),
        out_shape=[
            jax.ShapeDtypeStruct(blocks[0].shape, frontal.dtype),
            jax.ShapeDtypeStruct((group_rows, 2 * samples), jnp.float32),
        ],
        scratch_shapes=[
            pltpu.VMEM(own.shape, own.dtype),
            pltpu.SemaphoreType.DMA,
            pltpu.SemaphoreType.DMA((COPIES,)),
        ],
        cost_estimate=product_cost(frontal, samples, 4),
        compiler_params=pltpu.CompilerParams(vmem_limit_bytes=24 * 2**20),
    )(edges, in_hbm(frontal), in_hbm(own), *blocks, one, two)


def last_product(block, begun, places, last, n_col):
    group_rows, wide = begun.shape
    laid = jax.ShapeDtypeStruct((group_rows // 2, wide), jnp.float32)
    return pl.pallas_call(
        last_kernel,
        in_specs=[smem()] * 2 + vmem(4),
        out_specs=vmem(2),
        out_shape=[laid, laid],
        cost_estimate=product_cost(block, wide // 2, 4),
        compiler_params=pltpu.CompilerParams(vmem_limit_bytes=24 * 2**20),
    )(*places, block, begun, *last)


def squeeze_kernel(keep, swapped, here, *away):
    wide, half = here.shape
    samples = wide // 2
    here[...] = (keep[:half] + swapped[:half]).T
    row = lax.broadcasted_iota(jnp.int32, (EXTRA, half), 0)
    for k, out in enumerate(away):
        at = pl.ds((k + 1) * half, half)
        block = (keep[at, :] + swapped[at, :]).T
        tail = jnp.zeros(row.shape, jnp.float32)
        for side in range(2):
            rows = slice(side * samples, (side + 1) * samples)
            part = block[rows]
            most = jnp.maximum(jnp.max(jnp.abs(part), axis=0, keepdims=True), 1e-30)
            power = jnp.ceil(jnp.log2(most) * STEPS)
            scaled = part * (LEVELS * jnp.exp2(power * (-1.0 / STEPS)))
            whole = jnp.floor(scaled + 0.5).astype(jnp.int32)
            out[rows, :] = whole.astype(jnp.int16)
            tail = jnp.where(row == side, power, tail)
        out[pl.ds(2 * samples, EXTRA), :] = tail.astype(jnp.int32).astype(jnp.int16)


def squeeze(keep, swapped, chips):
    rows, wide = keep.shape
    half = rows // chips
    small = jax.ShapeDtypeStruct((wide + EXTRA, half), jnp.int16)
    return pl.pallas_call(
        squeeze_kernel,
        in_specs=vmem(2),
        out_specs=vmem(chips),
        out_shape=[jax.ShapeDtypeStruct((wide, half), jnp.float32)] + [small] * (chips - 1),
        compiler_params=pltpu.CompilerParams(vmem_limit_bytes=24 * 2**20),
    )(keep, swapped)


def thirds(value):
    high = value.astype(jnp.bfloat16)
    rest = value - high.astype(jnp.float32)
    middle = rest.astype(jnp.bfloat16)
    low = (rest - middle.astype(jnp.float32)).astype(jnp.bfloat16)
    return high, middle, low


def beside(left, right):
    wide = left.shape[1]
    lane = lax.broadcasted_iota(jnp.int32, left.shape, 1)
    joined = jnp.where(lane < wide // 2, left.astype(jnp.float32), right.astype(jnp.float32))
    return joined.astype(jnp.bfloat16)


def left_terms(high, middle, low):
    return jnp.concatenate([high, beside(middle, high), beside(low, middle)], axis=1)


def right_terms(high, middle, low):
    return jnp.concatenate([high, middle, high, low, high, middle], axis=0)


def plain_dot(a, b):
    return jnp.dot(a, b, preferred_element_type=jnp.float32)


def leaf_kernel(skel, plan, *refs):
    here, *parts = refs[:-8]
    mine_out, coeff_out, worst_out, mine, picked, turned, coeff, sems = refs[-8:]
    wide, half = here.shape
    samples = wide // 2
    capacity = 2 * half
    every = LEAF_MOST * skel

    sides = [here[pl.ds(0, samples), :], here[pl.ds(samples, samples), :]]
    for part in parts:
        tail = part[pl.ds(wide, EXTRA), :].astype(jnp.int32).astype(jnp.float32)
        step = jnp.exp2(tail * (1.0 / STEPS)) * (1.0 / LEVELS)
        for side in range(2):
            value = part[pl.ds(side * samples, samples), :].astype(jnp.int32).astype(jnp.float32)
            sides[side] = sides[side] + value * step[side : side + 1]
    mine_t = jnp.concatenate(sides, axis=1)
    turned[...] = mine_t
    send_mine = pltpu.make_async_copy(turned, mine_out, sems.at[0])
    send_mine.start()
    total = jnp.concatenate(sides, axis=0).T
    other = pltpu.roll(total, samples, 1)
    low_half = lax.broadcasted_iota(jnp.int32, total.shape, 1) < samples
    mine[pl.ds(0, half), :] = jnp.where(low_half, total, other)
    mine[pl.ds(half, half), :] = jnp.where(low_half, other, total)
    mine[pl.ds(capacity, 8), :] = jnp.zeros((8, wide), jnp.float32)
    for k in range(every):
        picked[pl.ds(k, 1), :] = mine[pl.ds(plan[PICKS + k], 1), :]
    begins = [plan[b] for b in range(LEAF_MOST)]
    count = plan[LEAF_MOST]
    chosen = picked[...]

    high, middle, low = thirds(chosen)
    across = left_terms(high, middle, low)
    down = jnp.concatenate([beside(high, middle), beside(high, low), beside(high, middle)], axis=1)
    gram = nt_dot(across, down)
    proj = plain_dot(across, right_terms(*thirds(mine_t)))

    slot = lax.broadcasted_iota(jnp.int32, (skel, capacity), 1)
    rank = jnp.zeros((skel, capacity), jnp.int32)
    for b in range(1, LEAF_MOST):
        rank += (slot >= begins[b]).astype(jnp.int32)
    hot = [rank == b for b in range(LEAF_MOST)]
    hot_rows = jnp.concatenate([h.astype(jnp.float32) for h in hot], axis=0).astype(jnp.bfloat16)

    lane_leaf = lax.broadcasted_iota(jnp.int32, (skel, every), 1) // skel
    lane_row = lax.broadcasted_iota(jnp.int32, (skel, every), 1) % skel
    below = lax.broadcasted_iota(jnp.int32, (skel, every), 0)
    joined = jnp.where((below == lane_row) & (count == 0), 1.0, 0.0)
    for b in range(LEAF_MOST):
        joined += jnp.where(lane_leaf == b, gram[b * skel : (b + 1) * skel], 0.0)
    terms = [term.astype(jnp.float32) for term in thirds(joined)]
    terms = jnp.concatenate(terms + [jnp.zeros_like(joined)], axis=1)
    turn = lax.broadcasted_iota(jnp.int32, terms.shape, 1) % skel
    spread = jnp.concatenate([jnp.where(turn == i, terms, 0.0) for i in range(skel)], axis=0)
    system = plain_dot(spread.astype(jnp.bfloat16), jnp.concatenate([hot_rows] * 4, axis=0))

    lines = [system[i * skel : (i + 1) * skel] for i in range(skel)]
    right = jnp.zeros((skel, capacity), jnp.float32)
    for b in range(LEAF_MOST):
        right += jnp.where(hot[b], proj[b * skel : (b + 1) * skel], 0.0)
    index = lax.broadcasted_iota(jnp.int32, (skel, capacity), 0)
    uppers = []
    pivots = []
    for j in range(skel):
        line = lines[j]
        inverse = 1.0 / line[j : j + 1]
        upper = line * inverse
        uppers.append(upper)
        pivots.append(inverse)
        for i in range(j + 1, skel):
            lines[i] = lines[i] - line[i : i + 1] * upper
        right = right - jnp.where(index > j, upper * right[j : j + 1], 0.0)
    solved = right * jnp.concatenate(pivots, axis=0)
    for j in range(skel - 2, -1, -1):
        known = jnp.where(index > j, uppers[j] * solved, 0.0)
        less = jnp.sum(known, axis=0, keepdims=True)
        solved = jnp.where(index == j, solved - less, solved)
    coeff[...] = solved
    send_coeff = pltpu.make_async_copy(coeff, coeff_out, sems.at[1])
    send_coeff.start()

    weights = jnp.concatenate([jnp.where(h, solved, 0.0) for h in hot], axis=0)
    upright = chosen.T[:samples]
    upright = thirds(jnp.concatenate([upright, upright], axis=1))
    rebuilt = plain_dot(left_terms(*upright), right_terms(*thirds(weights)))
    resid = mine_t - rebuilt
    err = jnp.sum(resid * resid, axis=0, keepdims=True)
    norm = jnp.sum(mine_t * mine_t, axis=0, keepdims=True)
    worst = jnp.zeros((1, 1), jnp.float32)
    for b in range(LEAF_MOST):
        near = hot[b][:1]
        err_leaf = jnp.sum(jnp.where(near, err, 0.0), axis=1, keepdims=True)
        norm_leaf = jnp.sum(jnp.where(near, norm, 0.0), axis=1, keepdims=True)
        worst = jnp.maximum(worst, jnp.sqrt(err_leaf) / jnp.sqrt(norm_leaf + 1e-06))
    worst_out[...] = jnp.broadcast_to(worst, worst_out.shape)
    send_mine.wait()
    send_coeff.wait()


def leaf_work(here, parts, plan):
    wide, half = here.shape
    samples = wide // 2
    skel = (plan.shape[0] - PICKS) // LEAF_MOST
    return pl.pallas_call(
        functools.partial(leaf_kernel, skel),
        in_specs=[smem()] + vmem(1 + len(parts)),
        out_specs=[hbm(), hbm(), vmem()],
        out_shape=[
            jax.ShapeDtypeStruct((samples, 2 * half), jnp.float32),
            jax.ShapeDtypeStruct((skel, 2 * half), jnp.float32),
            jax.ShapeDtypeStruct((1, LANES), jnp.float32),
        ],
        scratch_shapes=[
            pltpu.VMEM((2 * half + 8, wide), jnp.float32),
            pltpu.VMEM((LEAF_MOST * skel, wide), jnp.float32),
            pltpu.VMEM((samples, 2 * half), jnp.float32),
            pltpu.VMEM((skel, 2 * half), jnp.float32),
            pltpu.SemaphoreType.DMA((2,)),
        ],
        compiler_params=pltpu.CompilerParams(vmem_limit_bytes=12 * 2**20),
    )(plan, here, *parts)


def exchange(value, axis, flip):
    pairs = [(k, k ^ flip) for k in range(lax.axis_size(axis))]
    return lax.ppermute(value, axis, pairs)


def largest(value, axis):
    size = lax.axis_size(axis)
    every = jnp.broadcast_to(value[None], (size, *value.shape))
    return jnp.max(lax.all_to_all(every, axis, 0, 0), axis=0)


def local(frontal, sample_cols, leaf_first, leaf_owner, skeleton):
    n_col = lax.axis_size("col")
    n_row = lax.axis_size("row")
    own = sample_cols.T
    depth = own.shape[1]
    cut = depth // 2 // LANES * LANES
    one = exchange(own, "row", 1)
    two = exchange(own, "row", 2)
    *blocks, place_row, place_kind, plan, edges = bring(
        frontal, leaf_first, leaf_owner, skeleton.T, depth, n_row, n_col
    )
    one, two, edges = lax.optimization_barrier((one, two, edges))
    last = [exchange(two[:, :cut], "row", 1), exchange(one[:, cut:], "row", 2)]
    block_last, begun = near_product(frontal, own, edges, blocks, one, two)
    keep, swap = last_product(block_last, begun, (place_row, place_kind), last, n_col)
    swapped = exchange(swap, "col", 1)
    here, *away = squeeze(keep, swapped, n_col // 2)
    parts = [exchange(away[k - 1], "col", 2 * k) for k in range(n_col // 2 - 1, 0, -1)]
    mine, coeff, worst = leaf_work(here, parts, plan)
    worst = largest(worst, ("row", "col"))
    return (mine, coeff, worst[0, :1])


def solution(mesh):
    return jax.shard_map(
        local,
        mesh=mesh,
        in_specs=(P("row", "col"), P(("col", "row"), None), P(), P(), P()),
        out_specs=(P("row", "col"), P("row", "col"), P()),
        check_vma=False,
    )
```

```python
import functools

import jax
import jax.numpy as jnp
from jax import lax
from jax.experimental import pallas as pl
from jax.experimental.pallas import tpu as pltpu
from jax.sharding import PartitionSpec as P

UNIT = 32
LANES = 128
LEAF_MOST = 4
PICKS = 8
COPIES = 1
LEVELS = 32760.0
EXTRA = 16
PART = 1024
STEPS = 64.0
RUN_LEAVES = 4


def nt_dot(a, b):
    return lax.dot_general(a, b, (((1,), (1,)), ((), ())), preferred_element_type=jnp.float32)


def leaf_blocks(run_rows, width, edges, act):
    group_rows = edges.shape[0] // RUN_LEAVES * run_rows
    row_pos = lax.axis_index("row")
    first_col = lax.axis_index("col") * width
    depth = width // lax.axis_size("row")

    def one(at, carry):
        run = at // (run_rows // LANES)
        begin_row = row_pos * group_rows + run * run_rows
        begin_col = row_pos * group_rows + at * LANES
        inside = begin_col - first_col

        @pl.when((inside >= 0) & (inside < width))
        def _():
            shape = (run_rows, LANES)
            down = lax.broadcasted_iota(jnp.int32, shape, 0) + begin_row
            across = lax.broadcasted_iota(jnp.int32, shape, 1) + begin_col
            leaf_down = jnp.zeros(shape, jnp.int32)
            leaf_across = jnp.zeros(shape, jnp.int32)
            for k in range(1, RUN_LEAVES):
                edge = edges[run * RUN_LEAVES + k]
                leaf_down += (down >= edge).astype(jnp.int32)
                leaf_across += (across >= edge).astype(jnp.int32)
            column = jnp.clip(inside, 0, width - LANES)
            rows = pl.ds(pl.multiple_of(run * run_rows, run_rows), run_rows)
            act((column // depth) ^ row_pos, rows, column, leaf_down == leaf_across)

        return carry

    lax.fori_loop(0, group_rows // LANES, one, 0)


def multiply(items, value, rows):
    for block, begin, slab in items:
        twice = jnp.concatenate([slab[...], slab[...]], axis=0)
        add = nt_dot(block[rows, pl.ds(begin, slab.shape[1])], twice)
        value = add if value is None else value + add
    return value


def clear_runs(run_rows, width, edges, turns, blocks):
    def act(here, rows, column, same):
        for turn, block in zip(turns, blocks):

            @pl.when(here == turn)
            def _():
                inside = lax.rem(column, block.shape[1])
                lanes = pl.ds(pl.multiple_of(inside, LANES), LANES)
                part = block[rows, lanes].astype(jnp.float32)
                block[rows, lanes] = jnp.where(same, 0.0, part).astype(jnp.bfloat16)

    leaf_blocks(run_rows, width, edges, act)


def bring_block(frontal, turn, block, sems):
    group_rows, depth = block.shape
    begin = pl.multiple_of((lax.axis_index("row") ^ turn) * depth, LANES)
    part = group_rows // COPIES
    copies = []
    for at in range(COPIES):
        rows = pl.ds(at * part, part)
        piece = frontal.at[rows, pl.ds(begin, depth)]
        copies.append(pltpu.make_async_copy(piece, block.at[rows, :], sems.at[at]))
    return copies


def parts_of(group_rows):
    part = min(group_rows, PART)
    return [pl.ds(at, part) for at in range(0, group_rows, part)]


def plan_leaves(n_row, group_rows, capacity, first, owners, skel, plan):
    leaves = first.shape[0]
    per_group = leaves // n_row
    count_skel = skel.shape[0]
    row_pos = lax.axis_index("row")
    col_pos = lax.axis_index("col")

    def clear(at, carry):
        plan[at] = capacity
        return carry

    lax.fori_loop(0, plan.shape[0], clear, 0)

    def find(at, carry):
        count, filled = carry
        leaf = row_pos * per_group + at
        begin = first[leaf]
        following = first[jnp.minimum(leaf + 1, leaves - 1)]
        end = jnp.where(at + 1 < per_group, following, (row_pos + 1) * group_rows)
        hit = (owners[leaf] == col_pos) & (count < LEAF_MOST)

        @pl.when(hit)
        def _():
            plan[count] = filled
            for k in range(count_skel):
                plan[PICKS + count * count_skel + k] = filled + skel[k, leaf] - begin

        return jnp.where(hit, count + 1, count), jnp.where(hit, filled + end - begin, filled)

    count, _ = lax.fori_loop(0, per_group, find, (jnp.int32(0), jnp.int32(0)))
    plan[LEAF_MOST] = count


def bring_kernel(n_row, n_col, leaf_first, leaf_owner, skeleton, frontal, *refs):
    *blocks, place_row, place_kind, plan, first, owners, skel, edges, used, sems, block_sems = refs
    group_rows, width = frontal.shape
    leaves = leaf_first.shape[0]
    per_group = leaves // n_row
    run_rows = group_rows // (per_group // RUN_LEAVES)
    half = group_rows // n_col
    per_half = half // UNIT
    row_pos = lax.axis_index("row")
    col_pos = lax.axis_index("col")
    copies = [
        pltpu.make_async_copy(leaf_first, first, sems.at[0]),
        pltpu.make_async_copy(leaf_owner, owners, sems.at[1]),
        pltpu.make_async_copy(skeleton, skel, sems.at[2]),
    ]
    for turn, block in enumerate(blocks):
        copies.extend(bring_block(frontal, turn, block, block_sems.at[turn]))
    for copy in copies:
        copy.start()

    def clear(at, carry):
        used[at] = 0
        return carry

    lax.fori_loop(0, n_col, clear, 0)
    for copy in copies[:3]:
        copy.wait()

    def edge(at, carry):
        edges[at] = first[row_pos * per_group + at]
        return carry

    lax.fori_loop(0, per_group, edge, 0)

    def place(unit, leaf):
        row = row_pos * group_rows + unit * UNIT
        later = jnp.minimum(leaf + 1, leaves - 1)
        moved = (leaf + 1 < leaves) & (first[later] <= row)
        leaf = jnp.where(moved, later, leaf)
        owner = owners[leaf]
        slot = used[owner]
        used[owner] = slot + 1
        step = owner ^ col_pos
        place_row[unit] = step // 2 * half + slot % per_half * UNIT
        place_kind[unit] = step % 2 * 2 + slot // per_half
        return leaf

    lax.fori_loop(0, group_rows // UNIT, place, row_pos * per_group)
    plan_leaves(n_row, group_rows, 2 * half, first, owners, skel, plan)
    for copy in copies[3:]:
        copy.wait()
    clear_runs(run_rows, width, edges, range(len(blocks)), blocks)


def near_kernel(own, *refs):
    *blocks, one, two, total, near, sem = refs
    own_copy = pltpu.make_async_copy(own, near, sem)
    own_copy.start()
    items = [(blocks[1], 0, one), (blocks[2], 0, two)]
    for rows in parts_of(total.shape[0]):
        total[rows, :] = multiply(items, None, rows)
    own_copy.wait()
    for rows in parts_of(total.shape[0]):
        total[rows, :] = multiply([(blocks[0], 0, near)], total[rows, :], rows)


def last_kernel(place_row, place_kind, block, begun, left, right, keep, swap):
    items = [(block, 0, left), (block, left.shape[1], right)]
    wide = keep.shape[1]
    lane = lax.broadcasted_iota(jnp.int32, (UNIT, wide), 1) // (wide // 2)
    keep[...] = jnp.zeros(keep.shape, jnp.float32)
    swap[...] = jnp.zeros(swap.shape, jnp.float32)
    for rows in parts_of(block.shape[0]):
        value = multiply(items, begun[rows, :], rows)
        for at in range(rows.size // UNIT):
            unit = rows.start // UNIT + at
            to_rows = pl.ds(pl.multiple_of(place_row[unit], UNIT), UNIT)
            piece = value[at * UNIT : (at + 1) * UNIT]
            kind = place_kind[unit]
            pltpu.store(keep.at[to_rows, :], piece, mask=lane == kind)
            pltpu.store(swap.at[to_rows, :], piece, mask=lane + 2 == kind)


def vmem(count=None):
    spec = pl.BlockSpec(memory_space=pltpu.VMEM)
    return spec if count is None else [spec] * count


def smem():
    return pl.BlockSpec(memory_space=pltpu.SMEM)


def hbm():
    return pl.BlockSpec(memory_space=pltpu.HBM)


def in_hbm(value):
    return pltpu.with_memory_space_constraint(value, pltpu.HBM)


def product_cost(frontal, samples, slabs):
    group_rows, width = frontal.shape
    flops = 8 * group_rows * width * samples * slabs // 4
    return pl.CostEstimate(flops=flops, bytes_accessed=flops // samples, transcendentals=0)


def bring(frontal, leaf_first, leaf_owner, skeleton, depth, n_row, n_col):
    group_rows, width = frontal.shape
    leaves = leaf_first.shape[0]
    units = jax.ShapeDtypeStruct((group_rows // UNIT,), jnp.int32)
    block = jax.ShapeDtypeStruct((group_rows, depth), frontal.dtype)
    return pl.pallas_call(
        functools.partial(bring_kernel, n_row, n_col),
        in_specs=[hbm()] * 4,
        out_specs=vmem(n_row) + [smem()] * 3,
        out_shape=[block] * n_row
        + [
            units,
            units,
            jax.ShapeDtypeStruct((PICKS + LEAF_MOST * skeleton.shape[0],), jnp.int32),
        ],
        scratch_shapes=[
            pltpu.SMEM((leaves,), jnp.int32),
            pltpu.SMEM((leaves,), jnp.int32),
            pltpu.SMEM(skeleton.shape, jnp.int32),
            pltpu.SMEM((leaves // n_row,), jnp.int32),
            pltpu.SMEM((n_col,), jnp.int32),
            pltpu.SemaphoreType.DMA((3,)),
            pltpu.SemaphoreType.DMA((n_row, COPIES)),
        ],
        cost_estimate=product_cost(frontal, 64, 4),
        compiler_params=pltpu.CompilerParams(vmem_limit_bytes=24 * 2**20),
    )(*(in_hbm(x) for x in (leaf_first, leaf_owner, skeleton, frontal)))


def near_product(own, blocks, one, two):
    group_rows = blocks[0].shape[0]
    samples = own.shape[0]
    return pl.pallas_call(
        near_kernel,
        in_specs=[hbm()] + vmem(len(blocks) + 2),
        out_specs=vmem(),
        out_shape=jax.ShapeDtypeStruct((group_rows, 2 * samples), jnp.float32),
        scratch_shapes=[pltpu.VMEM(own.shape, own.dtype), pltpu.SemaphoreType.DMA],
        cost_estimate=product_cost(blocks[0], samples, 12),
        compiler_params=pltpu.CompilerParams(vmem_limit_bytes=24 * 2**20),
    )(in_hbm(own), *blocks, one, two)


def last_product(block, begun, places, last, n_col):
    group_rows, wide = begun.shape
    laid = jax.ShapeDtypeStruct((group_rows // 2, wide), jnp.float32)
    return pl.pallas_call(
        last_kernel,
        in_specs=[smem()] * 2 + vmem(4),
        out_specs=vmem(2),
        out_shape=[laid, laid],
        cost_estimate=product_cost(block, wide // 2, 4),
        compiler_params=pltpu.CompilerParams(vmem_limit_bytes=24 * 2**20),
    )(*places, block, begun, *last)


def squeeze_kernel(keep, swapped, here, *away):
    wide, half = here.shape
    samples = wide // 2
    here[...] = (keep[:half] + swapped[:half]).T
    row = lax.broadcasted_iota(jnp.int32, (EXTRA, half), 0)
    for k, out in enumerate(away):
        at = pl.ds((k + 1) * half, half)
        block = (keep[at, :] + swapped[at, :]).T
        tail = jnp.zeros(row.shape, jnp.float32)
        for side in range(2):
            rows = slice(side * samples, (side + 1) * samples)
            part = block[rows]
            most = jnp.maximum(jnp.max(jnp.abs(part), axis=0, keepdims=True), 1e-30)
            power = jnp.ceil(jnp.log2(most) * STEPS)
            scaled = part * (LEVELS * jnp.exp2(power * (-1.0 / STEPS)))
            whole = jnp.floor(scaled + 0.5).astype(jnp.int32)
            out[rows, :] = whole.astype(jnp.int16)
            tail = jnp.where(row == side, power, tail)
        out[pl.ds(2 * samples, EXTRA), :] = tail.astype(jnp.int32).astype(jnp.int16)


def squeeze(keep, swapped, chips):
    rows, wide = keep.shape
    half = rows // chips
    small = jax.ShapeDtypeStruct((wide + EXTRA, half), jnp.int16)
    return pl.pallas_call(
        squeeze_kernel,
        in_specs=vmem(2),
        out_specs=vmem(chips),
        out_shape=[jax.ShapeDtypeStruct((wide, half), jnp.float32)] + [small] * (chips - 1),
        compiler_params=pltpu.CompilerParams(vmem_limit_bytes=24 * 2**20),
    )(keep, swapped)


def thirds(value):
    high = value.astype(jnp.bfloat16)
    rest = value - high.astype(jnp.float32)
    middle = rest.astype(jnp.bfloat16)
    low = (rest - middle.astype(jnp.float32)).astype(jnp.bfloat16)
    return high, middle, low


def beside(left, right):
    wide = left.shape[1]
    lane = lax.broadcasted_iota(jnp.int32, left.shape, 1)
    joined = jnp.where(lane < wide // 2, left.astype(jnp.float32), right.astype(jnp.float32))
    return joined.astype(jnp.bfloat16)


def left_terms(high, middle, low):
    return jnp.concatenate([high, beside(middle, high), beside(low, middle)], axis=1)


def right_terms(high, middle, low):
    return jnp.concatenate([high, middle, high, low, high, middle], axis=0)


def plain_dot(a, b):
    return jnp.dot(a, b, preferred_element_type=jnp.float32)


def leaf_kernel(skel, plan, *refs):
    here, *parts = refs[:-8]
    mine_out, coeff_out, worst_out, mine, picked, turned, coeff, sems = refs[-8:]
    wide, half = here.shape
    samples = wide // 2
    capacity = 2 * half
    every = LEAF_MOST * skel

    sides = [here[pl.ds(0, samples), :], here[pl.ds(samples, samples), :]]
    for part in parts:
        tail = part[pl.ds(wide, EXTRA), :].astype(jnp.int32).astype(jnp.float32)
        step = jnp.exp2(tail * (1.0 / STEPS)) * (1.0 / LEVELS)
        for side in range(2):
            value = part[pl.ds(side * samples, samples), :].astype(jnp.int32).astype(jnp.float32)
            sides[side] = sides[side] + value * step[side : side + 1]
    mine_t = jnp.concatenate(sides, axis=1)
    turned[...] = mine_t
    send_mine = pltpu.make_async_copy(turned, mine_out, sems.at[0])
    send_mine.start()
    total = jnp.concatenate(sides, axis=0).T
    other = pltpu.roll(total, samples, 1)
    low_half = lax.broadcasted_iota(jnp.int32, total.shape, 1) < samples
    mine[pl.ds(0, half), :] = jnp.where(low_half, total, other)
    mine[pl.ds(half, half), :] = jnp.where(low_half, other, total)
    mine[pl.ds(capacity, 8), :] = jnp.zeros((8, wide), jnp.float32)
    for k in range(every):
        picked[pl.ds(k, 1), :] = mine[pl.ds(plan[PICKS + k], 1), :]
    begins = [plan[b] for b in range(LEAF_MOST)]
    count = plan[LEAF_MOST]
    chosen = picked[...]

    high, middle, low = thirds(chosen)
    across = left_terms(high, middle, low)
    down = jnp.concatenate([beside(high, middle), beside(high, low), beside(high, middle)], axis=1)
    gram = nt_dot(across, down)
    proj = plain_dot(across, right_terms(*thirds(mine_t)))

    slot = lax.broadcasted_iota(jnp.int32, (skel, capacity), 1)
    rank = jnp.zeros((skel, capacity), jnp.int32)
    for b in range(1, LEAF_MOST):
        rank += (slot >= begins[b]).astype(jnp.int32)
    hot = [rank == b for b in range(LEAF_MOST)]
    hot_rows = jnp.concatenate([h.astype(jnp.float32) for h in hot], axis=0).astype(jnp.bfloat16)

    lane_leaf = lax.broadcasted_iota(jnp.int32, (skel, every), 1) // skel
    lane_row = lax.broadcasted_iota(jnp.int32, (skel, every), 1) % skel
    below = lax.broadcasted_iota(jnp.int32, (skel, every), 0)
    joined = jnp.where((below == lane_row) & (count == 0), 1.0, 0.0)
    for b in range(LEAF_MOST):
        joined += jnp.where(lane_leaf == b, gram[b * skel : (b + 1) * skel], 0.0)
    terms = [term.astype(jnp.float32) for term in thirds(joined)]
    terms = jnp.concatenate(terms + [jnp.zeros_like(joined)], axis=1)
    turn = lax.broadcasted_iota(jnp.int32, terms.shape, 1) % skel
    spread = jnp.concatenate([jnp.where(turn == i, terms, 0.0) for i in range(skel)], axis=0)
    system = plain_dot(spread.astype(jnp.bfloat16), jnp.concatenate([hot_rows] * 4, axis=0))

    lines = [system[i * skel : (i + 1) * skel] for i in range(skel)]
    right = jnp.zeros((skel, capacity), jnp.float32)
    for b in range(LEAF_MOST):
        right += jnp.where(hot[b], proj[b * skel : (b + 1) * skel], 0.0)
    index = lax.broadcasted_iota(jnp.int32, (skel, capacity), 0)
    uppers = []
    pivots = []
    for j in range(skel):
        line = lines[j]
        inverse = 1.0 / line[j : j + 1]
        upper = line * inverse
        uppers.append(upper)
        pivots.append(inverse)
        for i in range(j + 1, skel):
            lines[i] = lines[i] - line[i : i + 1] * upper
        right = right - jnp.where(index > j, upper * right[j : j + 1], 0.0)
    solved = right * jnp.concatenate(pivots, axis=0)
    for j in range(skel - 2, -1, -1):
        known = jnp.where(index > j, uppers[j] * solved, 0.0)
        less = jnp.sum(known, axis=0, keepdims=True)
        solved = jnp.where(index == j, solved - less, solved)
    coeff[...] = solved
    send_coeff = pltpu.make_async_copy(coeff, coeff_out, sems.at[1])
    send_coeff.start()

    weights = jnp.concatenate([jnp.where(h, solved, 0.0) for h in hot], axis=0)
    upright = chosen.T[:samples]
    upright = thirds(jnp.concatenate([upright, upright], axis=1))
    rebuilt = plain_dot(left_terms(*upright), right_terms(*thirds(weights)))
    resid = mine_t - rebuilt
    err = jnp.sum(resid * resid, axis=0, keepdims=True)
    norm = jnp.sum(mine_t * mine_t, axis=0, keepdims=True)
    worst = jnp.zeros((1, 1), jnp.float32)
    for b in range(LEAF_MOST):
        near = hot[b][:1]
        err_leaf = jnp.sum(jnp.where(near, err, 0.0), axis=1, keepdims=True)
        norm_leaf = jnp.sum(jnp.where(near, norm, 0.0), axis=1, keepdims=True)
        worst = jnp.maximum(worst, jnp.sqrt(err_leaf) / jnp.sqrt(norm_leaf + 1e-06))
    worst_out[...] = jnp.broadcast_to(worst, worst_out.shape)
    send_mine.wait()
    send_coeff.wait()


def leaf_work(here, parts, plan):
    wide, half = here.shape
    samples = wide // 2
    skel = (plan.shape[0] - PICKS) // LEAF_MOST
    return pl.pallas_call(
        functools.partial(leaf_kernel, skel),
        in_specs=[smem()] + vmem(1 + len(parts)),
        out_specs=[hbm(), hbm(), vmem()],
        out_shape=[
            jax.ShapeDtypeStruct((samples, 2 * half), jnp.float32),
            jax.ShapeDtypeStruct((skel, 2 * half), jnp.float32),
            jax.ShapeDtypeStruct((1, LANES), jnp.float32),
        ],
        scratch_shapes=[
            pltpu.VMEM((2 * half + 8, wide), jnp.float32),
            pltpu.VMEM((LEAF_MOST * skel, wide), jnp.float32),
            pltpu.VMEM((samples, 2 * half), jnp.float32),
            pltpu.VMEM((skel, 2 * half), jnp.float32),
            pltpu.SemaphoreType.DMA((2,)),
        ],
        compiler_params=pltpu.CompilerParams(vmem_limit_bytes=12 * 2**20),
    )(plan, here, *parts)


def exchange(value, axis, flip):
    pairs = [(k, k ^ flip) for k in range(lax.axis_size(axis))]
    return lax.ppermute(value, axis, pairs)


def largest(value, axis):
    size = lax.axis_size(axis)
    every = jnp.broadcast_to(value[None], (size, *value.shape))
    return jnp.max(lax.all_to_all(every, axis, 0, 0), axis=0)


def local(frontal, sample_cols, leaf_first, leaf_owner, skeleton):
    n_col = lax.axis_size("col")
    n_row = lax.axis_size("row")
    own = sample_cols.T
    depth = own.shape[1]
    cut = depth // 2 // LANES * LANES
    one = exchange(own, "row", 1)
    two = exchange(own, "row", 2)
    *blocks, block_last, place_row, place_kind, plan = bring(
        frontal, leaf_first, leaf_owner, skeleton.T, depth, n_row, n_col
    )
    one, two, plan = lax.optimization_barrier((one, two, plan))
    last = [exchange(two[:, :cut], "row", 1), exchange(one[:, cut:], "row", 2)]
    begun = near_product(own, blocks, one, two)
    keep, swap = last_product(block_last, begun, (place_row, place_kind), last, n_col)
    swapped = exchange(swap, "col", 1)
    here, *away = squeeze(keep, swapped, n_col // 2)
    parts = [exchange(away[k - 1], "col", 2 * k) for k in range(n_col // 2 - 1, 0, -1)]
    mine, coeff, worst = leaf_work(here, parts, plan)
    worst = largest(worst, ("row", "col"))
    return (mine, coeff, worst[0, :1])


def solution(mesh):
    return jax.shard_map(
        local,
        mesh=mesh,
        in_specs=(P("row", "col"), P(("col", "row"), None), P(), P(), P()),
        out_specs=(P("row", "col"), P("row", "col"), P()),
        check_vma=False,
    )
```

```python
import functools

import jax
import jax.numpy as jnp
from jax import lax
from jax.experimental import pallas as pl
from jax.experimental.pallas import tpu as pltpu
from jax.sharding import PartitionSpec as P

UNIT = 32
LANES = 128
LEAF_MOST = 4
PICKS = 8
COPIES = 1
LEVELS = 32760.0
EXTRA = 16
PART = 1024
STEPS = 64.0
RUN_LEAVES = 4


def nt_dot(a, b):
    return lax.dot_general(a, b, (((1,), (1,)), ((), ())), preferred_element_type=jnp.float32)


def leaf_blocks(run_rows, width, edges, act):
    group_rows = edges.shape[0] // RUN_LEAVES * run_rows
    row_pos = lax.axis_index("row")
    first_col = lax.axis_index("col") * width
    depth = width // lax.axis_size("row")

    def one(at, carry):
        run = at // (run_rows // LANES)
        begin_row = row_pos * group_rows + run * run_rows
        begin_col = row_pos * group_rows + at * LANES
        inside = begin_col - first_col

        @pl.when((inside >= 0) & (inside < width))
        def _():
            shape = (run_rows, LANES)
            down = lax.broadcasted_iota(jnp.int32, shape, 0) + begin_row
            across = lax.broadcasted_iota(jnp.int32, shape, 1) + begin_col
            leaf_down = jnp.zeros(shape, jnp.int32)
            leaf_across = jnp.zeros(shape, jnp.int32)
            for k in range(1, RUN_LEAVES):
                edge = edges[run * RUN_LEAVES + k]
                leaf_down += (down >= edge).astype(jnp.int32)
                leaf_across += (across >= edge).astype(jnp.int32)
            column = jnp.clip(inside, 0, width - LANES)
            rows = pl.ds(pl.multiple_of(run * run_rows, run_rows), run_rows)
            act((column // depth) ^ row_pos, rows, column, leaf_down == leaf_across)

        return carry

    lax.fori_loop(0, group_rows // LANES, one, 0)


def multiply(items, value, rows):
    for block, begin, slab in items:
        twice = jnp.concatenate([slab[...], slab[...]], axis=0)
        add = nt_dot(block[rows, pl.ds(begin, slab.shape[1])], twice)
        value = add if value is None else value + add
    return value


def clear_runs(run_rows, width, edges, turns, blocks):
    def act(here, rows, column, same):
        for turn, block in zip(turns, blocks):

            @pl.when(here == turn)
            def _():
                inside = lax.rem(column, block.shape[1])
                lanes = pl.ds(pl.multiple_of(inside, LANES), LANES)
                part = block[rows, lanes].astype(jnp.float32)
                block[rows, lanes] = jnp.where(same, 0.0, part).astype(jnp.bfloat16)

    leaf_blocks(run_rows, width, edges, act)


def bring_block(frontal, turn, block, sems):
    group_rows, depth = block.shape
    begin = pl.multiple_of((lax.axis_index("row") ^ turn) * depth, LANES)
    part = group_rows // COPIES
    copies = []
    for at in range(COPIES):
        rows = pl.ds(at * part, part)
        piece = frontal.at[rows, pl.ds(begin, depth)]
        copies.append(pltpu.make_async_copy(piece, block.at[rows, :], sems.at[at]))
    return copies


def parts_of(group_rows):
    part = min(group_rows, PART)
    return [pl.ds(at, part) for at in range(0, group_rows, part)]


def plan_leaves(n_row, group_rows, capacity, first, owners, skel, plan):
    leaves = first.shape[0]
    per_group = leaves // n_row
    count_skel = skel.shape[0]
    row_pos = lax.axis_index("row")
    col_pos = lax.axis_index("col")

    def clear(at, carry):
        plan[at] = capacity
        return carry

    lax.fori_loop(0, plan.shape[0], clear, 0)

    def find(at, carry):
        count, filled = carry
        leaf = row_pos * per_group + at
        begin = first[leaf]
        following = first[jnp.minimum(leaf + 1, leaves - 1)]
        end = jnp.where(at + 1 < per_group, following, (row_pos + 1) * group_rows)
        hit = (owners[leaf] == col_pos) & (count < LEAF_MOST)

        @pl.when(hit)
        def _():
            plan[count] = filled
            for k in range(count_skel):
                plan[PICKS + count * count_skel + k] = filled + skel[k, leaf] - begin

        return jnp.where(hit, count + 1, count), jnp.where(hit, filled + end - begin, filled)

    count, _ = lax.fori_loop(0, per_group, find, (jnp.int32(0), jnp.int32(0)))
    plan[LEAF_MOST] = count


def bring_kernel(n_row, n_col, leaf_first, leaf_owner, skeleton, own, frontal, *refs):
    *blocks, near, place_row, place_kind, plan = refs[: n_row + 4]
    first, owners, skel, edges, used, sems, block_sems = refs[n_row + 4 :]
    group_rows, width = frontal.shape
    leaves = leaf_first.shape[0]
    per_group = leaves // n_row
    run_rows = group_rows // (per_group // RUN_LEAVES)
    half = group_rows // n_col
    per_half = half // UNIT
    row_pos = lax.axis_index("row")
    col_pos = lax.axis_index("col")
    copies = [
        pltpu.make_async_copy(leaf_first, first, sems.at[0]),
        pltpu.make_async_copy(leaf_owner, owners, sems.at[1]),
        pltpu.make_async_copy(skeleton, skel, sems.at[2]),
        pltpu.make_async_copy(own, near, sems.at[3]),
    ]
    for turn, block in enumerate(blocks):
        copies.extend(bring_block(frontal, turn, block, block_sems.at[turn]))
    for copy in copies:
        copy.start()

    def clear(at, carry):
        used[at] = 0
        return carry

    lax.fori_loop(0, n_col, clear, 0)
    for copy in copies[:3]:
        copy.wait()

    def edge(at, carry):
        edges[at] = first[row_pos * per_group + at]
        return carry

    lax.fori_loop(0, per_group, edge, 0)

    def place(unit, leaf):
        row = row_pos * group_rows + unit * UNIT
        later = jnp.minimum(leaf + 1, leaves - 1)
        moved = (leaf + 1 < leaves) & (first[later] <= row)
        leaf = jnp.where(moved, later, leaf)
        owner = owners[leaf]
        slot = used[owner]
        used[owner] = slot + 1
        step = owner ^ col_pos
        place_row[unit] = step // 2 * half + slot % per_half * UNIT
        place_kind[unit] = step % 2 * 2 + slot // per_half
        return leaf

    lax.fori_loop(0, group_rows // UNIT, place, row_pos * per_group)
    plan_leaves(n_row, group_rows, 2 * half, first, owners, skel, plan)
    for copy in copies[3:]:
        copy.wait()
    clear_runs(run_rows, width, edges, range(len(blocks)), blocks)


def near_kernel(*refs):
    *blocks, own, one, two, total = refs
    items = [(block, 0, slab) for block, slab in zip(blocks, (own, one, two))]
    for rows in parts_of(total.shape[0]):
        total[rows, :] = multiply(items, None, rows)


def last_kernel(place_row, place_kind, block, begun, left, right, keep, swap):
    items = [(block, 0, left), (block, left.shape[1], right)]
    wide = keep.shape[1]
    lane = lax.broadcasted_iota(jnp.int32, (UNIT, wide), 1) // (wide // 2)
    keep[...] = jnp.zeros(keep.shape, jnp.float32)
    swap[...] = jnp.zeros(swap.shape, jnp.float32)
    for rows in parts_of(block.shape[0]):
        value = multiply(items, begun[rows, :], rows)
        for at in range(rows.size // UNIT):
            unit = rows.start // UNIT + at
            to_rows = pl.ds(pl.multiple_of(place_row[unit], UNIT), UNIT)
            piece = value[at * UNIT : (at + 1) * UNIT]
            kind = place_kind[unit]
            pltpu.store(keep.at[to_rows, :], piece, mask=lane == kind)
            pltpu.store(swap.at[to_rows, :], piece, mask=lane + 2 == kind)


def vmem(count=None):
    spec = pl.BlockSpec(memory_space=pltpu.VMEM)
    return spec if count is None else [spec] * count


def smem():
    return pl.BlockSpec(memory_space=pltpu.SMEM)


def hbm():
    return pl.BlockSpec(memory_space=pltpu.HBM)


def in_hbm(value):
    return pltpu.with_memory_space_constraint(value, pltpu.HBM)


def product_cost(frontal, samples, slabs):
    group_rows, width = frontal.shape
    flops = 8 * group_rows * width * samples * slabs // 4
    return pl.CostEstimate(flops=flops, bytes_accessed=flops // samples, transcendentals=0)


def bring(frontal, own, leaf_first, leaf_owner, skeleton, n_row, n_col):
    group_rows, width = frontal.shape
    depth = own.shape[1]
    leaves = leaf_first.shape[0]
    units = jax.ShapeDtypeStruct((group_rows // UNIT,), jnp.int32)
    block = jax.ShapeDtypeStruct((group_rows, depth), frontal.dtype)
    return pl.pallas_call(
        functools.partial(bring_kernel, n_row, n_col),
        in_specs=[hbm()] * 5,
        out_specs=vmem(n_row + 1) + [smem()] * 3,
        out_shape=[block] * n_row
        + [
            jax.ShapeDtypeStruct(own.shape, own.dtype),
            units,
            units,
            jax.ShapeDtypeStruct((PICKS + LEAF_MOST * skeleton.shape[0],), jnp.int32),
        ],
        scratch_shapes=[
            pltpu.SMEM((leaves,), jnp.int32),
            pltpu.SMEM((leaves,), jnp.int32),
            pltpu.SMEM(skeleton.shape, jnp.int32),
            pltpu.SMEM((leaves // n_row,), jnp.int32),
            pltpu.SMEM((n_col,), jnp.int32),
            pltpu.SemaphoreType.DMA((4,)),
            pltpu.SemaphoreType.DMA((n_row, COPIES)),
        ],
        cost_estimate=product_cost(frontal, 64, 4),
        compiler_params=pltpu.CompilerParams(vmem_limit_bytes=24 * 2**20),
    )(*(in_hbm(x) for x in (leaf_first, leaf_owner, skeleton, own, frontal)))


def near_product(blocks, slabs):
    group_rows = blocks[0].shape[0]
    samples = slabs[0].shape[0]
    return pl.pallas_call(
        near_kernel,
        in_specs=vmem(2 * len(blocks)),
        out_specs=vmem(),
        out_shape=jax.ShapeDtypeStruct((group_rows, 2 * samples), jnp.float32),
        cost_estimate=product_cost(blocks[0], samples, 12),
        compiler_params=pltpu.CompilerParams(vmem_limit_bytes=24 * 2**20),
    )(*blocks, *slabs)


def last_product(block, begun, places, last, n_col):
    group_rows, wide = begun.shape
    laid = jax.ShapeDtypeStruct((group_rows // 2, wide), jnp.float32)
    return pl.pallas_call(
        last_kernel,
        in_specs=[smem()] * 2 + vmem(4),
        out_specs=vmem(2),
        out_shape=[laid, laid],
        cost_estimate=product_cost(block, wide // 2, 4),
        compiler_params=pltpu.CompilerParams(vmem_limit_bytes=24 * 2**20),
    )(*places, block, begun, *last)


def squeeze_kernel(keep, swapped, here, *away):
    wide, half = here.shape
    samples = wide // 2
    here[...] = (keep[:half] + swapped[:half]).T
    row = lax.broadcasted_iota(jnp.int32, (EXTRA, half), 0)
    for k, out in enumerate(away):
        at = pl.ds((k + 1) * half, half)
        block = (keep[at, :] + swapped[at, :]).T
        tail = jnp.zeros(row.shape, jnp.float32)
        for side in range(2):
            rows = slice(side * samples, (side + 1) * samples)
            part = block[rows]
            most = jnp.maximum(jnp.max(jnp.abs(part), axis=0, keepdims=True), 1e-30)
            power = jnp.ceil(jnp.log2(most) * STEPS)
            scaled = part * (LEVELS * jnp.exp2(power * (-1.0 / STEPS)))
            whole = jnp.floor(scaled + 0.5).astype(jnp.int32)
            out[rows, :] = whole.astype(jnp.int16)
            tail = jnp.where(row == side, power, tail)
        out[pl.ds(2 * samples, EXTRA), :] = tail.astype(jnp.int32).astype(jnp.int16)


def squeeze(keep, swapped, chips):
    rows, wide = keep.shape
    half = rows // chips
    small = jax.ShapeDtypeStruct((wide + EXTRA, half), jnp.int16)
    return pl.pallas_call(
        squeeze_kernel,
        in_specs=vmem(2),
        out_specs=vmem(chips),
        out_shape=[jax.ShapeDtypeStruct((wide, half), jnp.float32)] + [small] * (chips - 1),
        compiler_params=pltpu.CompilerParams(vmem_limit_bytes=24 * 2**20),
    )(keep, swapped)


def thirds(value):
    high = value.astype(jnp.bfloat16)
    rest = value - high.astype(jnp.float32)
    middle = rest.astype(jnp.bfloat16)
    low = (rest - middle.astype(jnp.float32)).astype(jnp.bfloat16)
    return high, middle, low


def beside(left, right):
    wide = left.shape[1]
    lane = lax.broadcasted_iota(jnp.int32, left.shape, 1)
    joined = jnp.where(lane < wide // 2, left.astype(jnp.float32), right.astype(jnp.float32))
    return joined.astype(jnp.bfloat16)


def left_terms(high, middle, low):
    return jnp.concatenate([high, beside(middle, high), beside(low, middle)], axis=1)


def right_terms(high, middle, low):
    return jnp.concatenate([high, middle, high, low, high, middle], axis=0)


def plain_dot(a, b):
    return jnp.dot(a, b, preferred_element_type=jnp.float32)


def leaf_kernel(skel, plan, *refs):
    here, *parts = refs[:-8]
    mine_out, coeff_out, worst_out, mine, picked, turned, coeff, sems = refs[-8:]
    wide, half = here.shape
    samples = wide // 2
    capacity = 2 * half
    every = LEAF_MOST * skel

    sides = [here[pl.ds(0, samples), :], here[pl.ds(samples, samples), :]]
    for part in parts:
        tail = part[pl.ds(wide, EXTRA), :].astype(jnp.int32).astype(jnp.float32)
        step = jnp.exp2(tail * (1.0 / STEPS)) * (1.0 / LEVELS)
        for side in range(2):
            value = part[pl.ds(side * samples, samples), :].astype(jnp.int32).astype(jnp.float32)
            sides[side] = sides[side] + value * step[side : side + 1]
    mine_t = jnp.concatenate(sides, axis=1)
    turned[...] = mine_t
    send_mine = pltpu.make_async_copy(turned, mine_out, sems.at[0])
    send_mine.start()
    total = jnp.concatenate(sides, axis=0).T
    other = pltpu.roll(total, samples, 1)
    low_half = lax.broadcasted_iota(jnp.int32, total.shape, 1) < samples
    mine[pl.ds(0, half), :] = jnp.where(low_half, total, other)
    mine[pl.ds(half, half), :] = jnp.where(low_half, other, total)
    mine[pl.ds(capacity, 8), :] = jnp.zeros((8, wide), jnp.float32)
    for k in range(every):
        picked[pl.ds(k, 1), :] = mine[pl.ds(plan[PICKS + k], 1), :]
    begins = [plan[b] for b in range(LEAF_MOST)]
    count = plan[LEAF_MOST]
    chosen = picked[...]

    high, middle, low = thirds(chosen)
    across = left_terms(high, middle, low)
    down = jnp.concatenate([beside(high, middle), beside(high, low), beside(high, middle)], axis=1)
    gram = nt_dot(across, down)
    proj = plain_dot(across, right_terms(*thirds(mine_t)))

    slot = lax.broadcasted_iota(jnp.int32, (skel, capacity), 1)
    rank = jnp.zeros((skel, capacity), jnp.int32)
    for b in range(1, LEAF_MOST):
        rank += (slot >= begins[b]).astype(jnp.int32)
    hot = [rank == b for b in range(LEAF_MOST)]
    hot_rows = jnp.concatenate([h.astype(jnp.float32) for h in hot], axis=0).astype(jnp.bfloat16)

    lane_leaf = lax.broadcasted_iota(jnp.int32, (skel, every), 1) // skel
    lane_row = lax.broadcasted_iota(jnp.int32, (skel, every), 1) % skel
    below = lax.broadcasted_iota(jnp.int32, (skel, every), 0)
    joined = jnp.where((below == lane_row) & (count == 0), 1.0, 0.0)
    for b in range(LEAF_MOST):
        joined += jnp.where(lane_leaf == b, gram[b * skel : (b + 1) * skel], 0.0)
    terms = [term.astype(jnp.float32) for term in thirds(joined)]
    terms = jnp.concatenate(terms + [jnp.zeros_like(joined)], axis=1)
    turn = lax.broadcasted_iota(jnp.int32, terms.shape, 1) % skel
    spread = jnp.concatenate([jnp.where(turn == i, terms, 0.0) for i in range(skel)], axis=0)
    system = plain_dot(spread.astype(jnp.bfloat16), jnp.concatenate([hot_rows] * 4, axis=0))

    lines = [system[i * skel : (i + 1) * skel] for i in range(skel)]
    right = jnp.zeros((skel, capacity), jnp.float32)
    for b in range(LEAF_MOST):
        right += jnp.where(hot[b], proj[b * skel : (b + 1) * skel], 0.0)
    index = lax.broadcasted_iota(jnp.int32, (skel, capacity), 0)
    uppers = []
    pivots = []
    for j in range(skel):
        line = lines[j]
        inverse = 1.0 / line[j : j + 1]
        upper = line * inverse
        uppers.append(upper)
        pivots.append(inverse)
        for i in range(j + 1, skel):
            lines[i] = lines[i] - line[i : i + 1] * upper
        right = right - jnp.where(index > j, upper * right[j : j + 1], 0.0)
    solved = right * jnp.concatenate(pivots, axis=0)
    for j in range(skel - 2, -1, -1):
        known = jnp.where(index > j, uppers[j] * solved, 0.0)
        less = jnp.sum(known, axis=0, keepdims=True)
        solved = jnp.where(index == j, solved - less, solved)
    coeff[...] = solved
    send_coeff = pltpu.make_async_copy(coeff, coeff_out, sems.at[1])
    send_coeff.start()

    weights = jnp.concatenate([jnp.where(h, solved, 0.0) for h in hot], axis=0)
    upright = chosen.T[:samples]
    upright = thirds(jnp.concatenate([upright, upright], axis=1))
    rebuilt = plain_dot(left_terms(*upright), right_terms(*thirds(weights)))
    resid = mine_t - rebuilt
    err = jnp.sum(resid * resid, axis=0, keepdims=True)
    norm = jnp.sum(mine_t * mine_t, axis=0, keepdims=True)
    worst = jnp.zeros((1, 1), jnp.float32)
    for b in range(LEAF_MOST):
        near = hot[b][:1]
        err_leaf = jnp.sum(jnp.where(near, err, 0.0), axis=1, keepdims=True)
        norm_leaf = jnp.sum(jnp.where(near, norm, 0.0), axis=1, keepdims=True)
        worst = jnp.maximum(worst, jnp.sqrt(err_leaf) / jnp.sqrt(norm_leaf + 1e-06))
    worst_out[...] = jnp.broadcast_to(worst, worst_out.shape)
    send_mine.wait()
    send_coeff.wait()


def leaf_work(here, parts, plan):
    wide, half = here.shape
    samples = wide // 2
    skel = (plan.shape[0] - PICKS) // LEAF_MOST
    return pl.pallas_call(
        functools.partial(leaf_kernel, skel),
        in_specs=[smem()] + vmem(1 + len(parts)),
        out_specs=[hbm(), hbm(), vmem()],
        out_shape=[
            jax.ShapeDtypeStruct((samples, 2 * half), jnp.float32),
            jax.ShapeDtypeStruct((skel, 2 * half), jnp.float32),
            jax.ShapeDtypeStruct((1, LANES), jnp.float32),
        ],
        scratch_shapes=[
            pltpu.VMEM((2 * half + 8, wide), jnp.float32),
            pltpu.VMEM((LEAF_MOST * skel, wide), jnp.float32),
            pltpu.VMEM((samples, 2 * half), jnp.float32),
            pltpu.VMEM((skel, 2 * half), jnp.float32),
            pltpu.SemaphoreType.DMA((2,)),
        ],
        compiler_params=pltpu.CompilerParams(vmem_limit_bytes=12 * 2**20),
    )(plan, here, *parts)


def exchange(value, axis, flip):
    pairs = [(k, k ^ flip) for k in range(lax.axis_size(axis))]
    return lax.ppermute(value, axis, pairs)


def largest(value, axis):
    size = lax.axis_size(axis)
    every = jnp.broadcast_to(value[None], (size, *value.shape))
    return jnp.max(lax.all_to_all(every, axis, 0, 0), axis=0)


def local(frontal, sample_cols, leaf_first, leaf_owner, skeleton):
    n_col = lax.axis_size("col")
    n_row = lax.axis_size("row")
    own = sample_cols.T
    depth = own.shape[1]
    cut = depth // 2 // LANES * LANES
    one = exchange(own, "row", 1)
    two = exchange(own, "row", 2)
    *blocks, block_last, near, place_row, place_kind, plan = bring(
        frontal, own, leaf_first, leaf_owner, skeleton.T, n_row, n_col
    )
    one, two, plan = lax.optimization_barrier((one, two, plan))
    last = [exchange(two[:, :cut], "row", 1), exchange(one[:, cut:], "row", 2)]
    begun = near_product(blocks, (near, one, two))
    keep, swap = last_product(block_last, begun, (place_row, place_kind), last, n_col)
    swapped = exchange(swap, "col", 1)
    here, *away = squeeze(keep, swapped, n_col // 2)
    parts = [exchange(away[k - 1], "col", 2 * k) for k in range(n_col // 2 - 1, 0, -1)]
    mine, coeff, worst = leaf_work(here, parts, plan)
    worst = largest(worst, ("row", "col"))
    return (mine, coeff, worst[0, :1])


def solution(mesh):
    return jax.shard_map(
        local,
        mesh=mesh,
        in_specs=(P("row", "col"), P(("col", "row"), None), P(), P(), P()),
        out_specs=(P("row", "col"), P("row", "col"), P()),
        check_vma=False,
    )
```

```python
import functools

import jax
import jax.numpy as jnp
from jax import lax
from jax.experimental import pallas as pl
from jax.experimental.pallas import tpu as pltpu
from jax.sharding import PartitionSpec as P

UNIT = 32
LANES = 128
LEAF_MOST = 4
PICKS = 8
COPIES = 4
LEVELS = 32760.0
EXTRA = 16
PART = 1024
STEPS = 64.0
RUN_LEAVES = 4


def nt_dot(a, b):
    return lax.dot_general(a, b, (((1,), (1,)), ((), ())), preferred_element_type=jnp.float32)


def leaf_blocks(run_rows, width, edges, act):
    group_rows = edges.shape[0] // RUN_LEAVES * run_rows
    row_pos = lax.axis_index("row")
    first_col = lax.axis_index("col") * width

    def one(at, carry):
        run = at // (run_rows // LANES)
        begin_row = row_pos * group_rows + run * run_rows
        begin_col = row_pos * group_rows + at * LANES
        inside = begin_col - first_col

        @pl.when((inside >= 0) & (inside < width))
        def _():
            shape = (run_rows, LANES)
            down = lax.broadcasted_iota(jnp.int32, shape, 0) + begin_row
            across = lax.broadcasted_iota(jnp.int32, shape, 1) + begin_col
            leaf_down = jnp.zeros(shape, jnp.int32)
            leaf_across = jnp.zeros(shape, jnp.int32)
            for k in range(1, RUN_LEAVES):
                edge = edges[run * RUN_LEAVES + k]
                leaf_down += (down >= edge).astype(jnp.int32)
                leaf_across += (across >= edge).astype(jnp.int32)
            column = jnp.clip(inside, 0, width - LANES)
            rows = pl.ds(pl.multiple_of(run * run_rows, run_rows), run_rows)
            act(rows, column, leaf_down == leaf_across)

        return carry

    lax.fori_loop(0, group_rows // LANES, one, 0)


def multiply(items, value, rows):
    for block, begin, slab in items:
        twice = jnp.concatenate([slab[...], slab[...]], axis=0)
        add = nt_dot(block[rows, pl.ds(begin, slab.shape[1])], twice)
        value = add if value is None else value + add
    return value


def clear_runs(run_rows, edges, held):
    def act(rows, column, same):
        lanes = pl.ds(pl.multiple_of(column, LANES), LANES)
        part = held[rows, lanes].astype(jnp.float32)
        held[rows, lanes] = jnp.where(same, 0.0, part).astype(jnp.bfloat16)

    leaf_blocks(run_rows, held.shape[1], edges, act)


def columns_of(turn, width):
    depth = width // lax.axis_size("row")
    return pl.multiple_of((lax.axis_index("row") ^ turn) * depth, LANES)


def parts_of(group_rows):
    part = min(group_rows, PART)
    return [pl.ds(at, part) for at in range(0, group_rows, part)]


def plan_leaves(n_row, group_rows, capacity, first, owners, skel, plan):
    leaves = first.shape[0]
    per_group = leaves // n_row
    count_skel = skel.shape[0]
    row_pos = lax.axis_index("row")
    col_pos = lax.axis_index("col")

    def clear(at, carry):
        plan[at] = capacity
        return carry

    lax.fori_loop(0, plan.shape[0], clear, 0)

    def find(at, carry):
        count, filled = carry
        leaf = row_pos * per_group + at
        begin = first[leaf]
        following = first[jnp.minimum(leaf + 1, leaves - 1)]
        end = jnp.where(at + 1 < per_group, following, (row_pos + 1) * group_rows)
        hit = (owners[leaf] == col_pos) & (count < LEAF_MOST)

        @pl.when(hit)
        def _():
            plan[count] = filled
            for k in range(count_skel):
                plan[PICKS + count * count_skel + k] = filled + skel[k, leaf] - begin

        return jnp.where(hit, count + 1, count), jnp.where(hit, filled + end - begin, filled)

    count, _ = lax.fori_loop(0, per_group, find, (jnp.int32(0), jnp.int32(0)))
    plan[LEAF_MOST] = count


def bring_kernel(n_row, n_col, leaf_first, leaf_owner, skeleton, own, frontal, *refs):
    held, near, place_row, place_kind, plan, first, owners, skel, edges, used, sems, row_sems = refs
    group_rows, width = frontal.shape
    leaves = leaf_first.shape[0]
    per_group = leaves // n_row
    run_rows = group_rows // (per_group // RUN_LEAVES)
    half = group_rows // n_col
    per_half = half // UNIT
    row_pos = lax.axis_index("row")
    col_pos = lax.axis_index("col")
    copies = [
        pltpu.make_async_copy(leaf_first, first, sems.at[0]),
        pltpu.make_async_copy(leaf_owner, owners, sems.at[1]),
        pltpu.make_async_copy(skeleton, skel, sems.at[2]),
        pltpu.make_async_copy(own, near, sems.at[3]),
    ]
    part = group_rows // COPIES
    for at in range(COPIES):
        rows = pl.ds(at * part, part)
        copies.append(pltpu.make_async_copy(frontal.at[rows, :], held.at[rows, :], row_sems.at[at]))
    for copy in copies:
        copy.start()

    def clear(at, carry):
        used[at] = 0
        return carry

    lax.fori_loop(0, n_col, clear, 0)
    for copy in copies[:3]:
        copy.wait()

    def edge(at, carry):
        edges[at] = first[row_pos * per_group + at]
        return carry

    lax.fori_loop(0, per_group, edge, 0)

    def place(unit, leaf):
        row = row_pos * group_rows + unit * UNIT
        later = jnp.minimum(leaf + 1, leaves - 1)
        moved = (leaf + 1 < leaves) & (first[later] <= row)
        leaf = jnp.where(moved, later, leaf)
        owner = owners[leaf]
        slot = used[owner]
        used[owner] = slot + 1
        step = owner ^ col_pos
        place_row[unit] = step // 2 * half + slot % per_half * UNIT
        place_kind[unit] = step % 2 * 2 + slot // per_half
        return leaf

    lax.fori_loop(0, group_rows // UNIT, place, row_pos * per_group)
    plan_leaves(n_row, group_rows, 2 * half, first, owners, skel, plan)
    for copy in copies[3:]:
        copy.wait()
    clear_runs(run_rows, edges, held)


def near_kernel(held, own, one, two, total):
    width = held.shape[1]
    items = [(held, columns_of(turn, width), slab) for turn, slab in enumerate((own, one, two))]
    for rows in parts_of(total.shape[0]):
        total[rows, :] = multiply(items, None, rows)


def last_kernel(place_row, place_kind, held, begun, left, right, keep, swap):
    begin = columns_of(3, held.shape[1])
    after = pl.multiple_of(begin + left.shape[1], LANES)
    items = [(held, begin, left), (held, after, right)]
    wide = keep.shape[1]
    lane = lax.broadcasted_iota(jnp.int32, (UNIT, wide), 1) // (wide // 2)
    keep[...] = jnp.zeros(keep.shape, jnp.float32)
    swap[...] = jnp.zeros(swap.shape, jnp.float32)
    for rows in parts_of(held.shape[0]):
        value = multiply(items, begun[rows, :], rows)
        for at in range(rows.size // UNIT):
            unit = rows.start // UNIT + at
            to_rows = pl.ds(pl.multiple_of(place_row[unit], UNIT), UNIT)
            piece = value[at * UNIT : (at + 1) * UNIT]
            kind = place_kind[unit]
            pltpu.store(keep.at[to_rows, :], piece, mask=lane == kind)
            pltpu.store(swap.at[to_rows, :], piece, mask=lane + 2 == kind)


def vmem(count=None):
    spec = pl.BlockSpec(memory_space=pltpu.VMEM)
    return spec if count is None else [spec] * count


def smem():
    return pl.BlockSpec(memory_space=pltpu.SMEM)


def hbm():
    return pl.BlockSpec(memory_space=pltpu.HBM)


def in_hbm(value):
    return pltpu.with_memory_space_constraint(value, pltpu.HBM)


def product_cost(frontal, samples, slabs):
    group_rows, width = frontal.shape
    flops = 8 * group_rows * width * samples * slabs // 4
    return pl.CostEstimate(flops=flops, bytes_accessed=flops // samples, transcendentals=0)


def bring(frontal, own, leaf_first, leaf_owner, skeleton, n_row, n_col):
    group_rows, width = frontal.shape
    leaves = leaf_first.shape[0]
    units = jax.ShapeDtypeStruct((group_rows // UNIT,), jnp.int32)
    return pl.pallas_call(
        functools.partial(bring_kernel, n_row, n_col),
        in_specs=[hbm()] * 5,
        out_specs=vmem(2) + [smem()] * 3,
        out_shape=[
            jax.ShapeDtypeStruct(frontal.shape, frontal.dtype),
            jax.ShapeDtypeStruct(own.shape, own.dtype),
            units,
            units,
            jax.ShapeDtypeStruct((PICKS + LEAF_MOST * skeleton.shape[0],), jnp.int32),
        ],
        scratch_shapes=[
            pltpu.SMEM((leaves,), jnp.int32),
            pltpu.SMEM((leaves,), jnp.int32),
            pltpu.SMEM(skeleton.shape, jnp.int32),
            pltpu.SMEM((leaves // n_row,), jnp.int32),
            pltpu.SMEM((n_col,), jnp.int32),
            pltpu.SemaphoreType.DMA((4,)),
            pltpu.SemaphoreType.DMA((COPIES,)),
        ],
        cost_estimate=product_cost(frontal, 64, 4),
        compiler_params=pltpu.CompilerParams(vmem_limit_bytes=24 * 2**20),
    )(*(in_hbm(x) for x in (leaf_first, leaf_owner, skeleton, own, frontal)))


def near_product(held, slabs):
    samples = slabs[0].shape[0]
    return pl.pallas_call(
        near_kernel,
        in_specs=vmem(1 + len(slabs)),
        out_specs=vmem(),
        out_shape=jax.ShapeDtypeStruct((held.shape[0], 2 * samples), jnp.float32),
        cost_estimate=product_cost(held, samples, 3),
        compiler_params=pltpu.CompilerParams(vmem_limit_bytes=24 * 2**20),
    )(held, *slabs)


def last_product(held, begun, places, last, n_col):
    group_rows, wide = begun.shape
    laid = jax.ShapeDtypeStruct((group_rows // 2, wide), jnp.float32)
    return pl.pallas_call(
        last_kernel,
        in_specs=[smem()] * 2 + vmem(4),
        out_specs=vmem(2),
        out_shape=[laid, laid],
        cost_estimate=product_cost(held, wide // 2, 1),
        compiler_params=pltpu.CompilerParams(vmem_limit_bytes=24 * 2**20),
    )(*places, held, begun, *last)


def squeeze_kernel(keep, swapped, here, *away):
    wide, half = here.shape
    samples = wide // 2
    here[...] = (keep[:half] + swapped[:half]).T
    row = lax.broadcasted_iota(jnp.int32, (EXTRA, half), 0)
    for k, out in enumerate(away):
        at = pl.ds((k + 1) * half, half)
        block = (keep[at, :] + swapped[at, :]).T
        tail = jnp.zeros(row.shape, jnp.float32)
        for side in range(2):
            rows = slice(side * samples, (side + 1) * samples)
            part = block[rows]
            most = jnp.maximum(jnp.max(jnp.abs(part), axis=0, keepdims=True), 1e-30)
            power = jnp.ceil(jnp.log2(most) * STEPS)
            scaled = part * (LEVELS * jnp.exp2(power * (-1.0 / STEPS)))
            whole = jnp.floor(scaled + 0.5).astype(jnp.int32)
            out[rows, :] = whole.astype(jnp.int16)
            tail = jnp.where(row == side, power, tail)
        out[pl.ds(2 * samples, EXTRA), :] = tail.astype(jnp.int32).astype(jnp.int16)


def squeeze(keep, swapped, chips):
    rows, wide = keep.shape
    half = rows // chips
    small = jax.ShapeDtypeStruct((wide + EXTRA, half), jnp.int16)
    return pl.pallas_call(
        squeeze_kernel,
        in_specs=vmem(2),
        out_specs=vmem(chips),
        out_shape=[jax.ShapeDtypeStruct((wide, half), jnp.float32)] + [small] * (chips - 1),
        compiler_params=pltpu.CompilerParams(vmem_limit_bytes=24 * 2**20),
    )(keep, swapped)


def thirds(value):
    high = value.astype(jnp.bfloat16)
    rest = value - high.astype(jnp.float32)
    middle = rest.astype(jnp.bfloat16)
    low = (rest - middle.astype(jnp.float32)).astype(jnp.bfloat16)
    return high, middle, low


def beside(left, right):
    wide = left.shape[1]
    lane = lax.broadcasted_iota(jnp.int32, left.shape, 1)
    joined = jnp.where(lane < wide // 2, left.astype(jnp.float32), right.astype(jnp.float32))
    return joined.astype(jnp.bfloat16)


def left_terms(high, middle, low):
    return jnp.concatenate([high, beside(middle, high), beside(low, middle)], axis=1)


def right_terms(high, middle, low):
    return jnp.concatenate([high, middle, high, low, high, middle], axis=0)


def plain_dot(a, b):
    return jnp.dot(a, b, preferred_element_type=jnp.float32)


def leaf_kernel(skel, plan, *refs):
    here, *parts = refs[:-8]
    mine_out, coeff_out, worst_out, mine, picked, turned, coeff, sems = refs[-8:]
    wide, half = here.shape
    samples = wide // 2
    capacity = 2 * half
    every = LEAF_MOST * skel

    sides = [here[pl.ds(0, samples), :], here[pl.ds(samples, samples), :]]
    for part in parts:
        tail = part[pl.ds(wide, EXTRA), :].astype(jnp.int32).astype(jnp.float32)
        step = jnp.exp2(tail * (1.0 / STEPS)) * (1.0 / LEVELS)
        for side in range(2):
            value = part[pl.ds(side * samples, samples), :].astype(jnp.int32).astype(jnp.float32)
            sides[side] = sides[side] + value * step[side : side + 1]
    mine_t = jnp.concatenate(sides, axis=1)
    turned[...] = mine_t
    send_mine = pltpu.make_async_copy(turned, mine_out, sems.at[0])
    send_mine.start()
    total = jnp.concatenate(sides, axis=0).T
    other = pltpu.roll(total, samples, 1)
    low_half = lax.broadcasted_iota(jnp.int32, total.shape, 1) < samples
    mine[pl.ds(0, half), :] = jnp.where(low_half, total, other)
    mine[pl.ds(half, half), :] = jnp.where(low_half, other, total)
    mine[pl.ds(capacity, 8), :] = jnp.zeros((8, wide), jnp.float32)
    for k in range(every):
        picked[pl.ds(k, 1), :] = mine[pl.ds(plan[PICKS + k], 1), :]
    begins = [plan[b] for b in range(LEAF_MOST)]
    count = plan[LEAF_MOST]
    chosen = picked[...]

    high, middle, low = thirds(chosen)
    across = left_terms(high, middle, low)
    down = jnp.concatenate([beside(high, middle), beside(high, low), beside(high, middle)], axis=1)
    gram = nt_dot(across, down)
    proj = plain_dot(across, right_terms(*thirds(mine_t)))

    slot = lax.broadcasted_iota(jnp.int32, (skel, capacity), 1)
    rank = jnp.zeros((skel, capacity), jnp.int32)
    for b in range(1, LEAF_MOST):
        rank += (slot >= begins[b]).astype(jnp.int32)
    hot = [rank == b for b in range(LEAF_MOST)]
    hot_rows = jnp.concatenate([h.astype(jnp.float32) for h in hot], axis=0).astype(jnp.bfloat16)

    lane_leaf = lax.broadcasted_iota(jnp.int32, (skel, every), 1) // skel
    lane_row = lax.broadcasted_iota(jnp.int32, (skel, every), 1) % skel
    below = lax.broadcasted_iota(jnp.int32, (skel, every), 0)
    joined = jnp.where((below == lane_row) & (count == 0), 1.0, 0.0)
    for b in range(LEAF_MOST):
        joined += jnp.where(lane_leaf == b, gram[b * skel : (b + 1) * skel], 0.0)
    terms = [term.astype(jnp.float32) for term in thirds(joined)]
    terms = jnp.concatenate(terms + [jnp.zeros_like(joined)], axis=1)
    turn = lax.broadcasted_iota(jnp.int32, terms.shape, 1) % skel
    spread = jnp.concatenate([jnp.where(turn == i, terms, 0.0) for i in range(skel)], axis=0)
    system = plain_dot(spread.astype(jnp.bfloat16), jnp.concatenate([hot_rows] * 4, axis=0))

    lines = [system[i * skel : (i + 1) * skel] for i in range(skel)]
    right = jnp.zeros((skel, capacity), jnp.float32)
    for b in range(LEAF_MOST):
        right += jnp.where(hot[b], proj[b * skel : (b + 1) * skel], 0.0)
    index = lax.broadcasted_iota(jnp.int32, (skel, capacity), 0)
    uppers = []
    pivots = []
    for j in range(skel):
        line = lines[j]
        inverse = 1.0 / line[j : j + 1]
        upper = line * inverse
        uppers.append(upper)
        pivots.append(inverse)
        for i in range(j + 1, skel):
            lines[i] = lines[i] - line[i : i + 1] * upper
        right = right - jnp.where(index > j, upper * right[j : j + 1], 0.0)
    solved = right * jnp.concatenate(pivots, axis=0)
    for j in range(skel - 2, -1, -1):
        known = jnp.where(index > j, uppers[j] * solved, 0.0)
        less = jnp.sum(known, axis=0, keepdims=True)
        solved = jnp.where(index == j, solved - less, solved)
    coeff[...] = solved
    send_coeff = pltpu.make_async_copy(coeff, coeff_out, sems.at[1])
    send_coeff.start()

    weights = jnp.concatenate([jnp.where(h, solved, 0.0) for h in hot], axis=0)
    upright = chosen.T[:samples]
    upright = thirds(jnp.concatenate([upright, upright], axis=1))
    rebuilt = plain_dot(left_terms(*upright), right_terms(*thirds(weights)))
    resid = mine_t - rebuilt
    err = jnp.sum(resid * resid, axis=0, keepdims=True)
    norm = jnp.sum(mine_t * mine_t, axis=0, keepdims=True)
    worst = jnp.zeros((1, 1), jnp.float32)
    for b in range(LEAF_MOST):
        near = hot[b][:1]
        err_leaf = jnp.sum(jnp.where(near, err, 0.0), axis=1, keepdims=True)
        norm_leaf = jnp.sum(jnp.where(near, norm, 0.0), axis=1, keepdims=True)
        worst = jnp.maximum(worst, jnp.sqrt(err_leaf) / jnp.sqrt(norm_leaf + 1e-06))
    worst_out[...] = jnp.broadcast_to(worst, worst_out.shape)
    send_mine.wait()
    send_coeff.wait()


def leaf_work(here, parts, plan):
    wide, half = here.shape
    samples = wide // 2
    skel = (plan.shape[0] - PICKS) // LEAF_MOST
    return pl.pallas_call(
        functools.partial(leaf_kernel, skel),
        in_specs=[smem()] + vmem(1 + len(parts)),
        out_specs=[hbm(), hbm(), vmem()],
        out_shape=[
            jax.ShapeDtypeStruct((samples, 2 * half), jnp.float32),
            jax.ShapeDtypeStruct((skel, 2 * half), jnp.float32),
            jax.ShapeDtypeStruct((1, LANES), jnp.float32),
        ],
        scratch_shapes=[
            pltpu.VMEM((2 * half + 8, wide), jnp.float32),
            pltpu.VMEM((LEAF_MOST * skel, wide), jnp.float32),
            pltpu.VMEM((samples, 2 * half), jnp.float32),
            pltpu.VMEM((skel, 2 * half), jnp.float32),
            pltpu.SemaphoreType.DMA((2,)),
        ],
        compiler_params=pltpu.CompilerParams(vmem_limit_bytes=12 * 2**20),
    )(plan, here, *parts)


def exchange(value, axis, flip):
    pairs = [(k, k ^ flip) for k in range(lax.axis_size(axis))]
    return lax.ppermute(value, axis, pairs)


def largest(value, axis):
    flip = 1
    while flip < lax.axis_size(axis):
        value = jnp.maximum(value, exchange(value, axis, flip))
        flip *= 2
    return value


def local(frontal, sample_cols, leaf_first, leaf_owner, skeleton):
    n_col = lax.axis_size("col")
    n_row = lax.axis_size("row")
    own = sample_cols.T
    depth = own.shape[1]
    cut = depth // 2 // LANES * LANES
    one = exchange(own, "row", 1)
    two = exchange(own, "row", 2)
    held, near, place_row, place_kind, plan = bring(
        frontal, own, leaf_first, leaf_owner, skeleton.T, n_row, n_col
    )
    one, two, plan = lax.optimization_barrier((one, two, plan))
    last = [exchange(two[:, :cut], "row", 1), exchange(one[:, cut:], "row", 2)]
    begun = near_product(held, (near, one, two))
    keep, swap = last_product(held, begun, (place_row, place_kind), last, n_col)
    swapped = exchange(swap, "col", 1)
    here, *away = squeeze(keep, swapped, n_col // 2)
    parts = [exchange(away[k - 1], "col", 2 * k) for k in range(n_col // 2 - 1, 0, -1)]
    mine, coeff, worst = leaf_work(here, parts, plan)
    worst = largest(largest(worst, "row"), "col")
    return (mine, coeff, worst[0, :1])


def solution(mesh):
    return jax.shard_map(
        local,
        mesh=mesh,
        in_specs=(P("row", "col"), P(("col", "row"), None), P(), P(), P()),
        out_specs=(P("row", "col"), P("row", "col"), P()),
        check_vma=False,
    )
```

```python
import functools

import jax
import jax.numpy as jnp
from jax import lax
from jax.experimental import pallas as pl
from jax.experimental.pallas import tpu as pltpu
from jax.sharding import PartitionSpec as P

UNIT = 32
LANES = 128
LEAF_MOST = 4
PICKS = 8
COPIES = 4
LEVELS = 32760.0
EXTRA = 16
PART = 1024
STEPS = 64.0
RUN_LEAVES = 4


def nt_dot(a, b):
    return lax.dot_general(a, b, (((1,), (1,)), ((), ())), preferred_element_type=jnp.float32)


def leaf_blocks(run_rows, width, edges, act):
    group_rows = edges.shape[0] // RUN_LEAVES * run_rows
    row_pos = lax.axis_index("row")
    first_col = lax.axis_index("col") * width

    def one(at, carry):
        run = at // (run_rows // LANES)
        begin_row = row_pos * group_rows + run * run_rows
        begin_col = row_pos * group_rows + at * LANES
        inside = begin_col - first_col

        @pl.when((inside >= 0) & (inside < width))
        def _():
            shape = (run_rows, LANES)
            down = lax.broadcasted_iota(jnp.int32, shape, 0) + begin_row
            across = lax.broadcasted_iota(jnp.int32, shape, 1) + begin_col
            leaf_down = jnp.zeros(shape, jnp.int32)
            leaf_across = jnp.zeros(shape, jnp.int32)
            for k in range(1, RUN_LEAVES):
                edge = edges[run * RUN_LEAVES + k]
                leaf_down += (down >= edge).astype(jnp.int32)
                leaf_across += (across >= edge).astype(jnp.int32)
            column = jnp.clip(inside, 0, width - LANES)
            rows = pl.ds(pl.multiple_of(run * run_rows, run_rows), run_rows)
            act(rows, column, leaf_down == leaf_across)

        return carry

    lax.fori_loop(0, group_rows // LANES, one, 0)


def multiply(items, value, rows):
    for block, begin, slab in items:
        twice = jnp.concatenate([slab[...], slab[...]], axis=0)
        add = nt_dot(block[rows, pl.ds(begin, slab.shape[1])], twice)
        value = add if value is None else value + add
    return value


def clear_runs(run_rows, edges, held):
    def act(rows, column, same):
        lanes = pl.ds(pl.multiple_of(column, LANES), LANES)
        part = held[rows, lanes].astype(jnp.float32)
        held[rows, lanes] = jnp.where(same, 0.0, part).astype(jnp.bfloat16)

    leaf_blocks(run_rows, held.shape[1], edges, act)


def columns_of(turn, width):
    depth = width // lax.axis_size("row")
    return pl.multiple_of((lax.axis_index("row") ^ turn) * depth, LANES)


def parts_of(group_rows):
    part = min(group_rows, PART)
    return [pl.ds(at, part) for at in range(0, group_rows, part)]


def plan_leaves(n_row, group_rows, capacity, first, owners, skel, plan):
    leaves = first.shape[0]
    per_group = leaves // n_row
    count_skel = skel.shape[0]
    row_pos = lax.axis_index("row")
    col_pos = lax.axis_index("col")

    def clear(at, carry):
        plan[at] = capacity
        return carry

    lax.fori_loop(0, plan.shape[0], clear, 0)

    def find(at, carry):
        count, filled = carry
        leaf = row_pos * per_group + at
        begin = first[leaf]
        following = first[jnp.minimum(leaf + 1, leaves - 1)]
        end = jnp.where(at + 1 < per_group, following, (row_pos + 1) * group_rows)
        hit = (owners[leaf] == col_pos) & (count < LEAF_MOST)

        @pl.when(hit)
        def _():
            plan[count] = filled
            for k in range(count_skel):
                plan[PICKS + count * count_skel + k] = filled + skel[k, leaf] - begin

        return jnp.where(hit, count + 1, count), jnp.where(hit, filled + end - begin, filled)

    count, _ = lax.fori_loop(0, per_group, find, (jnp.int32(0), jnp.int32(0)))
    plan[LEAF_MOST] = count


def bring_kernel(n_row, n_col, leaf_first, leaf_owner, skeleton, own, frontal, *refs):
    held, near, place_row, place_kind, plan, first, owners, skel, edges, used, sems, row_sems = refs
    group_rows, width = frontal.shape
    leaves = leaf_first.shape[0]
    per_group = leaves // n_row
    run_rows = group_rows // (per_group // RUN_LEAVES)
    half = group_rows // n_col
    per_half = half // UNIT
    row_pos = lax.axis_index("row")
    col_pos = lax.axis_index("col")
    copies = [
        pltpu.make_async_copy(leaf_first, first, sems.at[0]),
        pltpu.make_async_copy(leaf_owner, owners, sems.at[1]),
        pltpu.make_async_copy(skeleton, skel, sems.at[2]),
        pltpu.make_async_copy(own, near, sems.at[3]),
    ]
    part = group_rows // COPIES
    for at in range(COPIES):
        rows = pl.ds(at * part, part)
        copies.append(pltpu.make_async_copy(frontal.at[rows, :], held.at[rows, :], row_sems.at[at]))
    for copy in copies:
        copy.start()

    def clear(at, carry):
        used[at] = 0
        return carry

    lax.fori_loop(0, n_col, clear, 0)
    for copy in copies[:3]:
        copy.wait()

    def edge(at, carry):
        edges[at] = first[row_pos * per_group + at]
        return carry

    lax.fori_loop(0, per_group, edge, 0)

    def place(unit, leaf):
        row = row_pos * group_rows + unit * UNIT
        later = jnp.minimum(leaf + 1, leaves - 1)
        moved = (leaf + 1 < leaves) & (first[later] <= row)
        leaf = jnp.where(moved, later, leaf)
        owner = owners[leaf]
        slot = used[owner]
        used[owner] = slot + 1
        step = owner ^ col_pos
        place_row[unit] = step // 2 * half + slot % per_half * UNIT
        place_kind[unit] = step % 2 * 2 + slot // per_half
        return leaf

    lax.fori_loop(0, group_rows // UNIT, place, row_pos * per_group)
    plan_leaves(n_row, group_rows, 2 * half, first, owners, skel, plan)
    for copy in copies[3:]:
        copy.wait()
    clear_runs(run_rows, edges, held)


def near_kernel(held, own, one, two, total):
    width = held.shape[1]
    items = [(held, columns_of(turn, width), slab) for turn, slab in enumerate((own, one, two))]
    for rows in parts_of(total.shape[0]):
        total[rows, :] = multiply(items, None, rows)


def left_kernel(held, begun, left, total):
    items = [(held, columns_of(3, held.shape[1]), left)]
    for rows in parts_of(total.shape[0]):
        total[rows, :] = multiply(items, begun[rows, :], rows)


def last_kernel(place_row, place_kind, held, begun, right, keep, swap):
    width = held.shape[1]
    cut = width // lax.axis_size("row") - right.shape[1]
    items = [(held, pl.multiple_of(columns_of(3, width) + cut, LANES), right)]
    wide = keep.shape[1]
    lane = lax.broadcasted_iota(jnp.int32, (UNIT, wide), 1) // (wide // 2)
    keep[...] = jnp.zeros(keep.shape, jnp.float32)
    swap[...] = jnp.zeros(swap.shape, jnp.float32)
    for rows in parts_of(held.shape[0]):
        value = multiply(items, begun[rows, :], rows)
        for at in range(rows.size // UNIT):
            unit = rows.start // UNIT + at
            to_rows = pl.ds(pl.multiple_of(place_row[unit], UNIT), UNIT)
            piece = value[at * UNIT : (at + 1) * UNIT]
            kind = place_kind[unit]
            pltpu.store(keep.at[to_rows, :], piece, mask=lane == kind)
            pltpu.store(swap.at[to_rows, :], piece, mask=lane + 2 == kind)


def vmem(count=None):
    spec = pl.BlockSpec(memory_space=pltpu.VMEM)
    return spec if count is None else [spec] * count


def smem():
    return pl.BlockSpec(memory_space=pltpu.SMEM)


def hbm():
    return pl.BlockSpec(memory_space=pltpu.HBM)


def in_hbm(value):
    return pltpu.with_memory_space_constraint(value, pltpu.HBM)


def product_cost(frontal, samples, slabs):
    group_rows, width = frontal.shape
    flops = 8 * group_rows * width * samples * slabs // 4
    return pl.CostEstimate(flops=flops, bytes_accessed=flops // samples, transcendentals=0)


def bring(frontal, own, leaf_first, leaf_owner, skeleton, n_row, n_col):
    group_rows, width = frontal.shape
    leaves = leaf_first.shape[0]
    units = jax.ShapeDtypeStruct((group_rows // UNIT,), jnp.int32)
    return pl.pallas_call(
        functools.partial(bring_kernel, n_row, n_col),
        in_specs=[hbm()] * 5,
        out_specs=vmem(2) + [smem()] * 3,
        out_shape=[
            jax.ShapeDtypeStruct(frontal.shape, frontal.dtype),
            jax.ShapeDtypeStruct(own.shape, own.dtype),
            units,
            units,
            jax.ShapeDtypeStruct((PICKS + LEAF_MOST * skeleton.shape[0],), jnp.int32),
        ],
        scratch_shapes=[
            pltpu.SMEM((leaves,), jnp.int32),
            pltpu.SMEM((leaves,), jnp.int32),
            pltpu.SMEM(skeleton.shape, jnp.int32),
            pltpu.SMEM((leaves // n_row,), jnp.int32),
            pltpu.SMEM((n_col,), jnp.int32),
            pltpu.SemaphoreType.DMA((4,)),
            pltpu.SemaphoreType.DMA((COPIES,)),
        ],
        cost_estimate=product_cost(frontal, 64, 4),
        compiler_params=pltpu.CompilerParams(vmem_limit_bytes=24 * 2**20),
    )(*(in_hbm(x) for x in (leaf_first, leaf_owner, skeleton, own, frontal)))


def near_product(held, slabs):
    samples = slabs[0].shape[0]
    return pl.pallas_call(
        near_kernel,
        in_specs=vmem(1 + len(slabs)),
        out_specs=vmem(),
        out_shape=jax.ShapeDtypeStruct((held.shape[0], 2 * samples), jnp.float32),
        cost_estimate=product_cost(held, samples, 3),
        compiler_params=pltpu.CompilerParams(vmem_limit_bytes=24 * 2**20),
    )(held, *slabs)


def left_product(held, begun, left):
    return pl.pallas_call(
        left_kernel,
        in_specs=vmem(3),
        out_specs=vmem(),
        out_shape=jax.ShapeDtypeStruct(begun.shape, jnp.float32),
        cost_estimate=product_cost(held, left.shape[0], 1),
        compiler_params=pltpu.CompilerParams(vmem_limit_bytes=24 * 2**20),
    )(held, begun, left)


def last_product(held, begun, places, last, n_col):
    group_rows, wide = begun.shape
    laid = jax.ShapeDtypeStruct((group_rows // 2, wide), jnp.float32)
    return pl.pallas_call(
        last_kernel,
        in_specs=[smem()] * 2 + vmem(3),
        out_specs=vmem(2),
        out_shape=[laid, laid],
        cost_estimate=product_cost(held, wide // 2, 1),
        compiler_params=pltpu.CompilerParams(vmem_limit_bytes=24 * 2**20),
    )(*places, held, begun, last)


def squeeze_kernel(keep, swapped, here, *away):
    wide, half = here.shape
    samples = wide // 2
    here[...] = (keep[:half] + swapped[:half]).T
    row = lax.broadcasted_iota(jnp.int32, (EXTRA, half), 0)
    for k, out in enumerate(away):
        at = pl.ds((k + 1) * half, half)
        block = (keep[at, :] + swapped[at, :]).T
        tail = jnp.zeros(row.shape, jnp.float32)
        for side in range(2):
            rows = slice(side * samples, (side + 1) * samples)
            part = block[rows]
            most = jnp.maximum(jnp.max(jnp.abs(part), axis=0, keepdims=True), 1e-30)
            power = jnp.ceil(jnp.log2(most) * STEPS)
            scaled = part * (LEVELS * jnp.exp2(power * (-1.0 / STEPS)))
            whole = jnp.floor(scaled + 0.5).astype(jnp.int32)
            out[rows, :] = whole.astype(jnp.int16)
            tail = jnp.where(row == side, power, tail)
        out[pl.ds(2 * samples, EXTRA), :] = tail.astype(jnp.int32).astype(jnp.int16)


def squeeze(keep, swapped, chips):
    rows, wide = keep.shape
    half = rows // chips
    small = jax.ShapeDtypeStruct((wide + EXTRA, half), jnp.int16)
    return pl.pallas_call(
        squeeze_kernel,
        in_specs=vmem(2),
        out_specs=vmem(chips),
        out_shape=[jax.ShapeDtypeStruct((wide, half), jnp.float32)] + [small] * (chips - 1),
        compiler_params=pltpu.CompilerParams(vmem_limit_bytes=24 * 2**20),
    )(keep, swapped)


def thirds(value):
    high = value.astype(jnp.bfloat16)
    rest = value - high.astype(jnp.float32)
    middle = rest.astype(jnp.bfloat16)
    low = (rest - middle.astype(jnp.float32)).astype(jnp.bfloat16)
    return high, middle, low


def beside(left, right):
    wide = left.shape[1]
    lane = lax.broadcasted_iota(jnp.int32, left.shape, 1)
    joined = jnp.where(lane < wide // 2, left.astype(jnp.float32), right.astype(jnp.float32))
    return joined.astype(jnp.bfloat16)


def left_terms(high, middle, low):
    return jnp.concatenate([high, beside(middle, high), beside(low, middle)], axis=1)


def right_terms(high, middle, low):
    return jnp.concatenate([high, middle, high, low, high, middle], axis=0)


def plain_dot(a, b):
    return jnp.dot(a, b, preferred_element_type=jnp.float32)


def leaf_kernel(skel, plan, *refs):
    here, *parts = refs[:-8]
    mine_out, coeff_out, worst_out, mine, picked, turned, coeff, sems = refs[-8:]
    wide, half = here.shape
    samples = wide // 2
    capacity = 2 * half
    every = LEAF_MOST * skel

    sides = [here[pl.ds(0, samples), :], here[pl.ds(samples, samples), :]]
    for part in parts:
        tail = part[pl.ds(wide, EXTRA), :].astype(jnp.int32).astype(jnp.float32)
        step = jnp.exp2(tail * (1.0 / STEPS)) * (1.0 / LEVELS)
        for side in range(2):
            value = part[pl.ds(side * samples, samples), :].astype(jnp.int32).astype(jnp.float32)
            sides[side] = sides[side] + value * step[side : side + 1]
    mine_t = jnp.concatenate(sides, axis=1)
    turned[...] = mine_t
    send_mine = pltpu.make_async_copy(turned, mine_out, sems.at[0])
    send_mine.start()
    total = jnp.concatenate(sides, axis=0).T
    other = pltpu.roll(total, samples, 1)
    low_half = lax.broadcasted_iota(jnp.int32, total.shape, 1) < samples
    mine[pl.ds(0, half), :] = jnp.where(low_half, total, other)
    mine[pl.ds(half, half), :] = jnp.where(low_half, other, total)
    mine[pl.ds(capacity, 8), :] = jnp.zeros((8, wide), jnp.float32)
    for k in range(every):
        picked[pl.ds(k, 1), :] = mine[pl.ds(plan[PICKS + k], 1), :]
    begins = [plan[b] for b in range(LEAF_MOST)]
    count = plan[LEAF_MOST]
    chosen = picked[...]

    high, middle, low = thirds(chosen)
    across = left_terms(high, middle, low)
    down = jnp.concatenate([beside(high, middle), beside(high, low), beside(high, middle)], axis=1)
    gram = nt_dot(across, down)
    proj = plain_dot(across, right_terms(*thirds(mine_t)))

    slot = lax.broadcasted_iota(jnp.int32, (skel, capacity), 1)
    rank = jnp.zeros((skel, capacity), jnp.int32)
    for b in range(1, LEAF_MOST):
        rank += (slot >= begins[b]).astype(jnp.int32)
    hot = [rank == b for b in range(LEAF_MOST)]
    hot_rows = jnp.concatenate([h.astype(jnp.float32) for h in hot], axis=0).astype(jnp.bfloat16)

    lane_leaf = lax.broadcasted_iota(jnp.int32, (skel, every), 1) // skel
    lane_row = lax.broadcasted_iota(jnp.int32, (skel, every), 1) % skel
    below = lax.broadcasted_iota(jnp.int32, (skel, every), 0)
    joined = jnp.where((below == lane_row) & (count == 0), 1.0, 0.0)
    for b in range(LEAF_MOST):
        joined += jnp.where(lane_leaf == b, gram[b * skel : (b + 1) * skel], 0.0)
    terms = [term.astype(jnp.float32) for term in thirds(joined)]
    terms = jnp.concatenate(terms + [jnp.zeros_like(joined)], axis=1)
    turn = lax.broadcasted_iota(jnp.int32, terms.shape, 1) % skel
    spread = jnp.concatenate([jnp.where(turn == i, terms, 0.0) for i in range(skel)], axis=0)
    system = plain_dot(spread.astype(jnp.bfloat16), jnp.concatenate([hot_rows] * 4, axis=0))

    lines = [system[i * skel : (i + 1) * skel] for i in range(skel)]
    right = jnp.zeros((skel, capacity), jnp.float32)
    for b in range(LEAF_MOST):
        right += jnp.where(hot[b], proj[b * skel : (b + 1) * skel], 0.0)
    index = lax.broadcasted_iota(jnp.int32, (skel, capacity), 0)
    uppers = []
    pivots = []
    for j in range(skel):
        line = lines[j]
        inverse = 1.0 / line[j : j + 1]
        upper = line * inverse
        uppers.append(upper)
        pivots.append(inverse)
        for i in range(j + 1, skel):
            lines[i] = lines[i] - line[i : i + 1] * upper
        right = right - jnp.where(index > j, upper * right[j : j + 1], 0.0)
    solved = right * jnp.concatenate(pivots, axis=0)
    for j in range(skel - 2, -1, -1):
        known = jnp.where(index > j, uppers[j] * solved, 0.0)
        less = jnp.sum(known, axis=0, keepdims=True)
        solved = jnp.where(index == j, solved - less, solved)
    coeff[...] = solved
    send_coeff = pltpu.make_async_copy(coeff, coeff_out, sems.at[1])
    send_coeff.start()

    weights = jnp.concatenate([jnp.where(h, solved, 0.0) for h in hot], axis=0)
    upright = chosen.T[:samples]
    upright = thirds(jnp.concatenate([upright, upright], axis=1))
    rebuilt = plain_dot(left_terms(*upright), right_terms(*thirds(weights)))
    resid = mine_t - rebuilt
    err = jnp.sum(resid * resid, axis=0, keepdims=True)
    norm = jnp.sum(mine_t * mine_t, axis=0, keepdims=True)
    worst = jnp.zeros((1, 1), jnp.float32)
    for b in range(LEAF_MOST):
        near = hot[b][:1]
        err_leaf = jnp.sum(jnp.where(near, err, 0.0), axis=1, keepdims=True)
        norm_leaf = jnp.sum(jnp.where(near, norm, 0.0), axis=1, keepdims=True)
        worst = jnp.maximum(worst, jnp.sqrt(err_leaf) / jnp.sqrt(norm_leaf + 1e-06))
    worst_out[...] = jnp.broadcast_to(worst, worst_out.shape)
    send_mine.wait()
    send_coeff.wait()


def leaf_work(here, parts, plan):
    wide, half = here.shape
    samples = wide // 2
    skel = (plan.shape[0] - PICKS) // LEAF_MOST
    return pl.pallas_call(
        functools.partial(leaf_kernel, skel),
        in_specs=[smem()] + vmem(1 + len(parts)),
        out_specs=[hbm(), hbm(), vmem()],
        out_shape=[
            jax.ShapeDtypeStruct((samples, 2 * half), jnp.float32),
            jax.ShapeDtypeStruct((skel, 2 * half), jnp.float32),
            jax.ShapeDtypeStruct((1, LANES), jnp.float32),
        ],
        scratch_shapes=[
            pltpu.VMEM((2 * half + 8, wide), jnp.float32),
            pltpu.VMEM((LEAF_MOST * skel, wide), jnp.float32),
            pltpu.VMEM((samples, 2 * half), jnp.float32),
            pltpu.VMEM((skel, 2 * half), jnp.float32),
            pltpu.SemaphoreType.DMA((2,)),
        ],
        compiler_params=pltpu.CompilerParams(vmem_limit_bytes=12 * 2**20),
    )(plan, here, *parts)


def exchange(value, axis, flip):
    pairs = [(k, k ^ flip) for k in range(lax.axis_size(axis))]
    return lax.ppermute(value, axis, pairs)


def largest(value, axis):
    size = lax.axis_size(axis)
    every = jnp.broadcast_to(value[None], (size, *value.shape))
    return jnp.max(lax.all_to_all(every, axis, 0, 0), axis=0)


def local(frontal, sample_cols, leaf_first, leaf_owner, skeleton):
    n_col = lax.axis_size("col")
    n_row = lax.axis_size("row")
    own = sample_cols.T
    depth = own.shape[1]
    cut = depth // 2 // LANES * LANES
    one = exchange(own, "row", 1)
    two = exchange(own, "row", 2)
    held, near, place_row, place_kind, plan = bring(
        frontal, own, leaf_first, leaf_owner, skeleton.T, n_row, n_col
    )
    one, two, plan = lax.optimization_barrier((one, two, plan))
    left = exchange(two[:, :cut], "row", 1)
    right = exchange(one[:, cut:], "row", 2)
    begun = near_product(held, (near, one, two))
    begun = left_product(held, begun, left)
    keep, swap = last_product(held, begun, (place_row, place_kind), right, n_col)
    swapped = exchange(swap, "col", 1)
    here, *away = squeeze(keep, swapped, n_col // 2)
    parts = [exchange(away[k - 1], "col", 2 * k) for k in range(n_col // 2 - 1, 0, -1)]
    mine, coeff, worst = leaf_work(here, parts, plan)
    worst = largest(worst, ("row", "col"))
    return (mine, coeff, worst[0, :1])


def solution(mesh):
    return jax.shard_map(
        local,
        mesh=mesh,
        in_specs=(P("row", "col"), P(("col", "row"), None), P(), P(), P()),
        out_specs=(P("row", "col"), P("row", "col"), P()),
        check_vma=False,
    )
```

```python
import functools

import jax
import jax.numpy as jnp
from jax import lax
from jax.experimental import pallas as pl
from jax.experimental.pallas import tpu as pltpu
from jax.sharding import PartitionSpec as P

UNIT = 32
LANES = 128
LEAF_MOST = 4
PICKS = 8
COPIES = 4
LEVELS = 32760.0
EXTRA = 16
PART = 1024
STEPS = 64.0
RUN_LEAVES = 4


def nt_dot(a, b):
    return lax.dot_general(a, b, (((1,), (1,)), ((), ())), preferred_element_type=jnp.float32)


def leaf_blocks(run_rows, width, edges, act):
    group_rows = edges.shape[0] // RUN_LEAVES * run_rows
    row_pos = lax.axis_index("row")
    first_col = lax.axis_index("col") * width

    def one(at, carry):
        run = at // (run_rows // LANES)
        begin_row = row_pos * group_rows + run * run_rows
        begin_col = row_pos * group_rows + at * LANES
        inside = begin_col - first_col

        @pl.when((inside >= 0) & (inside < width))
        def _():
            shape = (run_rows, LANES)
            down = lax.broadcasted_iota(jnp.int32, shape, 0) + begin_row
            across = lax.broadcasted_iota(jnp.int32, shape, 1) + begin_col
            leaf_down = jnp.zeros(shape, jnp.int32)
            leaf_across = jnp.zeros(shape, jnp.int32)
            for k in range(1, RUN_LEAVES):
                edge = edges[run * RUN_LEAVES + k]
                leaf_down += (down >= edge).astype(jnp.int32)
                leaf_across += (across >= edge).astype(jnp.int32)
            column = jnp.clip(inside, 0, width - LANES)
            rows = pl.ds(pl.multiple_of(run * run_rows, run_rows), run_rows)
            act(rows, column, leaf_down == leaf_across)

        return carry

    lax.fori_loop(0, group_rows // LANES, one, 0)


def multiply(items, value, rows):
    for block, begin, slab in items:
        twice = jnp.concatenate([slab[...], slab[...]], axis=0)
        add = nt_dot(block[rows, pl.ds(begin, slab.shape[1])], twice)
        value = add if value is None else value + add
    return value


def clear_runs(run_rows, edges, held):
    def act(rows, column, same):
        lanes = pl.ds(pl.multiple_of(column, LANES), LANES)
        part = held[rows, lanes].astype(jnp.float32)
        held[rows, lanes] = jnp.where(same, 0.0, part).astype(jnp.bfloat16)

    leaf_blocks(run_rows, held.shape[1], edges, act)


def columns_of(turn, width):
    depth = width // lax.axis_size("row")
    return pl.multiple_of((lax.axis_index("row") ^ turn) * depth, LANES)


def parts_of(group_rows):
    part = min(group_rows, PART)
    return [pl.ds(at, part) for at in range(0, group_rows, part)]


def plan_leaves(n_row, group_rows, capacity, first, owners, skel, plan):
    leaves = first.shape[0]
    per_group = leaves // n_row
    count_skel = skel.shape[0]
    row_pos = lax.axis_index("row")
    col_pos = lax.axis_index("col")

    def clear(at, carry):
        plan[at] = capacity
        return carry

    lax.fori_loop(0, plan.shape[0], clear, 0)

    def find(at, carry):
        count, filled = carry
        leaf = row_pos * per_group + at
        begin = first[leaf]
        following = first[jnp.minimum(leaf + 1, leaves - 1)]
        end = jnp.where(at + 1 < per_group, following, (row_pos + 1) * group_rows)
        hit = (owners[leaf] == col_pos) & (count < LEAF_MOST)

        @pl.when(hit)
        def _():
            plan[count] = filled
            for k in range(count_skel):
                plan[PICKS + count * count_skel + k] = filled + skel[k, leaf] - begin

        return jnp.where(hit, count + 1, count), jnp.where(hit, filled + end - begin, filled)

    count, _ = lax.fori_loop(0, per_group, find, (jnp.int32(0), jnp.int32(0)))
    plan[LEAF_MOST] = count


def bring_kernel(n_row, n_col, leaf_first, leaf_owner, skeleton, own, frontal, *refs):
    held, near, place_row, place_kind, plan, first, owners, skel, edges, used, sems, row_sems = refs
    group_rows, width = frontal.shape
    leaves = leaf_first.shape[0]
    per_group = leaves // n_row
    run_rows = group_rows // (per_group // RUN_LEAVES)
    half = group_rows // n_col
    per_half = half // UNIT
    row_pos = lax.axis_index("row")
    col_pos = lax.axis_index("col")
    copies = [
        pltpu.make_async_copy(leaf_first, first, sems.at[0]),
        pltpu.make_async_copy(leaf_owner, owners, sems.at[1]),
        pltpu.make_async_copy(skeleton, skel, sems.at[2]),
        pltpu.make_async_copy(own, near, sems.at[3]),
    ]
    part = group_rows // COPIES
    for at in range(COPIES):
        rows = pl.ds(at * part, part)
        copies.append(pltpu.make_async_copy(frontal.at[rows, :], held.at[rows, :], row_sems.at[at]))
    for copy in copies:
        copy.start()

    def clear(at, carry):
        used[at] = 0
        return carry

    lax.fori_loop(0, n_col, clear, 0)
    for copy in copies[:3]:
        copy.wait()

    def edge(at, carry):
        edges[at] = first[row_pos * per_group + at]
        return carry

    lax.fori_loop(0, per_group, edge, 0)

    def place(unit, leaf):
        row = row_pos * group_rows + unit * UNIT
        later = jnp.minimum(leaf + 1, leaves - 1)
        moved = (leaf + 1 < leaves) & (first[later] <= row)
        leaf = jnp.where(moved, later, leaf)
        owner = owners[leaf]
        slot = used[owner]
        used[owner] = slot + 1
        step = owner ^ col_pos
        place_row[unit] = step // 2 * half + slot % per_half * UNIT
        place_kind[unit] = step % 2 * 2 + slot // per_half
        return leaf

    lax.fori_loop(0, group_rows // UNIT, place, row_pos * per_group)
    plan_leaves(n_row, group_rows, 2 * half, first, owners, skel, plan)
    for copy in copies[3:]:
        copy.wait()
    clear_runs(run_rows, edges, held)


def near_kernel(held, own, one, two, total):
    width = held.shape[1]
    items = [(held, columns_of(turn, width), slab) for turn, slab in enumerate((own, one, two))]
    for rows in parts_of(total.shape[0]):
        total[rows, :] = multiply(items, None, rows)


def left_kernel(held, begun, left, total):
    items = [(held, columns_of(3, held.shape[1]), left)]
    for rows in parts_of(total.shape[0]):
        total[rows, :] = multiply(items, begun[rows, :], rows)


def last_kernel(place_row, place_kind, held, begun, right, keep, swap):
    width = held.shape[1]
    cut = width // lax.axis_size("row") - right.shape[1]
    items = [(held, pl.multiple_of(columns_of(3, width) + cut, LANES), right)]
    wide = keep.shape[1]
    lane = lax.broadcasted_iota(jnp.int32, (UNIT, wide), 1) // (wide // 2)
    keep[...] = jnp.zeros(keep.shape, jnp.float32)
    swap[...] = jnp.zeros(swap.shape, jnp.float32)
    for rows in parts_of(held.shape[0]):
        value = multiply(items, begun[rows, :], rows)
        for at in range(rows.size // UNIT):
            unit = rows.start // UNIT + at
            to_rows = pl.ds(pl.multiple_of(place_row[unit], UNIT), UNIT)
            piece = value[at * UNIT : (at + 1) * UNIT]
            kind = place_kind[unit]
            pltpu.store(keep.at[to_rows, :], piece, mask=lane == kind)
            pltpu.store(swap.at[to_rows, :], piece, mask=lane + 2 == kind)


def vmem(count=None):
    spec = pl.BlockSpec(memory_space=pltpu.VMEM)
    return spec if count is None else [spec] * count


def smem():
    return pl.BlockSpec(memory_space=pltpu.SMEM)


def hbm():
    return pl.BlockSpec(memory_space=pltpu.HBM)


def in_hbm(value):
    return pltpu.with_memory_space_constraint(value, pltpu.HBM)


def product_cost(frontal, samples, slabs):
    group_rows, width = frontal.shape
    flops = 8 * group_rows * width * samples * slabs // 4
    return pl.CostEstimate(flops=flops, bytes_accessed=flops // samples, transcendentals=0)


def bring(frontal, own, leaf_first, leaf_owner, skeleton, n_row, n_col):
    group_rows, width = frontal.shape
    leaves = leaf_first.shape[0]
    units = jax.ShapeDtypeStruct((group_rows // UNIT,), jnp.int32)
    return pl.pallas_call(
        functools.partial(bring_kernel, n_row, n_col),
        in_specs=[hbm()] * 5,
        out_specs=vmem(2) + [smem()] * 3,
        out_shape=[
            jax.ShapeDtypeStruct(frontal.shape, frontal.dtype),
            jax.ShapeDtypeStruct(own.shape, own.dtype),
            units,
            units,
            jax.ShapeDtypeStruct((PICKS + LEAF_MOST * skeleton.shape[0],), jnp.int32),
        ],
        scratch_shapes=[
            pltpu.SMEM((leaves,), jnp.int32),
            pltpu.SMEM((leaves,), jnp.int32),
            pltpu.SMEM(skeleton.shape, jnp.int32),
            pltpu.SMEM((leaves // n_row,), jnp.int32),
            pltpu.SMEM((n_col,), jnp.int32),
            pltpu.SemaphoreType.DMA((4,)),
            pltpu.SemaphoreType.DMA((COPIES,)),
        ],
        cost_estimate=product_cost(frontal, 64, 4),
        compiler_params=pltpu.CompilerParams(vmem_limit_bytes=24 * 2**20),
    )(*(in_hbm(x) for x in (leaf_first, leaf_owner, skeleton, own, frontal)))


def near_product(held, slabs):
    samples = slabs[0].shape[0]
    return pl.pallas_call(
        near_kernel,
        in_specs=vmem(1 + len(slabs)),
        out_specs=vmem(),
        out_shape=jax.ShapeDtypeStruct((held.shape[0], 2 * samples), jnp.float32),
        cost_estimate=product_cost(held, samples, 3),
        compiler_params=pltpu.CompilerParams(vmem_limit_bytes=24 * 2**20),
    )(held, *slabs)


def left_product(held, begun, left):
    return pl.pallas_call(
        left_kernel,
        in_specs=vmem(3),
        out_specs=vmem(),
        out_shape=jax.ShapeDtypeStruct(begun.shape, jnp.float32),
        cost_estimate=product_cost(held, left.shape[0], 1),
        compiler_params=pltpu.CompilerParams(vmem_limit_bytes=24 * 2**20),
    )(held, begun, left)


def last_product(held, begun, places, last, n_col):
    group_rows, wide = begun.shape
    laid = jax.ShapeDtypeStruct((group_rows // 2, wide), jnp.float32)
    return pl.pallas_call(
        last_kernel,
        in_specs=[smem()] * 2 + vmem(3),
        out_specs=vmem(2),
        out_shape=[laid, laid],
        cost_estimate=product_cost(held, wide // 2, 1),
        compiler_params=pltpu.CompilerParams(vmem_limit_bytes=24 * 2**20),
    )(*places, held, begun, last)


def squeeze_kernel(keep, swapped, here, *away):
    wide, half = here.shape
    samples = wide // 2
    here[...] = (keep[:half] + swapped[:half]).T
    row = lax.broadcasted_iota(jnp.int32, (EXTRA, half), 0)
    for k, out in enumerate(away):
        at = pl.ds((k + 1) * half, half)
        block = (keep[at, :] + swapped[at, :]).T
        tail = jnp.zeros(row.shape, jnp.float32)
        for side in range(2):
            rows = slice(side * samples, (side + 1) * samples)
            part = block[rows]
            most = jnp.maximum(jnp.max(jnp.abs(part), axis=0, keepdims=True), 1e-30)
            power = jnp.ceil(jnp.log2(most) * STEPS)
            scaled = part * (LEVELS * jnp.exp2(power * (-1.0 / STEPS)))
            whole = jnp.floor(scaled + 0.5).astype(jnp.int32)
            out[rows, :] = whole.astype(jnp.int16)
            tail = jnp.where(row == side, power, tail)
        out[pl.ds(2 * samples, EXTRA), :] = tail.astype(jnp.int32).astype(jnp.int16)


def squeeze(keep, swapped, chips):
    rows, wide = keep.shape
    half = rows // chips
    small = jax.ShapeDtypeStruct((wide + EXTRA, half), jnp.int16)
    return pl.pallas_call(
        squeeze_kernel,
        in_specs=vmem(2),
        out_specs=vmem(chips),
        out_shape=[jax.ShapeDtypeStruct((wide, half), jnp.float32)] + [small] * (chips - 1),
        compiler_params=pltpu.CompilerParams(vmem_limit_bytes=24 * 2**20),
    )(keep, swapped)


def thirds(value):
    high = value.astype(jnp.bfloat16)
    rest = value - high.astype(jnp.float32)
    middle = rest.astype(jnp.bfloat16)
    low = (rest - middle.astype(jnp.float32)).astype(jnp.bfloat16)
    return high, middle, low


def beside(left, right):
    wide = left.shape[1]
    lane = lax.broadcasted_iota(jnp.int32, left.shape, 1)
    joined = jnp.where(lane < wide // 2, left.astype(jnp.float32), right.astype(jnp.float32))
    return joined.astype(jnp.bfloat16)


def left_terms(high, middle, low):
    return jnp.concatenate([high, beside(middle, high), beside(low, middle)], axis=1)


def right_terms(high, middle, low):
    return jnp.concatenate([high, middle, high, low, high, middle], axis=0)


def plain_dot(a, b):
    return jnp.dot(a, b, preferred_element_type=jnp.float32)


def leaf_kernel(skel, plan, *refs):
    here, *parts = refs[:-8]
    mine_out, coeff_out, worst_out, mine, picked, turned, coeff, sems = refs[-8:]
    wide, half = here.shape
    samples = wide // 2
    capacity = 2 * half
    every = LEAF_MOST * skel

    sides = [here[pl.ds(0, samples), :], here[pl.ds(samples, samples), :]]
    for part in parts:
        tail = part[pl.ds(wide, EXTRA), :].astype(jnp.int32).astype(jnp.float32)
        step = jnp.exp2(tail * (1.0 / STEPS)) * (1.0 / LEVELS)
        for side in range(2):
            value = part[pl.ds(side * samples, samples), :].astype(jnp.int32).astype(jnp.float32)
            sides[side] = sides[side] + value * step[side : side + 1]
    mine_t = jnp.concatenate(sides, axis=1)
    turned[...] = mine_t
    send_mine = pltpu.make_async_copy(turned, mine_out, sems.at[0])
    send_mine.start()
    total = jnp.concatenate(sides, axis=0).T
    other = pltpu.roll(total, samples, 1)
    low_half = lax.broadcasted_iota(jnp.int32, total.shape, 1) < samples
    mine[pl.ds(0, half), :] = jnp.where(low_half, total, other)
    mine[pl.ds(half, half), :] = jnp.where(low_half, other, total)
    mine[pl.ds(capacity, 8), :] = jnp.zeros((8, wide), jnp.float32)
    for k in range(every):
        picked[pl.ds(k, 1), :] = mine[pl.ds(plan[PICKS + k], 1), :]
    begins = [plan[b] for b in range(LEAF_MOST)]
    count = plan[LEAF_MOST]
    chosen = picked[...]

    high, middle, low = thirds(chosen)
    across = left_terms(high, middle, low)
    down = jnp.concatenate([beside(high, middle), beside(high, low), beside(high, middle)], axis=1)
    gram = nt_dot(across, down)
    proj = plain_dot(across, right_terms(*thirds(mine_t)))

    slot = lax.broadcasted_iota(jnp.int32, (skel, capacity), 1)
    rank = jnp.zeros((skel, capacity), jnp.int32)
    for b in range(1, LEAF_MOST):
        rank += (slot >= begins[b]).astype(jnp.int32)
    hot = [rank == b for b in range(LEAF_MOST)]
    hot_rows = jnp.concatenate([h.astype(jnp.float32) for h in hot], axis=0).astype(jnp.bfloat16)

    lane_leaf = lax.broadcasted_iota(jnp.int32, (skel, every), 1) // skel
    lane_row = lax.broadcasted_iota(jnp.int32, (skel, every), 1) % skel
    below = lax.broadcasted_iota(jnp.int32, (skel, every), 0)
    joined = jnp.where((below == lane_row) & (count == 0), 1.0, 0.0)
    for b in range(LEAF_MOST):
        joined += jnp.where(lane_leaf == b, gram[b * skel : (b + 1) * skel], 0.0)
    terms = [term.astype(jnp.float32) for term in thirds(joined)]
    terms = jnp.concatenate(terms + [jnp.zeros_like(joined)], axis=1)
    turn = lax.broadcasted_iota(jnp.int32, terms.shape, 1) % skel
    spread = jnp.concatenate([jnp.where(turn == i, terms, 0.0) for i in range(skel)], axis=0)
    system = plain_dot(spread.astype(jnp.bfloat16), jnp.concatenate([hot_rows] * 4, axis=0))

    lines = [system[i * skel : (i + 1) * skel] for i in range(skel)]
    right = jnp.zeros((skel, capacity), jnp.float32)
    for b in range(LEAF_MOST):
        right += jnp.where(hot[b], proj[b * skel : (b + 1) * skel], 0.0)
    index = lax.broadcasted_iota(jnp.int32, (skel, capacity), 0)
    uppers = []
    pivots = []
    for j in range(skel):
        line = lines[j]
        inverse = 1.0 / line[j : j + 1]
        upper = line * inverse
        uppers.append(upper)
        pivots.append(inverse)
        for i in range(j + 1, skel):
            lines[i] = lines[i] - line[i : i + 1] * upper
        right = right - jnp.where(index > j, upper * right[j : j + 1], 0.0)
    solved = right * jnp.concatenate(pivots, axis=0)
    for j in range(skel - 2, -1, -1):
        known = jnp.where(index > j, uppers[j] * solved, 0.0)
        less = jnp.sum(known, axis=0, keepdims=True)
        solved = jnp.where(index == j, solved - less, solved)
    coeff[...] = solved
    send_coeff = pltpu.make_async_copy(coeff, coeff_out, sems.at[1])
    send_coeff.start()

    weights = jnp.concatenate([jnp.where(h, solved, 0.0) for h in hot], axis=0)
    upright = chosen.T[:samples]
    upright = thirds(jnp.concatenate([upright, upright], axis=1))
    rebuilt = plain_dot(left_terms(*upright), right_terms(*thirds(weights)))
    resid = mine_t - rebuilt
    err = jnp.sum(resid * resid, axis=0, keepdims=True)
    norm = jnp.sum(mine_t * mine_t, axis=0, keepdims=True)
    worst = jnp.zeros((1, 1), jnp.float32)
    for b in range(LEAF_MOST):
        near = hot[b][:1]
        err_leaf = jnp.sum(jnp.where(near, err, 0.0), axis=1, keepdims=True)
        norm_leaf = jnp.sum(jnp.where(near, norm, 0.0), axis=1, keepdims=True)
        worst = jnp.maximum(worst, jnp.sqrt(err_leaf) / jnp.sqrt(norm_leaf + 1e-06))
    worst_out[...] = jnp.broadcast_to(worst, worst_out.shape)
    send_mine.wait()
    send_coeff.wait()


def leaf_work(here, parts, plan):
    wide, half = here.shape
    samples = wide // 2
    skel = (plan.shape[0] - PICKS) // LEAF_MOST
    return pl.pallas_call(
        functools.partial(leaf_kernel, skel),
        in_specs=[smem()] + vmem(1 + len(parts)),
        out_specs=[hbm(), hbm(), vmem()],
        out_shape=[
            jax.ShapeDtypeStruct((samples, 2 * half), jnp.float32),
            jax.ShapeDtypeStruct((skel, 2 * half), jnp.float32),
            jax.ShapeDtypeStruct((1, LANES), jnp.float32),
        ],
        scratch_shapes=[
            pltpu.VMEM((2 * half + 8, wide), jnp.float32),
            pltpu.VMEM((LEAF_MOST * skel, wide), jnp.float32),
            pltpu.VMEM((samples, 2 * half), jnp.float32),
            pltpu.VMEM((skel, 2 * half), jnp.float32),
            pltpu.SemaphoreType.DMA((2,)),
        ],
        compiler_params=pltpu.CompilerParams(vmem_limit_bytes=12 * 2**20),
    )(plan, here, *parts)


def exchange(value, axis, flip):
    pairs = [(k, k ^ flip) for k in range(lax.axis_size(axis))]
    return lax.ppermute(value, axis, pairs)


def largest(value, axis):
    size = lax.axis_size(axis)
    every = jnp.broadcast_to(value[None], (size, *value.shape))
    return jnp.max(lax.all_to_all(every, axis, 0, 0), axis=0)


def local(frontal, sample_cols, leaf_first, leaf_owner, skeleton):
    n_col = lax.axis_size("col")
    n_row = lax.axis_size("row")
    own = sample_cols.T
    depth = own.shape[1]
    cut = depth * 3 // 5 // LANES * LANES
    one = exchange(own, "row", 1)
    two = exchange(own, "row", 2)
    held, near, place_row, place_kind, plan = bring(
        frontal, own, leaf_first, leaf_owner, skeleton.T, n_row, n_col
    )
    one, two, plan = lax.optimization_barrier((one, two, plan))
    left = exchange(two[:, :cut], "row", 1)
    right = exchange(one[:, cut:], "row", 2)
    begun = near_product(held, (near, one, two))
    begun = left_product(held, begun, left)
    keep, swap = last_product(held, begun, (place_row, place_kind), right, n_col)
    swapped = exchange(swap, "col", 1)
    here, *away = squeeze(keep, swapped, n_col // 2)
    flips = sorted(range(n_col // 2 - 1, 0, -1), key=lambda flip: flip != n_col // 4)
    parts = [exchange(away[flip - 1], "col", 2 * flip) for flip in flips]
    mine, coeff, worst = leaf_work(here, parts, plan)
    worst = largest(worst, ("row", "col"))
    return (mine, coeff, worst[0, :1])


def solution(mesh):
    return jax.shard_map(
        local,
        mesh=mesh,
        in_specs=(P("row", "col"), P(("col", "row"), None), P(), P(), P()),
        out_specs=(P("row", "col"), P("row", "col"), P()),
        check_vma=False,
    )
```
